256 devices in a mesh: slow: 8 (over y, core), fast: 32 (over z, x).
Axes of the slice: x: 4, y: 4, z: 8, core: 2. Of those that a mesh axis runs over, the one named last changes fastest.
Arguments:
- observed: float32 [64, 512, 256], P('slow', 'fast'), may hold values from -1 to 3
- start_field: float32 [64, 512, 256], P('slow', 'fast'), may hold values from -6 to 6
- diagonal: float32 [64, 512, 256], P('slow', 'fast'), may hold values from 0.02 to 2
- noise: float32 [2, 64, 512, 256], P(None, 'slow', 'fast'), may hold values from -6 to 6
- sweeps: int32 [3], replicated, may hold values from 2 to 4, as said below
Outputs:
- sampled: float32 [64, 512, 256], P('slow', 'fast')
The draws below stay inside these ranges and needn't reach their ends.
Inputs may be any that keep to these rules, and one draw needn't show every extreme that they name: `sweeps`: a permutation of 2, 3 and 4.
All inputs are finite; a program needn't handle non-finite values.
Results may differ from the reference program's by a relative error of at most 0.0001.
Values sent between devices are 32-bit elements; how exact they have to be, the bound alone decides.
No kernel may reach another device: no remote copies, remote signals or barrier semaphores. Data moves between devices by JAX's collectives and lax.ppermute only.
A program may use at most 128 MiB of HBM per device.

```python
import math
import jax
import jax.numpy as jnp
from jax import lax

STEPS = 2
NY = 64
NZ = 512
NX = 256


def draw_sweeps(key, part):
    key = jax.random.fold_in(key, 7)
    return (jax.random.permutation(key, 3) + 2).astype(jnp.int32)


def block_levels(own_key, extent, shards, least, largest):
    def one(dim, shards_of):
        steps = jax.random.uniform(jax.random.fold_in(jax.random.fold_in(own_key, 6), dim), (shards_of,), jnp.float32, least / len(shards), largest / len(shards))
        return jnp.repeat(jnp.exp(steps), extent[dim] // shards_of).reshape((-1,) + (1,) * (len(extent) - dim - 1))

    factor_of = one(*shards[0])
    for cut in shards[1:]:
        factor_of = factor_of * one(*cut)
    return factor_of


def scatter_about(key, extent, deviation, limit, pieces=(), dtype=jnp.bfloat16):
    result = jax.random.normal(key, extent, jnp.float32) * deviation
    if len(pieces) > 0:
        result = block_levels(key, extent, pieces, -0.22, 0.18) * result
    return jnp.clip(result, min=-limit, max=limit).astype(dtype)


def setup_inputs(seed: int = 0) -> dict:
    keys = jax.random.split(jax.random.key(seed), 6)
    observed = jnp.clip(-1.0 + 4.0 * jax.random.uniform(keys[0], (NY, NZ, NX), jnp.float32) ** block_levels(keys[0], (NY, NZ, NX), ((0, 8), (1, 32)), -0.2, 0.2), -1.0, 3.0)
    start_field = scatter_about(keys[1], (NY, NZ, NX), 1.0, 6.0, ((0, 8), (1, 32)), jnp.float32)
    diagonal = jnp.clip(jnp.exp(math.log(2.0) - 4.6051702 * jax.random.uniform(keys[2], (NY, NZ, NX), jnp.float32) ** block_levels(keys[2], (NY, NZ, NX), ((0, 8), (1, 32)), -0.2, 0.2)), 0.02, 2.0)
    noise = scatter_about(keys[3], (STEPS, NY, NZ, NX), 1.0, 6.0, ((1, 8), (2, 32)), jnp.float32)
    sweeps = draw_sweeps(jax.random.fold_in(keys[5], 71), 0)
    return {"observed": observed, "start_field": start_field, "diagonal": diagonal, "noise": noise, "sweeps": sweeps}


OMEGA = 0.7


def operate(field, diag, scale):
    padded = jnp.pad(field, 1)
    beside = padded[2:, 1:-1, 1:-1] + padded[:-2, 1:-1, 1:-1]
    beside = beside + padded[1:-1, 2:, 1:-1] + padded[1:-1, :-2, 1:-1]
    beside = beside + padded[1:-1, 1:-1, 2:] + padded[1:-1, 1:-1, :-2]
    return (diag + 6.0 * scale) * field - scale * beside


def smooth(error, rhs, diag, scale, count):
    def turn(index, error):
        return error + OMEGA * (rhs - operate(error, diag, scale)) / (diag + 6.0 * scale)
    return lax.fori_loop(0, count, turn, error)


def restrict(field):
    a, b, c = field.shape
    return field.reshape(a // 2, 2, b // 2, 2, c // 2, 2).mean(axis=(1, 3, 5))


def prolong(field):
    return jnp.repeat(jnp.repeat(jnp.repeat(field, 2, 0), 2, 1), 2, 2)


def reference(observed, start_field, diagonal, noise, sweeps):
    diag_mid = restrict(diagonal)
    diag_low = restrict(diag_mid)

    def coarsest(rhs_low):
        err_low = smooth(jnp.zeros_like(rhs_low), rhs_low, diag_low, 0.0625, sweeps[2])
        first, second, third = diag_low.shape
        faces = 2.0 * (first * second + first * third + second * third)
        numer = jnp.sum(rhs_low - operate(err_low, diag_low, 0.0625))
        denom = jnp.sum(diag_low) + 0.0625 * faces
        return err_low + numer / denom

    def vcycle(rhs):
        err_top = smooth(jnp.zeros_like(rhs), rhs, diagonal, 1.0, sweeps[0])
        rhs_mid = restrict(rhs - operate(err_top, diagonal, 1.0))
        err_mid = smooth(jnp.zeros_like(rhs_mid), rhs_mid, diag_mid, 0.25, sweeps[1])
        rhs_low = restrict(rhs_mid - operate(err_mid, diag_mid, 0.25))
        err_low = coarsest(rhs_low)
        err_mid = smooth(err_mid + prolong(err_low), rhs_mid, diag_mid, 0.25, sweeps[1])
        err_top = smooth(err_top + prolong(err_mid), rhs, diagonal, 1.0, sweeps[0])
        return err_top

    sampled = start_field
    for step in range(STEPS):
        rhs = observed - operate(sampled, diagonal, 1.0) + 2.0 * noise[step]
        sampled = sampled + 0.5 * vcycle(rhs)
    return sampled
```

```python
import functools

import jax
import jax.numpy as jnp
from jax import lax
from jax.experimental import pallas as pl
from jax.experimental.pallas import tpu as pltpu
from jax.sharding import PartitionSpec as P

OMEGA = 0.7
KEEP = 1.0 - OMEGA
F32 = jnp.float32

YB, ZB, LANES = 8, 8, 128
YW, ZW = 3 * YB, 3 * ZB
ZM = 40
YM = 32
YPOST = 16


def lane_iota(rows):
    return lax.broadcasted_iota(jnp.int32, (rows, LANES), 1)


def row_iota(rows):
    return lax.broadcasted_iota(jnp.int32, (rows, LANES), 0)


def parity_matrix(transposed):
    row = lax.broadcasted_iota(jnp.int32, (2 * LANES, 2 * LANES), 0)
    col = lax.broadcasted_iota(jnp.int32, (2 * LANES, 2 * LANES), 1)
    if transposed:
        row, col = col, row
    return jnp.where(row == 2 * (col & (LANES - 1)) + (col >> 7), 1.0, 0.0).astype(F32)


def exact_dot(a, b):
    return lax.dot(a, b, precision=lax.Precision.HIGHEST, preferred_element_type=F32)


def fine_neighbours(u, lead, y, lanes):
    rows = u.shape[-2]
    here = [[u[(*lead, pz, px, y)] for px in range(2)] for pz in range(2)]
    beside = [[None, None], [None, None]]
    for pz in range(2):
        for px in range(2):
            total = u[(*lead, pz, px, y - 1)] + u[(*lead, pz, px, y + 1)]
            other = here[1 - pz][px]
            total = total + (other + pltpu.roll(other, 1 if pz == 0 else rows - 1, 0))
            other = here[pz][1 - px]
            if px == 0:
                moved = jnp.where(lanes == 0, 0.0, pltpu.roll(other, 1, 1))
            else:
                moved = jnp.where(lanes == LANES - 1, 0.0, pltpu.roll(other, LANES - 1, 1))
            beside[pz][px] = total + (other + moved)
    return here, beside


def flat_neighbours(u, lead, y, lanes, step):
    rows = u.shape[-2]
    here = u[(*lead, y)]
    total = u[(*lead, y - 1)] + u[(*lead, y + 1)]
    total = total + (pltpu.roll(here, 1, 0) + pltpu.roll(here, rows - 1, 0))
    left = jnp.where(lanes < step, 0.0, pltpu.roll(here, step, 1))
    right = jnp.where(lanes >= LANES - step, 0.0, pltpu.roll(here, LANES - step, 1))
    return here, total + (left + right)


def fine_sweeps(u, q, k, count, first, rows, lanes):
    def sweep(turn, at):
        def one(y, carry):
            here, beside = fine_neighbours(u, (at,), y + 1, lanes)
            for pz in range(2):
                for px in range(2):
                    u[1 - at, pz, px, y + 1] = (
                        KEEP * here[pz][px] + q[pz, px, y] + k[pz, px, y] * beside[pz][px]
                    )
            return carry

        lax.fori_loop(0, rows, one, 0, unroll=2)
        return 1 - at

    return lax.fori_loop(0, count, sweep, jnp.int32(first))


def flat_sweeps(u, q, k, count, first, low, rows, lanes, step, unroll, shift=0):
    def sweep(turn, at):
        def one(y, carry):
            here, beside = flat_neighbours(u, (at,), y, lanes, step)
            u[1 - at, y] = KEEP * here + q[y - shift] + k[y - shift] * beside
            return carry

        lax.fori_loop(low, low + rows, one, 0, unroll=unroll)
        return 1 - at

    return lax.fori_loop(0, count, sweep, jnp.int32(first))


def split_kernel(observed, start, diagonal, noise, fields, later, halves):
    matrix = parity_matrix(False)
    jobs = (
        (start[...], fields.at[0]),
        (observed[...] + 2.0 * noise[0], fields.at[1]),
        (diagonal[...], fields.at[2]),
        (observed[...] + 2.0 * noise[1], later),
    )
    for n, (value, out) in enumerate(jobs):
        both = exact_dot(value.reshape(YB * 2 * ZB, 2 * LANES), matrix)
        for px in range(2):
            halves[n, px] = both[:, px * LANES : (px + 1) * LANES]
        for pz in range(2):
            for px in range(2):
                part = halves[n, px, pl.ds(pz, YB * ZB, stride=2), :]
                out[pz, px] = part.reshape(YB, ZB, LANES)


def inside(axis, which):
    at = lax.axis_index(axis) + (which - 1)
    return jnp.where((at >= 0) & (at < lax.axis_size(axis)), 1.0, 0.0).astype(F32)


def wide(ref, zb_field, pz, px, y):
    return jnp.concatenate([ref[zb, zb_field, pz, px, y] for zb in range(3)], axis=0)


def before_kernel(first, sweeps, *refs):
    if first:
        mid, low, high = refs[:3]
        left_out, own_out, right_out, epre, qpost, kpost, k, dn = refs[3:11]
        u, q = refs[11:]
    else:
        mid, low, high, k, dn = refs[:5]
        left_out, own_out, right_out, epre, qpost = refs[5:10]
        u, q = refs[10:]
    lanes = lane_iota(ZW)
    rows = row_iota(ZW)
    mask_z = [inside("fast", b) for b in range(3)]
    mask_y = [inside("slow", b) for b in range(3)]
    row_mask = jnp.where(rows < ZB, mask_z[0], jnp.where(rows < 2 * ZB, 1.0, mask_z[2]))
    zero = jnp.zeros((ZW, LANES), F32)
    for at in range(2):
        for pz in range(2):
            for px in range(2):
                u[at, pz, px, 0] = zero
                u[at, pz, px, YW + 1] = zero
    blocks = (low, mid, high)
    for yb, ref in enumerate(blocks):

        def fill(y, carry):
            for pz in range(2):
                for px in range(2):
                    value = wide(ref, 0, pz, px, y)
                    u[0, pz, px, 1 + yb * YB + y] = jnp.where(row_mask * mask_y[yb] > 0.5, value, 0.0)
            return carry

        lax.fori_loop(0, YB, fill, 0, unroll=2)
    for yb, ref in enumerate(blocks):

        def right_side(y, carry):
            row = yb * YB + y
            here, beside = fine_neighbours(u, (0,), row + 1, lanes)
            for pz in range(2):
                for px in range(2):
                    if first:
                        full = wide(ref, 2, pz, px, y) + 6.0
                        gain = (OMEGA / full) * (row_mask * mask_y[yb])
                        k[pz, px, row] = gain
                        if yb == 1:
                            dn[pz, px, y] = full * (1.0 / OMEGA)
                        rhs = wide(ref, 1, pz, px, y) - full * here[pz][px] + beside[pz][px]
                        start = gain * rhs
                    else:
                        gain = k[pz, px, row]
                        start = gain * (wide(ref, 1, pz, px, y) + beside[pz][px]) - OMEGA * here[pz][px]
                    q[pz, px, row] = start
                    u[1, pz, px, row + 1] = start
            return carry

        lax.fori_loop(0, YB, right_side, 0, unroll=2)
    at = fine_sweeps(u, q, k, sweeps[0] - 1, 1, YW, lanes)

    def restrict(ym, carry):
        total = zero
        diag = zero
        for half in range(2):
            row = YB + 2 * ym + half
            here, beside = fine_neighbours(u, (at,), row + 1, lanes)
            for pz in range(2):
                for px in range(2):
                    scaled = q[pz, px, row] - OMEGA * here[pz][px] + k[pz, px, row] * beside[pz][px]
                    total = total + scaled * dn[pz, px, 2 * ym + half]
                    if first:
                        diag = diag + wide(mid, 2, pz, px, 2 * ym + half)
        for n, value in enumerate((total, diag) if first else (total,)):
            value = value * 0.125
            right_out[n, ym] = value[: 2 * ZB]
            own_out[n, ym] = value[ZB : 2 * ZB]
            left_out[n, ym] = value[ZB:]
        return carry

    lax.fori_loop(0, YB // 2, restrict, 0)

    def keep(y, carry):
        for pz in range(2):
            for px in range(2):
                epre[pz, px, y] = u[at, pz, px, y + 5]
                qpost[pz, px, y] = q[pz, px, y + 4]
                if first:
                    kpost[pz, px, y] = k[pz, px, y + 4]
        return carry

    lax.fori_loop(0, YPOST, keep, 0, unroll=2)


PADM, PADL = 8, 4


def coarse_kernel(first, sweeps, *refs):
    window = refs[0]
    if first:
        part, e1_out, q1_out, e2_out, k1_out, k1, d1, k2, d2, g2sum = refs[1:11]
        v, q1, t, w, q2, x2 = refs[11:]
    else:
        k1, d1, k2, d2, g2sum = refs[1:6]
        part, e1_out, q1_out, e2_out = refs[6:10]
        v, q1, t, w, q2, x2 = refs[10:]
    fast = lax.axis_index("fast")
    slow = lax.axis_index("slow")
    lanes = lane_iota(ZM)
    even = (lanes & 1) == 0
    zrow = row_iota(ZM) + (fast * ZB - 2 * ZB)
    mask = jnp.where((zrow >= 0) & (zrow < lax.axis_size("fast") * ZB), 1.0, 0.0).astype(F32)
    zero = jnp.zeros((ZM, LANES), F32)
    for n in range(PADM):
        for at in range(2):
            v[at, n] = zero
            v[at, PADM + YM + n] = zero
        q1[n] = zero
        q1[PADM + YM + n] = zero
        if first:
            k1[n] = zero
            k1[PADM + YM + n] = zero
    for block in range(8):
        for ym in range(4):
            y = block * 4 + ym
            if first:
                full = window[block, 1, ym] + 1.5
                gain = (OMEGA / full) * mask
                k1[PADM + y] = gain * 0.25
                d1[y] = full * (1.0 / OMEGA)
                start = gain * window[block, 0, ym]
            else:
                start = (4.0 * k1[PADM + y]) * window[block, 0, ym]
            q1[PADM + y] = start
            v[0, PADM + y] = start
    at = flat_sweeps(v, q1, k1, sweeps[1] - 1, 0, PADM, YM, lanes, 1, 4)
    for yc in range(YM // 2):
        t[yc, ZM:] = jnp.zeros((8, LANES), F32)

    def pair_sum(value):
        return value + jnp.where(even, pltpu.roll(value, LANES - 1, 1), pltpu.roll(value, 1, 1))

    def restrict(yc, carry):
        total = zero
        for half in range(2):
            y = PADM + 2 * yc + half
            here, beside = flat_neighbours(v, (at,), y, lanes, 1)
            total = total + (q1[y] - OMEGA * here + k1[y] * beside) * d1[2 * yc + half]
        t[yc, :ZM] = pair_sum(total)
        return carry

    lax.fori_loop(0, YM // 2, restrict, 0, unroll=2)
    lanes2 = lane_iota(24)
    rows2 = row_iota(24)
    zrow2 = rows2 + (fast * 4 - 8)
    mask2 = jnp.where(
        (zrow2 >= 0) & (zrow2 < lax.axis_size("fast") * 4) & (rows2 < 20), 1.0, 0.0
    ).astype(F32)
    zero2 = jnp.zeros((24, LANES), F32)
    for n in range(PADL):
        for b in range(2):
            w[b, n] = zero2
            w[b, PADL + 16 + n] = zero2

    def halve(yc):
        return (t[yc, pl.ds(0, 24, stride=2), :] + t[yc, pl.ds(1, 24, stride=2), :]) * 0.125

    if first:
        own = jnp.where((rows2 >= 8) & (rows2 < 12), 0.5, 0.0).astype(F32)
        for yc in range(16):
            w[1, PADL + yc] = halve(yc)

        def coarse_diag(yc, carry):
            y = 2 * yc
            value = window[y // 4, 1, y % 4] + window[(y + 1) // 4, 1, (y + 1) % 4]
            t[yc, :ZM] = pair_sum(value)
            return carry

        lax.fori_loop(0, 16, coarse_diag, 0, unroll=2)
        total = zero2
        for yc in range(16):
            g2 = halve(yc)
            full = g2 + 0.375
            gain = (OMEGA / full) * mask2
            k2[yc] = gain * 0.0625
            d2[yc] = full * (1.0 / OMEGA)
            total = total + g2 * own
            start = gain * w[1, PADL + yc]
            q2[yc] = start
            w[0, PADL + yc] = start
        g2sum[...] = total
    else:
        own = jnp.where((rows2 >= 8) & (rows2 < 12), 0.5, 0.0).astype(F32)
        for yc in range(16):
            start = (16.0 * k2[yc]) * halve(yc)
            q2[yc] = start
            w[0, PADL + yc] = start
    at2 = flat_sweeps(w, q2, k2, sweeps[2] - 1, 0, PADL, 16, lanes2, 2, 4, PADL)

    def left_over(yc, total):
        here, beside = flat_neighbours(w, (at2,), yc + PADL, lanes2, 2)
        return total + (q2[yc] - OMEGA * here + k2[yc] * beside) * d2[yc]

    total = lax.fori_loop(0, 16, left_over, zero2, unroll=4)
    numer = jnp.sum(total * own)
    denom = jnp.sum(g2sum[...])
    lanes_p = lane_iota(part.shape[0])
    part[...] = jnp.where(lanes_p == 0, numer, jnp.where(lanes_p == 1, denom, 0.0))

    def give(y, carry):
        row = 4 * slow + (PADM - 6) + y
        e1_out[y] = v[at, row, ZB : 4 * ZB]
        q1_out[y] = q1[row, ZB : 4 * ZB]
        if first:
            k1_out[y] = k1[row, ZB : 4 * ZB]
        return carry

    lax.fori_loop(0, YPOST, give, 0)

    def give2(y, carry):
        value = w[at2, 2 * slow + (PADL - 3) + y]
        x2[y, pl.ds(0, 24, stride=2), :] = value
        x2[y, pl.ds(1, 24, stride=2), :] = value
        e2_out[y] = x2[y, ZB : 4 * ZB]
        return carry

    lax.fori_loop(0, YPOST // 2, give2, 0)


def after_kernel(last, faces, sweeps, parts, e1, q1, k1, e2, epre, q, k, field, later, out, v, u, halves):
    lanes = lane_iota(ZW)
    lanes_p = lane_iota(parts.shape[0])
    every = parts[...]
    numer = jnp.sum(jnp.where(lanes_p == 0, every, 0.0))
    denom = jnp.sum(jnp.where(lanes_p == 1, every, 0.0)) + 0.0625 * faces
    shift = jnp.full((ZW, LANES), numer, F32) / jnp.full((ZW, LANES), denom, F32)
    zero = jnp.zeros((ZW, LANES), F32)
    for at in range(2):
        for y in (0, YPOST + 1):
            v[at, y] = zero
            for pz in range(2):
                for px in range(2):
                    u[at, pz, px, y] = zero
    for y in range(YPOST):
        raised = e1[y] + (e2[y // 2] + shift)
        v[0, y + 1] = jnp.where(k1[y] > 0.0, raised, 0.0)
    at = flat_sweeps(v, q1, k1, sweeps[1], 0, 1, YPOST, lanes, 1, 4, 1)

    def raise_fine(ym, carry):
        value = v[at, ym + 5]
        for half in range(2):
            y = 2 * ym + half
            for pz in range(2):
                for px in range(2):
                    u[0, pz, px, y + 1] = jnp.where(
                        k[pz, px, y] > 0.0, epre[pz, px, y] + value, 0.0
                    )
        return carry

    lax.fori_loop(0, YPOST // 2, raise_fine, 0)
    at = fine_sweeps(u, q, k, sweeps[0], 0, YPOST, lanes)
    for pz in range(2):
        for px in range(2):
            value = field[pz, px] + 0.5 * u[at, pz, px, 5:13, ZB : 2 * ZB]
            if last:
                halves[px, pl.ds(pz, YB * ZB, stride=2), :] = value.reshape(YB * ZB, LANES)
            else:
                out[0, pz, px] = value
                out[1, pz, px] = later[pz, px]
    if last:
        both = jnp.concatenate([halves[0], halves[1]], axis=1)
        out[...] = exact_dot(both, parity_matrix(True)).reshape(YB, 2 * ZB, 2 * LANES)


def vmem(count):
    return [pl.BlockSpec(memory_space=pltpu.VMEM)] * count


def call(kernel, outs, scratch, scalars, *arrays):
    specs = [pl.BlockSpec(memory_space=pltpu.SMEM)] * len(scalars)
    return pl.pallas_call(
        kernel,
        out_shape=[jax.ShapeDtypeStruct(s, F32) for s in outs],
        in_specs=specs + vmem(len(arrays)),
        out_specs=vmem(len(outs)),
        scratch_shapes=[pltpu.VMEM(s, F32) for s in scratch],
        compiler_params=pltpu.CompilerParams(vmem_limit_bytes=40 * 1024 * 1024),
    )(*scalars, *arrays)


def both_ways(to_right, to_left, axis):
    count = lax.axis_size(axis)
    up = [(i, (i + 1) % count) for i in range(count)]
    down = [(target, source) for source, target in up]
    return lax.ppermute(to_right, axis, up), lax.ppermute(to_left, axis, down)


def window_of(fields):
    left, right = both_ways(fields, fields, "fast")
    mid = jnp.stack([left, fields, right])
    low, high = both_ways(mid, mid, "slow")
    return mid, low, high


def body(observed, start_field, diagonal, noise, sweeps):
    block = (2, 2, YB, ZB, LANES)
    post = (2, 2, YPOST, ZW, LANES)
    whole = (2, 2, YW, ZW, LANES)
    fast_count, slow_count = lax.axis_size("fast"), lax.axis_size("slow")
    first, second, third = YB * slow_count // 4, 2 * ZB * fast_count // 4, 2 * LANES // 4
    faces = 2.0 * (first * second + first * third + second * third)
    fields, later = call(
        split_kernel, [(3, *block), block], [(4, 2, YB * 2 * ZB, LANES)], (),
        observed, start_field, diagonal, noise,
    )
    field = fields[0]
    kept_fine = kept_low = None
    for step in range(2):
        opening = step == 0
        count = 2 if opening else 1
        mid, low, high = window_of(fields)
        outs = [(count, 4, 16, LANES), (count, 4, 8, LANES), (count, 4, 16, LANES), post, post]
        scratch = [(2, 2, 2, YW + 2, ZW, LANES), whole]
        if opening:
            outs += [post, whole, (2, 2, YB, ZW, LANES)]
            given = (mid, low, high)
        else:
            given = (mid, low, high, kept_fine[1], kept_fine[2])
        got = call(functools.partial(before_kernel, opening), outs, scratch, (sweeps,), *given)
        to_left, own, to_right, epre, q = got[:5]
        if opening:
            kept_fine = got[5:]
        left, right = both_ways(to_right, to_left, "fast")
        strip = jnp.concatenate([left, own, right], axis=2)
        strip = jnp.broadcast_to(strip[None], (slow_count, *strip.shape))
        strip = lax.all_to_all(strip, "slow", 0, 0, tiled=True)
        outs = [(fast_count, LANES), (YPOST, ZW, LANES), (YPOST, ZW, LANES), (YPOST // 2, ZW, LANES)]
        scratch = [
            (2, YM + 2 * PADM, ZM, LANES),
            (YM + 2 * PADM, ZM, LANES),
            (16, ZM + 8, LANES),
            (2, 16 + 2 * PADL, 24, LANES),
            (16, 24, LANES),
            (YPOST // 2, 48, LANES),
        ]
        if opening:
            outs += [
                (YPOST, ZW, LANES),
                (YM + 2 * PADM, ZM, LANES), (YM, ZM, LANES),
                (16, 24, LANES), (16, 24, LANES), (24, LANES),
            ]
            given = (strip,)
        else:
            given = (strip, *kept_low[1:])
        got = call(functools.partial(coarse_kernel, opening), outs, scratch, (sweeps,), *given)
        part, e1, q1, e2 = got[:4]
        if opening:
            kept_low = got[4:]
        parts = lax.all_to_all(part, "fast", 0, 0, tiled=True)
        outs = [(2, *block) if opening else (YB, 2 * ZB, 2 * LANES)]
        scratch = [(2, YPOST + 2, ZW, LANES), (2, 2, 2, YPOST + 2, ZW, LANES), (2, YB * 2 * ZB, LANES)]
        (fields,) = call(
            functools.partial(after_kernel, not opening, faces), outs, scratch, (sweeps,),
            parts, e1, q1, kept_low[0], e2, epre, q, kept_fine[0], field, later,
        )
        field = fields[0]
    return fields


def solution(mesh):
    placed = (
        P("slow", "fast", None),
        P("slow", "fast", None),
        P("slow", "fast", None),
        P(None, "slow", "fast", None),
        P(),
    )
    return jax.shard_map(
        body, mesh=mesh, in_specs=placed, out_specs=P("slow", "fast", None), check_vma=False
    )
```

```python
import functools

import jax
import jax.numpy as jnp
from jax import lax
from jax.experimental import pallas as pl
from jax.experimental.pallas import tpu as pltpu
from jax.sharding import PartitionSpec as P

OMEGA = 0.7
KEEP = 1.0 - OMEGA
F32 = jnp.float32

YB, ZB, LANES = 8, 8, 128
YW, ZW = 3 * YB, 3 * ZB
ZM, YM = 40, 32
YPOST = 16
PADM, PADL = 8, 4
PARITIES = ((0, 0), (0, 1), (1, 0), (1, 1))


def lane_iota(rows):
    return lax.broadcasted_iota(jnp.int32, (rows, LANES), 1)


def row_iota(rows):
    return lax.broadcasted_iota(jnp.int32, (rows, LANES), 0)


def parity_matrix(transposed):
    row = lax.broadcasted_iota(jnp.int32, (2 * LANES, 2 * LANES), 0)
    col = lax.broadcasted_iota(jnp.int32, (2 * LANES, 2 * LANES), 1)
    if transposed:
        row, col = col, row
    return jnp.where(row == 2 * (col & (LANES - 1)) + (col >> 7), 1.0, 0.0).astype(F32)


def exact_dot(a, b):
    return lax.dot(a, b, precision=lax.Precision.HIGHEST, preferred_element_type=F32)


def over(low, high, chunk, one):
    turns, rest = divmod(high - low, chunk)
    assert rest == 0
    if turns == 1:
        for n in range(chunk):
            one(low + n)
        return

    def turn(at, carry):
        for n in range(chunk):
            one(low + at * chunk + n)
        return carry

    lax.fori_loop(0, turns, turn, 0)


def fine_neighbours(u, y, lanes):
    rows = u.shape[-2]
    here = {p: u[(*p, y)] for p in PARITIES}
    beside = {}
    for pz, px in PARITIES:
        total = u[pz, px, y - 1] + u[pz, px, y + 1]
        other = here[1 - pz, px]
        total = total + (other + pltpu.roll(other, 1 if pz == 0 else rows - 1, 0))
        other = here[pz, 1 - px]
        if px == 0:
            moved = jnp.where(lanes == 0, 0.0, pltpu.roll(other, 1, 1))
        else:
            moved = jnp.where(lanes == LANES - 1, 0.0, pltpu.roll(other, LANES - 1, 1))
        beside[pz, px] = total + (other + moved)
    return here, beside


def flat_neighbours(u, y, lanes, step):
    rows = u.shape[-2]
    here = u[y]
    total = u[y - 1] + u[y + 1]
    total = total + (pltpu.roll(here, 1, 0) + pltpu.roll(here, rows - 1, 0))
    left = jnp.where(lanes < step, 0.0, pltpu.roll(here, step, 1))
    right = jnp.where(lanes >= LANES - step, 0.0, pltpu.roll(here, LANES - step, 1))
    return here, total + (left + right)


def fine_sweep(source, target, q, k, low, high, chunk, lanes, shift=0, offset=0):
    def one(y):
        here, beside = fine_neighbours(source, y, lanes)
        for p in PARITIES:
            target[(*p, y - shift)] = (
                KEEP * here[p] + q[(*p, y + offset)] + k[(*p, y + offset)] * beside[p]
            )

    over(low, high, chunk, one)


def flat_sweep(source, target, q, k, low, high, chunk, lanes, step):
    def one(y):
        here, beside = flat_neighbours(source, y, lanes, step)
        target[y] = KEEP * here + q(y) + k(y) * beside

    over(low, high, chunk, one)


def split_kernel(observed, start, diagonal, noise, fields, later, a, b, c, d, halves, sems):
    copies = [
        pltpu.make_async_copy(source, target, sems.at[n])
        for n, (source, target) in enumerate(((start, a), (diagonal, b), (observed, c), (noise, d)))
    ]
    for copy in copies:
        copy.start()
    matrix = parity_matrix(False)

    def split(n, value, out):
        both = exact_dot(value.reshape(YB * 2 * ZB, 2 * LANES), matrix)
        for px in range(2):
            halves[n, px] = both[:, px * LANES : (px + 1) * LANES]
        for pz, px in PARITIES:
            part = halves[n, px, pl.ds(pz, YB * ZB, stride=2), :]
            out[pz, px] = part.reshape(YB, ZB, LANES)

    copies[0].wait()
    split(0, a[...], fields.at[0])
    copies[1].wait()
    split(1, b[...], fields.at[2])
    copies[2].wait()
    copies[3].wait()
    split(2, c[...] + 2.0 * d[0], fields.at[1])
    split(3, c[...] + 2.0 * d[1], later)


def inside(axis, which):
    at = lax.axis_index(axis) + (which - 1)
    return jnp.where((at >= 0) & (at < lax.axis_size(axis)), 1.0, 0.0).astype(F32)


def wide(ref, field, p, y):
    return jnp.concatenate([ref[(zb, field, *p, y)] for zb in range(3)], axis=0)


def before_kernel(first, sweeps, *refs):
    if first:
        mid, low, high = refs[:3]
        left_out, own_out, right_out, epre, q, k, dn = refs[3:10]
        s, a, b = refs[10:]
    else:
        mid, low, high, k, dn = refs[:5]
        left_out, own_out, right_out, epre, q = refs[5:10]
        s, a, b = refs[10:]
    lanes = lane_iota(ZW)
    rows = row_iota(ZW)
    row_mask = jnp.where(
        rows < ZB, inside("fast", 0), jnp.where(rows < 2 * ZB, 1.0, inside("fast", 2))
    )
    blocks = (low, mid, high)
    masks = [row_mask * inside("slow", 0), row_mask, row_mask * inside("slow", 2)]
    for yb, ref in enumerate(blocks):

        def fill(y):
            for p in PARITIES:
                value = wide(ref, 0, p, y)
                s[(*p, yb * YB + y)] = jnp.where(masks[yb] > 0.5, value, 0.0)

        over(0, YB, 8, fill)
    for yb, ref in enumerate(blocks):

        def right_side(y):
            row = yb * YB + y
            here, beside = fine_neighbours(s, row, lanes)
            for p in PARITIES:
                if first:
                    full = wide(ref, 2, p, y) + 6.0
                    gain = (OMEGA / full) * masks[yb]
                    k[(*p, row)] = gain
                    if yb == 1:
                        dn[(*p, y)] = full * (1.0 / OMEGA)
                else:
                    gain = k[(*p, row)]
                start = gain * (wide(ref, 1, p, y) + beside[p]) - OMEGA * here[p]
                q[(*p, row)] = start
                a[(*p, row)] = start
                b[(*p, row)] = start

        if yb == 1:
            over(0, YB, 4, right_side)
        else:
            over(1 - yb // 2, YB - yb // 2, 7, right_side)

    @pl.when(sweeps[0] >= 4)
    def _():
        fine_sweep(a, b, q, k, 2, 22, 10, lanes)

    @pl.when(sweeps[0] >= 3)
    def _():
        fine_sweep(b, a, q, k, 3, 21, 9, lanes)

    fine_sweep(a, epre, q, k, 4, 20, 8, lanes, shift=4)
    zero = jnp.zeros((ZW, LANES), F32)

    def restrict(ym):
        total = zero
        diag = zero
        for half in range(2):
            row = YB + 2 * ym + half
            here, beside = fine_neighbours(epre, row - 4, lanes)
            for p in PARITIES:
                scaled = q[(*p, row)] - OMEGA * here[p] + k[(*p, row)] * beside[p]
                total = total + scaled * dn[(*p, 2 * ym + half)]
                if first:
                    diag = diag + wide(mid, 2, p, 2 * ym + half)
        for n, value in enumerate((total, diag) if first else (total,)):
            value = value * 0.125
            right_out[n, ym] = value[: 2 * ZB]
            own_out[n, ym] = value[ZB : 2 * ZB]
            left_out[n, ym] = value[ZB:]

    over(0, YB // 2, 4, restrict)


def coarse_kernel(first, sweeps, *refs):
    window = refs[0]
    if first:
        part, e1, q1, e2_out, k1, d1, k2, d2, g2sum = refs[1:10]
        va, t, wa, wb, q2, x2 = refs[10:]
    else:
        k1, d1, k2, d2, g2sum = refs[1:6]
        part, e1, q1, e2_out = refs[6:10]
        va, t, wa, wb, q2, x2 = refs[10:]
    fast = lax.axis_index("fast")
    slow = lax.axis_index("slow")
    lanes = lane_iota(ZM)
    even = (lanes & 1) == 0
    zrow = row_iota(ZM) + (fast * ZB - 2 * ZB)
    mask = jnp.where((zrow >= 0) & (zrow < lax.axis_size("fast") * ZB), 1.0, 0.0).astype(F32)
    zero = jnp.zeros((ZM, LANES), F32)
    for n in (*range(PADM), *range(PADM + YM, YM + 2 * PADM)):
        va[n] = zero
        e1[n] = zero
        q1[n] = zero
        if first:
            k1[n] = zero

    def opening(block):
        for ym in range(4):
            y = block * 4 + ym
            if first:
                full = window[block, 1, ym] + 1.5
                gain = (OMEGA / full) * mask
                k1[PADM + y] = gain * 0.25
                d1[y] = full * (1.0 / OMEGA)
                start = gain * window[block, 0, ym]
            else:
                start = (4.0 * k1[PADM + y]) * window[block, 0, ym]
            q1[PADM + y] = start
            va[PADM + y] = start
            e1[PADM + y] = start

    over(0, YM // 4, 2, opening)
    of_q1, of_k1 = (lambda y: q1[y]), (lambda y: k1[y])

    @pl.when(sweeps[1] >= 4)
    def _():
        flat_sweep(va, e1, of_q1, of_k1, PADM, PADM + YM, 8, lanes, 1)

    @pl.when(sweeps[1] >= 3)
    def _():
        flat_sweep(e1, va, of_q1, of_k1, PADM, PADM + YM, 8, lanes, 1)

    flat_sweep(va, e1, of_q1, of_k1, PADM, PADM + YM, 8, lanes, 1)

    def pair_sum(value):
        return value + jnp.where(even, pltpu.roll(value, LANES - 1, 1), pltpu.roll(value, 1, 1))

    def restrict(yc):
        total = zero
        for half in range(2):
            y = PADM + 2 * yc + half
            here, beside = flat_neighbours(e1, y, lanes, 1)
            total = total + (q1[y] - OMEGA * here + k1[y] * beside) * d1[2 * yc + half]
        t[yc, :ZM] = pair_sum(total)
        t[yc, ZM:] = jnp.zeros((8, LANES), F32)

    over(0, YM // 2, 4, restrict)
    lanes2 = lane_iota(24)
    rows2 = row_iota(24)
    zrow2 = rows2 + (fast * 4 - 8)
    mask2 = jnp.where(
        (zrow2 >= 0) & (zrow2 < lax.axis_size("fast") * 4) & (rows2 < 20), 1.0, 0.0
    ).astype(F32)
    own = jnp.where((rows2 >= 8) & (rows2 < 12), 0.5, 0.0).astype(F32)
    zero2 = jnp.zeros((24, LANES), F32)
    for n in (*range(PADL), *range(PADL + 16, 16 + 2 * PADL)):
        wa[n] = zero2
        wb[n] = zero2

    def halve(yc):
        return (t[yc, pl.ds(0, 24, stride=2), :] + t[yc, pl.ds(1, 24, stride=2), :]) * 0.125

    if first:
        for yc in range(16):
            q2[yc] = halve(yc)

        def coarse_diag(yc):
            block, ym = yc // 2, 2 * (yc % 2)
            t[yc, :ZM] = pair_sum(window[block, 1, ym] + window[block, 1, ym + 1])

        over(0, 16, 4, coarse_diag)
        total = zero2
        for yc in range(16):
            g2 = halve(yc)
            full = g2 + 0.375
            gain = (OMEGA / full) * mask2
            k2[yc] = gain * 0.0625
            d2[yc] = full * (1.0 / OMEGA)
            total = total + g2 * own
            start = gain * q2[yc]
            q2[yc] = start
            wa[PADL + yc] = start
            wb[PADL + yc] = start
        g2sum[...] = total
    else:
        for yc in range(16):
            start = (16.0 * k2[yc]) * halve(yc)
            q2[yc] = start
            wa[PADL + yc] = start
            wb[PADL + yc] = start
    of_q2, of_k2 = (lambda y: q2[y - PADL]), (lambda y: k2[y - PADL])

    @pl.when(sweeps[2] >= 4)
    def _():
        flat_sweep(wa, wb, of_q2, of_k2, PADL, PADL + 16, 16, lanes2, 2)

    @pl.when(sweeps[2] >= 3)
    def _():
        flat_sweep(wb, wa, of_q2, of_k2, PADL, PADL + 16, 16, lanes2, 2)

    flat_sweep(wa, wb, of_q2, of_k2, PADL, PADL + 16, 16, lanes2, 2)
    total = zero2
    for yc in range(16):
        here, beside = flat_neighbours(wb, yc + PADL, lanes2, 2)
        total = total + (q2[yc] - OMEGA * here + k2[yc] * beside) * d2[yc]
    numer = jnp.sum(total * own)
    denom = jnp.sum(g2sum[...])
    lanes_p = lane_iota(part.shape[0])
    part[...] = jnp.where(lanes_p == 0, numer, jnp.where(lanes_p == 1, denom, 0.0))
    for y in range(YPOST // 2):
        value = wb[2 * slow + (PADL - 3) + y]
        x2[y, pl.ds(0, 24, stride=2), :] = value
        x2[y, pl.ds(1, 24, stride=2), :] = value
        e2_out[y] = x2[y, ZB : 4 * ZB]


def after_kernel(last, faces, sweeps, parts, e1, q1, k1, e2, epre, q, k, field, later, out, va, vb, a, b, halves):
    lanes = lane_iota(ZW)
    lanes_p = lane_iota(parts.shape[0])
    every = parts[...]
    numer = jnp.sum(jnp.where(lanes_p == 0, every, 0.0))
    denom = jnp.sum(jnp.where(lanes_p == 1, every, 0.0)) + 0.0625 * faces
    shift = jnp.full((ZW, LANES), numer, F32) / jnp.full((ZW, LANES), denom, F32)
    base = 4 * lax.axis_index("slow") + (PADM - 6)

    def of_q1(y):
        return q1[base + y, ZB : 4 * ZB]

    def of_k1(y):
        return k1[base + y, ZB : 4 * ZB]

    for y in range(YPOST):
        raised = e1[base + y, ZB : 4 * ZB] + (e2[y // 2] + shift)
        raised = jnp.where(of_k1(y) > 0.0, raised, 0.0)
        va[y] = raised
        vb[y] = raised

    @pl.when(sweeps[1] >= 4)
    def _():
        flat_sweep(vb, va, of_q1, of_k1, 1, 15, 14, lanes, 1)

    @pl.when(sweeps[1] >= 3)
    def _():
        flat_sweep(va, vb, of_q1, of_k1, 2, 14, 12, lanes, 1)

    flat_sweep(vb, va, of_q1, of_k1, 3, 13, 10, lanes, 1)
    flat_sweep(va, vb, of_q1, of_k1, 4, 12, 8, lanes, 1)

    def raise_fine(ym):
        value = vb[ym + 4]
        for half in range(2):
            y = 2 * ym + half
            for p in PARITIES:
                raised = jnp.where(k[(*p, y + 4)] > 0.0, epre[(*p, y)] + value, 0.0)
                a[(*p, y)] = raised
                b[(*p, y)] = raised

    over(0, YPOST // 2, 4, raise_fine)

    @pl.when(sweeps[0] >= 4)
    def _():
        fine_sweep(b, a, q, k, 1, 15, 7, lanes, offset=4)

    @pl.when(sweeps[0] >= 3)
    def _():
        fine_sweep(a, b, q, k, 2, 14, 6, lanes, offset=4)

    fine_sweep(b, a, q, k, 3, 13, 10, lanes, offset=4)
    fine_sweep(a, b, q, k, 4, 12, 8, lanes, offset=4)
    for pz, px in PARITIES:
        value = field[pz, px] + 0.5 * b[pz, px, 4:12, ZB : 2 * ZB]
        if last:
            halves[px, pl.ds(pz, YB * ZB, stride=2), :] = value.reshape(YB * ZB, LANES)
        else:
            out[0, pz, px] = value
            out[1, pz, px] = later[pz, px]
    if last:
        both = jnp.concatenate([halves[0], halves[1]], axis=1)
        out[...] = exact_dot(both, parity_matrix(True)).reshape(YB, 2 * ZB, 2 * LANES)


def call(kernel, outs, scratch, scalars, *arrays, space=pltpu.VMEM, megabytes=16):
    specs = [pl.BlockSpec(memory_space=pltpu.SMEM)] * len(scalars)
    return pl.pallas_call(
        kernel,
        out_shape=[jax.ShapeDtypeStruct(s, F32) for s in outs],
        in_specs=specs + [pl.BlockSpec(memory_space=space)] * len(arrays),
        out_specs=[pl.BlockSpec(memory_space=pltpu.VMEM)] * len(outs),
        scratch_shapes=[pltpu.VMEM(s, F32) if isinstance(s, tuple) else s for s in scratch],
        compiler_params=pltpu.CompilerParams(vmem_limit_bytes=megabytes * 1024 * 1024),
    )(*scalars, *arrays)


def both_ways(to_right, to_left, axis):
    count = lax.axis_size(axis)
    up = [(i, (i + 1) % count) for i in range(count)]
    down = [(target, source) for source, target in up]
    return lax.ppermute(to_right, axis, up), lax.ppermute(to_left, axis, down)


def window_of(fields):
    left, right = both_ways(fields, fields, "fast")
    mid = jnp.stack([left, fields, right])
    low, high = both_ways(mid, mid, "slow")
    return mid, low, high


def body(observed, start_field, diagonal, noise, sweeps):
    natural = observed.shape
    block = (2, 2, YB, ZB, LANES)
    post = (2, 2, YPOST, ZW, LANES)
    whole = (2, 2, YW, ZW, LANES)
    middle = (YM + 2 * PADM, ZM, LANES)
    low_window = (16, 24, LANES)
    fast_count, slow_count = lax.axis_size("fast"), lax.axis_size("slow")
    first, second, third = YB * slow_count // 4, 2 * ZB * fast_count // 4, 2 * LANES // 4
    faces = 2.0 * (first * second + first * third + second * third)
    fields, later = call(
        split_kernel, [(3, *block), block],
        [natural, natural, natural, (2, *natural), (4, 2, YB * 2 * ZB, LANES), pltpu.SemaphoreType.DMA((4,))],
        (), observed, start_field, diagonal, noise, space=pltpu.HBM,
    )
    field = fields[0]
    kept_fine = kept_low = None
    for step in range(2):
        opening = step == 0
        count = 2 if opening else 1
        mid, low, high = window_of(fields)
        outs = [(count, 4, 16, LANES), (count, 4, 8, LANES), (count, 4, 16, LANES), post, whole]
        if opening:
            outs += [whole, (2, 2, YB, ZW, LANES)]
            given = (mid, low, high)
        else:
            given = (mid, low, high, *kept_fine)
        got = call(functools.partial(before_kernel, opening), outs, [whole] * 3, (sweeps,), *given)
        to_left, own, to_right, epre, q = got[:5]
        if opening:
            kept_fine = got[5:]
        left, right = both_ways(to_right, to_left, "fast")
        strip = jnp.concatenate([left, own, right], axis=2)
        strip = jnp.broadcast_to(strip[None], (slow_count, *strip.shape))
        strip = lax.all_to_all(strip, "slow", 0, 0, tiled=True)
        outs = [(fast_count, LANES), middle, middle, (YPOST // 2, ZW, LANES)]
        scratch = [
            middle, (16, ZM + 8, LANES), (16 + 2 * PADL, 24, LANES), (16 + 2 * PADL, 24, LANES),
            low_window, (YPOST // 2, 48, LANES),
        ]
        if opening:
            outs += [middle, (YM, ZM, LANES), low_window, low_window, (24, LANES)]
            given = (strip,)
        else:
            given = (strip, *kept_low)
        got = call(functools.partial(coarse_kernel, opening), outs, scratch, (sweeps,), *given)
        part, e1, q1, e2 = got[:4]
        if opening:
            kept_low = got[4:]
        parts = lax.all_to_all(part, "fast", 0, 0, tiled=True)
        outs = [(2, *block) if opening else natural]
        scratch = [(YPOST, ZW, LANES)] * 2 + [post] * 2 + [(2, YB * 2 * ZB, LANES)]
        (fields,) = call(
            functools.partial(after_kernel, not opening, faces), outs, scratch, (sweeps,),
            parts, e1, q1, kept_low[0], e2, epre, q, kept_fine[0], field, later,
        )
        field = fields[0]
    return fields


def solution(mesh):
    placed = (
        P("slow", "fast", None),
        P("slow", "fast", None),
        P("slow", "fast", None),
        P(None, "slow", "fast", None),
        P(),
    )
    return jax.shard_map(
        body, mesh=mesh, in_specs=placed, out_specs=P("slow", "fast", None), check_vma=False
    )
```

```python
import functools

import jax
import jax.numpy as jnp
from jax import lax
from jax.experimental import pallas as pl
from jax.experimental.pallas import tpu as pltpu
from jax.sharding import PartitionSpec as P

OMEGA = 0.7
KEEP = 1.0 - OMEGA
F32 = jnp.float32

YB, ZB, LANES = 8, 8, 128
YW, ZW = 3 * YB, 3 * ZB
ZM, YM = 40, 32
YPOST = 16
PADM, PADL = 8, 4
PARITIES = ((0, 0), (0, 1), (1, 0), (1, 1))


def lane_iota(rows):
    return lax.broadcasted_iota(jnp.int32, (rows, LANES), 1)


def row_iota(rows):
    return lax.broadcasted_iota(jnp.int32, (rows, LANES), 0)


def parity_matrix(transposed):
    row = lax.broadcasted_iota(jnp.int32, (2 * LANES, 2 * LANES), 0)
    col = lax.broadcasted_iota(jnp.int32, (2 * LANES, 2 * LANES), 1)
    if transposed:
        row, col = col, row
    return jnp.where(row == 2 * (col & (LANES - 1)) + (col >> 7), 1.0, 0.0).astype(F32)


def exact_dot(a, b):
    return lax.dot(a, b, precision=lax.Precision.HIGHEST, preferred_element_type=F32)


def over(low, high, chunk, one):
    turns, rest = divmod(high - low, chunk)
    assert rest == 0
    if turns == 1:
        for n in range(chunk):
            one(low + n)
        return

    def turn(at, carry):
        for n in range(chunk):
            one(low + at * chunk + n)
        return carry

    lax.fori_loop(0, turns, turn, 0)


def fine_neighbours(u, y, lanes):
    rows = u.shape[-2]
    here = {p: u[(*p, y)] for p in PARITIES}
    beside = {}
    for pz, px in PARITIES:
        total = u[pz, px, y - 1] + u[pz, px, y + 1]
        other = here[1 - pz, px]
        total = total + (other + pltpu.roll(other, 1 if pz == 0 else rows - 1, 0))
        other = here[pz, 1 - px]
        if px == 0:
            moved = jnp.where(lanes == 0, 0.0, pltpu.roll(other, 1, 1))
        else:
            moved = jnp.where(lanes == LANES - 1, 0.0, pltpu.roll(other, LANES - 1, 1))
        beside[pz, px] = total + (other + moved)
    return here, beside


def flat_neighbours(u, y, lanes, step):
    rows = u.shape[-2]
    here = u[y]
    total = u[y - 1] + u[y + 1]
    total = total + (pltpu.roll(here, 1, 0) + pltpu.roll(here, rows - 1, 0))
    left = jnp.where(lanes < step, 0.0, pltpu.roll(here, step, 1))
    right = jnp.where(lanes >= LANES - step, 0.0, pltpu.roll(here, LANES - step, 1))
    return here, total + (left + right)


def fine_sweep(source, target, q, k, low, high, chunk, lanes, shift=0, offset=0):
    def one(y):
        here, beside = fine_neighbours(source, y, lanes)
        for p in PARITIES:
            target[(*p, y - shift)] = (
                KEEP * here[p] + q[(*p, y + offset)] + k[(*p, y + offset)] * beside[p]
            )

    over(low, high, chunk, one)


def flat_sweep(source, target, q, k, low, high, chunk, lanes, step):
    def one(y):
        here, beside = flat_neighbours(source, y, lanes, step)
        target[y] = KEEP * here + q(y) + k(y) * beside

    over(low, high, chunk, one)


def split_kernel(observed, start, diagonal, noise, fields, later, a, b, c, d, halves, sems):
    copies = [
        pltpu.make_async_copy(source, target, sems.at[n])
        for n, (source, target) in enumerate(((start, a), (diagonal, b), (observed, c), (noise, d)))
    ]
    for copy in copies:
        copy.start()
    matrix = parity_matrix(False)

    def split(n, value, out):
        both = exact_dot(value.reshape(YB * 2 * ZB, 2 * LANES), matrix)
        for px in range(2):
            halves[n, px] = both[:, px * LANES : (px + 1) * LANES]
        for pz, px in PARITIES:
            part = halves[n, px, pl.ds(pz, YB * ZB, stride=2), :]
            out[pz, px] = part.reshape(YB, ZB, LANES)

    copies[0].wait()
    split(0, a[...], fields.at[0])
    copies[1].wait()
    split(1, b[...], fields.at[2])
    copies[2].wait()
    copies[3].wait()
    split(2, c[...] + 2.0 * d[0], fields.at[1])
    split(3, c[...] + 2.0 * d[1], later)


def inside(axis, which):
    at = lax.axis_index(axis) + (which - 1)
    return jnp.where((at >= 0) & (at < lax.axis_size(axis)), 1.0, 0.0).astype(F32)


def wide(ref, field, p, y):
    return jnp.concatenate([ref[(zb, field, *p, y)] for zb in range(3)], axis=0)


def before_kernel(first, sweeps, *refs):
    if first:
        mid, low, high = refs[:3]
        left_out, own_out, right_out, epre, q, k, dn = refs[3:10]
        s, a, b = refs[10:]
    else:
        mid, low, high, k, dn = refs[:5]
        left_out, own_out, right_out, epre, q = refs[5:10]
        s, a, b = refs[10:]
    lanes = lane_iota(ZW)
    rows = row_iota(ZW)
    row_mask = jnp.where(
        rows < ZB, inside("fast", 0), jnp.where(rows < 2 * ZB, 1.0, inside("fast", 2))
    )
    blocks = (low, mid, high)
    masks = [row_mask * inside("slow", 0), row_mask, row_mask * inside("slow", 2)]
    for yb, ref in enumerate(blocks):

        def fill(y):
            for p in PARITIES:
                value = wide(ref, 0, p, y)
                s[(*p, yb * YB + y)] = jnp.where(masks[yb] > 0.5, value, 0.0)

        over(0, YB, 8, fill)
    for yb, ref in enumerate(blocks):

        def right_side(y):
            row = yb * YB + y
            here, beside = fine_neighbours(s, row, lanes)
            for p in PARITIES:
                if first:
                    full = wide(ref, 2, p, y) + 6.0
                    gain = (OMEGA / full) * masks[yb]
                    k[(*p, row)] = gain
                    if yb == 1:
                        dn[(*p, y)] = full * (1.0 / OMEGA)
                else:
                    gain = k[(*p, row)]
                start = gain * (wide(ref, 1, p, y) + beside[p]) - OMEGA * here[p]
                q[(*p, row)] = start
                a[(*p, row)] = start
                b[(*p, row)] = start

        if yb == 1:
            over(0, YB, 4, right_side)
        else:
            over(1 - yb // 2, YB - yb // 2, 7, right_side)

    @pl.when(sweeps[0] >= 4)
    def _():
        fine_sweep(a, b, q, k, 2, 22, 10, lanes)

    @pl.when(sweeps[0] >= 3)
    def _():
        fine_sweep(b, a, q, k, 3, 21, 9, lanes)

    fine_sweep(a, epre, q, k, 4, 20, 8, lanes, shift=4)
    zero = jnp.zeros((ZW, LANES), F32)

    def restrict(ym):
        total = zero
        diag = zero
        for half in range(2):
            row = YB + 2 * ym + half
            here, beside = fine_neighbours(epre, row - 4, lanes)
            for p in PARITIES:
                scaled = q[(*p, row)] - OMEGA * here[p] + k[(*p, row)] * beside[p]
                total = total + scaled * dn[(*p, 2 * ym + half)]
                if first:
                    diag = diag + wide(mid, 2, p, 2 * ym + half)
        for n, value in enumerate((total, diag) if first else (total,)):
            value = value * 0.125
            right_out[n, ym] = value[: 2 * ZB]
            own_out[n, ym] = value[ZB : 2 * ZB]
            left_out[n, ym] = value[ZB:]

    over(0, YB // 2, 4, restrict)


def coarse_kernel(first, sweeps, *refs):
    window = refs[0]
    if first:
        part, e1, q1, e2_out, k1, d1, k2, d2, g2sum = refs[1:10]
        va, t, wa, wb, q2, x2 = refs[10:]
    else:
        k1, d1, k2, d2, g2sum = refs[1:6]
        part, e1, q1, e2_out = refs[6:10]
        va, t, wa, wb, q2, x2 = refs[10:]
    fast = lax.axis_index("fast")
    slow = lax.axis_index("slow")
    lanes = lane_iota(ZM)
    even = (lanes & 1) == 0
    zrow = row_iota(ZM) + (fast * ZB - 2 * ZB)
    mask = jnp.where((zrow >= 0) & (zrow < lax.axis_size("fast") * ZB), 1.0, 0.0).astype(F32)
    zero = jnp.zeros((ZM, LANES), F32)
    for n in (*range(PADM), *range(PADM + YM, YM + 2 * PADM)):
        va[n] = zero
        e1[n] = zero
        q1[n] = zero
        if first:
            k1[n] = zero

    def opening(block):
        for ym in range(4):
            y = block * 4 + ym
            if first:
                full = window[block, 1, ym] + 1.5
                gain = (OMEGA / full) * mask
                k1[PADM + y] = gain * 0.25
                d1[y] = full * (1.0 / OMEGA)
                start = gain * window[block, 0, ym]
            else:
                start = (4.0 * k1[PADM + y]) * window[block, 0, ym]
            q1[PADM + y] = start
            va[PADM + y] = start
            e1[PADM + y] = start

    over(0, YM // 4, 2, opening)
    of_q1, of_k1 = (lambda y: q1[y]), (lambda y: k1[y])

    @pl.when(sweeps[1] >= 4)
    def _():
        flat_sweep(va, e1, of_q1, of_k1, PADM, PADM + YM, 8, lanes, 1)

    @pl.when(sweeps[1] >= 3)
    def _():
        flat_sweep(e1, va, of_q1, of_k1, PADM, PADM + YM, 8, lanes, 1)

    flat_sweep(va, e1, of_q1, of_k1, PADM, PADM + YM, 8, lanes, 1)

    def pair_sum(value):
        return value + jnp.where(even, pltpu.roll(value, LANES - 1, 1), pltpu.roll(value, 1, 1))

    def restrict(yc):
        total = zero
        for half in range(2):
            y = PADM + 2 * yc + half
            here, beside = flat_neighbours(e1, y, lanes, 1)
            total = total + (q1[y] - OMEGA * here + k1[y] * beside) * d1[2 * yc + half]
        t[yc, :ZM] = pair_sum(total)
        t[yc, ZM:] = jnp.zeros((8, LANES), F32)

    over(0, YM // 2, 4, restrict)
    lanes2 = lane_iota(24)
    rows2 = row_iota(24)
    zrow2 = rows2 + (fast * 4 - 8)
    mask2 = jnp.where(
        (zrow2 >= 0) & (zrow2 < lax.axis_size("fast") * 4) & (rows2 < 20), 1.0, 0.0
    ).astype(F32)
    own = jnp.where((rows2 >= 8) & (rows2 < 12), 0.5, 0.0).astype(F32)
    zero2 = jnp.zeros((24, LANES), F32)
    for n in (*range(PADL), *range(PADL + 16, 16 + 2 * PADL)):
        wa[n] = zero2
        wb[n] = zero2

    def halve(yc):
        return (t[yc, pl.ds(0, 24, stride=2), :] + t[yc, pl.ds(1, 24, stride=2), :]) * 0.125

    if first:
        for yc in range(16):
            q2[yc] = halve(yc)

        def coarse_diag(yc):
            block, ym = yc // 2, 2 * (yc % 2)
            t[yc, :ZM] = pair_sum(window[block, 1, ym] + window[block, 1, ym + 1])

        over(0, 16, 4, coarse_diag)
        total = zero2
        for yc in range(16):
            g2 = halve(yc)
            full = g2 + 0.375
            gain = (OMEGA / full) * mask2
            k2[yc] = gain * 0.0625
            d2[yc] = full * (1.0 / OMEGA)
            total = total + g2 * own
            start = gain * q2[yc]
            q2[yc] = start
            wa[PADL + yc] = start
            wb[PADL + yc] = start
        g2sum[...] = total
    else:
        for yc in range(16):
            start = (16.0 * k2[yc]) * halve(yc)
            q2[yc] = start
            wa[PADL + yc] = start
            wb[PADL + yc] = start
    of_q2, of_k2 = (lambda y: q2[y - PADL]), (lambda y: k2[y - PADL])

    @pl.when(sweeps[2] >= 4)
    def _():
        flat_sweep(wa, wb, of_q2, of_k2, PADL, PADL + 16, 16, lanes2, 2)

    @pl.when(sweeps[2] >= 3)
    def _():
        flat_sweep(wb, wa, of_q2, of_k2, PADL, PADL + 16, 16, lanes2, 2)

    flat_sweep(wa, wb, of_q2, of_k2, PADL, PADL + 16, 16, lanes2, 2)
    total = zero2
    for yc in range(16):
        here, beside = flat_neighbours(wb, yc + PADL, lanes2, 2)
        total = total + (q2[yc] - OMEGA * here + k2[yc] * beside) * d2[yc]
    numer = jnp.sum(total * own)
    denom = jnp.sum(g2sum[...])
    lanes_p = lane_iota(part.shape[0])
    part[...] = jnp.where(lanes_p == 0, numer, jnp.where(lanes_p == 1, denom, 0.0))
    for y in range(YPOST // 2):
        value = wb[2 * slow + (PADL - 3) + y]
        x2[y, pl.ds(0, 24, stride=2), :] = value
        x2[y, pl.ds(1, 24, stride=2), :] = value
        e2_out[y] = x2[y, ZB : 4 * ZB]


def after_kernel(last, faces, sweeps, parts, e1, q1, k1, e2, epre, q, k, field, later, out, va, vb, a, b, halves):
    lanes = lane_iota(ZW)
    lanes_p = lane_iota(parts.shape[0])
    every = parts[...]
    numer = jnp.sum(jnp.where(lanes_p == 0, every, 0.0))
    denom = jnp.sum(jnp.where(lanes_p == 1, every, 0.0)) + 0.0625 * faces
    shift = jnp.full((ZW, LANES), numer, F32) / jnp.full((ZW, LANES), denom, F32)
    base = 4 * lax.axis_index("slow") + (PADM - 6)

    def of_q1(y):
        return q1[base + y, ZB : 4 * ZB]

    def of_k1(y):
        return k1[base + y, ZB : 4 * ZB]

    for y in range(YPOST):
        raised = e1[base + y, ZB : 4 * ZB] + (e2[y // 2] + shift)
        raised = jnp.where(of_k1(y) > 0.0, raised, 0.0)
        va[y] = raised
        vb[y] = raised

    @pl.when(sweeps[1] >= 4)
    def _():
        flat_sweep(vb, va, of_q1, of_k1, 1, 15, 14, lanes, 1)

    @pl.when(sweeps[1] >= 3)
    def _():
        flat_sweep(va, vb, of_q1, of_k1, 2, 14, 12, lanes, 1)

    flat_sweep(vb, va, of_q1, of_k1, 3, 13, 10, lanes, 1)
    flat_sweep(va, vb, of_q1, of_k1, 4, 12, 8, lanes, 1)

    def raise_fine(ym):
        value = vb[ym + 4]
        for half in range(2):
            y = 2 * ym + half
            for p in PARITIES:
                raised = jnp.where(k[(*p, y + 4)] > 0.0, epre[(*p, y)] + value, 0.0)
                a[(*p, y)] = raised
                b[(*p, y)] = raised

    over(0, YPOST // 2, 4, raise_fine)

    @pl.when(sweeps[0] >= 4)
    def _():
        fine_sweep(b, a, q, k, 1, 15, 7, lanes, offset=4)

    @pl.when(sweeps[0] >= 3)
    def _():
        fine_sweep(a, b, q, k, 2, 14, 6, lanes, offset=4)

    fine_sweep(b, a, q, k, 3, 13, 10, lanes, offset=4)
    fine_sweep(a, b, q, k, 4, 12, 8, lanes, offset=4)
    for pz, px in PARITIES:
        value = field[pz, px] + 0.5 * b[pz, px, 4:12, ZB : 2 * ZB]
        if last:
            halves[px, pl.ds(pz, YB * ZB, stride=2), :] = value.reshape(YB * ZB, LANES)
        else:
            out[0, pz, px] = value
            out[1, pz, px] = later[pz, px]
    if last:
        both = jnp.concatenate([halves[0], halves[1]], axis=1)
        out[...] = exact_dot(both, parity_matrix(True)).reshape(YB, 2 * ZB, 2 * LANES)


def call(kernel, outs, scratch, scalars, *arrays, space=pltpu.VMEM, megabytes=16, kept=True):
    specs = [pl.BlockSpec(memory_space=pltpu.SMEM)] * len(scalars)
    if space == pltpu.HBM:
        arrays = [pltpu.with_memory_space_constraint(x, pltpu.HBM) for x in arrays]
    return pl.pallas_call(
        kernel,
        out_shape=[pltpu.VMEM(s, F32) if kept else jax.ShapeDtypeStruct(s, F32) for s in outs],
        in_specs=specs + [pl.BlockSpec(memory_space=space)] * len(arrays),
        out_specs=[pl.BlockSpec(memory_space=pltpu.VMEM)] * len(outs),
        scratch_shapes=[pltpu.VMEM(s, F32) if isinstance(s, tuple) else s for s in scratch],
        compiler_params=pltpu.CompilerParams(vmem_limit_bytes=megabytes * 1024 * 1024),
    )(*scalars, *arrays)


def both_ways(to_right, to_left, axis):
    count = lax.axis_size(axis)
    up = [(i, (i + 1) % count) for i in range(count)]
    down = [(target, source) for source, target in up]
    return lax.ppermute(to_right, axis, up), lax.ppermute(to_left, axis, down)


def window_of(fields):
    left, right = both_ways(fields, fields, "fast")
    mid = jnp.stack([left, fields, right])
    low, high = both_ways(mid, mid, "slow")
    return mid, low, high


def body(observed, start_field, diagonal, noise, sweeps):
    natural = observed.shape
    block = (2, 2, YB, ZB, LANES)
    post = (2, 2, YPOST, ZW, LANES)
    whole = (2, 2, YW, ZW, LANES)
    middle = (YM + 2 * PADM, ZM, LANES)
    low_window = (16, 24, LANES)
    fast_count, slow_count = lax.axis_size("fast"), lax.axis_size("slow")
    first, second, third = YB * slow_count // 4, 2 * ZB * fast_count // 4, 2 * LANES // 4
    faces = 2.0 * (first * second + first * third + second * third)
    fields, later = call(
        split_kernel, [(3, *block), block],
        [natural, natural, natural, (2, *natural), (4, 2, YB * 2 * ZB, LANES), pltpu.SemaphoreType.DMA((4,))],
        (), observed, start_field, diagonal, noise, space=pltpu.HBM,
    )
    field = fields[0]
    kept_fine = kept_low = None
    for step in range(2):
        opening = step == 0
        count = 2 if opening else 1
        mid, low, high = window_of(fields)
        outs = [(count, 4, 16, LANES), (count, 4, 8, LANES), (count, 4, 16, LANES), post, whole]
        if opening:
            outs += [whole, (2, 2, YB, ZW, LANES)]
            given = (mid, low, high)
        else:
            given = (mid, low, high, *kept_fine)
        got = call(functools.partial(before_kernel, opening), outs, [whole] * 3, (sweeps,), *given)
        to_left, own, to_right, epre, q = got[:5]
        if opening:
            kept_fine = got[5:]
        left, right = both_ways(to_right, to_left, "fast")
        strip = jnp.concatenate([left, own, right], axis=2)
        strip = jnp.broadcast_to(strip[None], (slow_count, *strip.shape))
        strip = lax.all_to_all(strip, "slow", 0, 0, tiled=True)
        outs = [(fast_count, LANES), middle, middle, (YPOST // 2, ZW, LANES)]
        scratch = [
            middle, (16, ZM + 8, LANES), (16 + 2 * PADL, 24, LANES), (16 + 2 * PADL, 24, LANES),
            low_window, (YPOST // 2, 48, LANES),
        ]
        if opening:
            outs += [middle, (YM, ZM, LANES), low_window, low_window, (24, LANES)]
            given = (strip,)
        else:
            given = (strip, *kept_low)
        got = call(functools.partial(coarse_kernel, opening), outs, scratch, (sweeps,), *given)
        part, e1, q1, e2 = got[:4]
        if opening:
            kept_low = got[4:]
        parts = lax.all_to_all(part, "fast", 0, 0, tiled=True)
        outs = [(2, *block) if opening else natural]
        scratch = [(YPOST, ZW, LANES)] * 2 + [post] * 2 + [(2, YB * 2 * ZB, LANES)]
        (fields,) = call(
            functools.partial(after_kernel, not opening, faces), outs, scratch, (sweeps,),
            parts, e1, q1, kept_low[0], e2, epre, q, kept_fine[0], field, later, kept=opening,
        )
        field = fields[0]
    return fields


def solution(mesh):
    placed = (
        P("slow", "fast", None),
        P("slow", "fast", None),
        P("slow", "fast", None),
        P(None, "slow", "fast", None),
        P(),
    )
    return jax.shard_map(
        body, mesh=mesh, in_specs=placed, out_specs=P("slow", "fast", None), check_vma=False
    )
```

```python
import functools

import jax
import jax.numpy as jnp
from jax import lax
from jax.experimental import pallas as pl
from jax.experimental.pallas import tpu as pltpu
from jax.sharding import PartitionSpec as P

OMEGA = 0.7
KEEP = 1.0 - OMEGA
F32 = jnp.float32

YB, ZB, LANES = 8, 8, 128
YW, ZW = 3 * YB, 3 * ZB
ZM, YM = 40, 32
YPOST = 16
PADM, PADL = 8, 4
PARITIES = ((0, 0), (0, 1), (1, 0), (1, 1))


def lane_iota(rows):
    return lax.broadcasted_iota(jnp.int32, (rows, LANES), 1)


def row_iota(rows):
    return lax.broadcasted_iota(jnp.int32, (rows, LANES), 0)


def parity_matrix(transposed):
    row = lax.broadcasted_iota(jnp.int32, (2 * LANES, 2 * LANES), 0)
    col = lax.broadcasted_iota(jnp.int32, (2 * LANES, 2 * LANES), 1)
    if transposed:
        row, col = col, row
    return jnp.where(row == 2 * (col & (LANES - 1)) + (col >> 7), 1.0, 0.0).astype(F32)


def exact_dot(a, b):
    return lax.dot(a, b, precision=lax.Precision.HIGHEST, preferred_element_type=F32)


def over(low, high, chunk, one):
    turns, rest = divmod(high - low, chunk)
    assert rest == 0
    if turns == 1:
        for n in range(chunk):
            one(low + n)
        return

    def turn(at, carry):
        for n in range(chunk):
            one(low + at * chunk + n)
        return carry

    lax.fori_loop(0, turns, turn, 0)


def fine_neighbours(u, y, lanes):
    rows = u.shape[-2]
    here = {p: u[(*p, y)] for p in PARITIES}
    beside = {}
    for pz, px in PARITIES:
        total = u[pz, px, y - 1] + u[pz, px, y + 1]
        other = here[1 - pz, px]
        total = total + (other + pltpu.roll(other, 1 if pz == 0 else rows - 1, 0))
        other = here[pz, 1 - px]
        if px == 0:
            moved = jnp.where(lanes == 0, 0.0, pltpu.roll(other, 1, 1))
        else:
            moved = jnp.where(lanes == LANES - 1, 0.0, pltpu.roll(other, LANES - 1, 1))
        beside[pz, px] = total + (other + moved)
    return here, beside


def flat_neighbours(u, y, lanes, step):
    rows = u.shape[-2]
    here = u[y]
    total = u[y - 1] + u[y + 1]
    total = total + (pltpu.roll(here, 1, 0) + pltpu.roll(here, rows - 1, 0))
    left = jnp.where(lanes < step, 0.0, pltpu.roll(here, step, 1))
    right = jnp.where(lanes >= LANES - step, 0.0, pltpu.roll(here, LANES - step, 1))
    return here, total + (left + right)


def fine_sweep(source, target, q, k, low, high, chunk, lanes, shift=0, offset=0):
    def one(y):
        here, beside = fine_neighbours(source, y, lanes)
        for p in PARITIES:
            target[(*p, y - shift)] = (
                KEEP * here[p] + q[(*p, y + offset)] + k[(*p, y + offset)] * beside[p]
            )

    over(low, high, chunk, one)


def flat_sweep(source, target, q, k, low, high, chunk, lanes, step):
    def one(y):
        here, beside = flat_neighbours(source, y, lanes, step)
        target[y] = KEEP * here + q(y) + k(y) * beside

    over(low, high, chunk, one)


def split_kernel(observed, start, diagonal, noise, fields, later, a, b, c, d, halves, sems):
    copies = [
        pltpu.make_async_copy(source, target, sems.at[n])
        for n, (source, target) in enumerate(((start, a), (diagonal, b), (observed, c), (noise, d)))
    ]
    for copy in copies:
        copy.start()
    matrix = parity_matrix(False)

    def split(n, value, out):
        both = exact_dot(value.reshape(YB * 2 * ZB, 2 * LANES), matrix)
        for px in range(2):
            halves[n, px] = both[:, px * LANES : (px + 1) * LANES]
        for pz, px in PARITIES:
            part = halves[n, px, pl.ds(pz, YB * ZB, stride=2), :]
            out[pz, px] = part.reshape(YB, ZB, LANES)

    copies[0].wait()
    split(0, a[...], fields.at[0])
    copies[1].wait()
    split(1, b[...], fields.at[2])
    copies[2].wait()
    copies[3].wait()
    split(2, c[...] + 2.0 * d[0], fields.at[1])
    split(3, c[...] + 2.0 * d[1], later)


def inside(axis, which):
    at = lax.axis_index(axis) + (which - 1)
    return jnp.where((at >= 0) & (at < lax.axis_size(axis)), 1.0, 0.0).astype(F32)


def wide(ref, field, p, y):
    return jnp.concatenate([ref[(zb, field, *p, y)] for zb in range(3)], axis=0)


def before_kernel(first, sweeps, *refs):
    if first:
        mid, low, high = refs[:3]
        left_out, own_out, right_out, epre, q, k, dn = refs[3:10]
        s, a, b = refs[10:]
    else:
        mid, low, high, k, dn = refs[:5]
        left_out, own_out, right_out, epre, q = refs[5:10]
        s, a, b = refs[10:]
    lanes = lane_iota(ZW)
    rows = row_iota(ZW)
    row_mask = jnp.where(
        rows < ZB, inside("fast", 0), jnp.where(rows < 2 * ZB, 1.0, inside("fast", 2))
    )
    blocks = (low, mid, high)
    masks = [row_mask * inside("slow", 0), row_mask, row_mask * inside("slow", 2)]
    for yb, ref in enumerate(blocks):

        def fill(y):
            for p in PARITIES:
                value = wide(ref, 0, p, y)
                s[(*p, yb * YB + y)] = jnp.where(masks[yb] > 0.5, value, 0.0)

        over(0, YB, 8, fill)
    for yb, ref in enumerate(blocks):

        def right_side(y):
            row = yb * YB + y
            here, beside = fine_neighbours(s, row, lanes)
            for p in PARITIES:
                if first:
                    full = wide(ref, 2, p, y) + 6.0
                    gain = (OMEGA / full) * masks[yb]
                    k[(*p, row)] = gain
                    if yb == 1:
                        dn[(*p, y)] = full * (1.0 / OMEGA)
                else:
                    gain = k[(*p, row)]
                start = gain * (wide(ref, 1, p, y) + beside[p]) - OMEGA * here[p]
                q[(*p, row)] = start
                a[(*p, row)] = start
                b[(*p, row)] = start

        if yb == 1:
            over(0, YB, 4, right_side)
        else:
            over(1 - yb // 2, YB - yb // 2, 7, right_side)

    @pl.when(sweeps[0] >= 4)
    def _():
        fine_sweep(a, b, q, k, 2, 22, 10, lanes)

    @pl.when(sweeps[0] >= 3)
    def _():
        fine_sweep(b, a, q, k, 3, 21, 9, lanes)

    fine_sweep(a, epre, q, k, 4, 20, 8, lanes, shift=4)
    zero = jnp.zeros((ZW, LANES), F32)

    def restrict(ym):
        total = zero
        diag = zero
        for half in range(2):
            row = YB + 2 * ym + half
            here, beside = fine_neighbours(epre, row - 4, lanes)
            for p in PARITIES:
                scaled = q[(*p, row)] - OMEGA * here[p] + k[(*p, row)] * beside[p]
                total = total + scaled * dn[(*p, 2 * ym + half)]
                if first:
                    diag = diag + wide(mid, 2, p, 2 * ym + half)
        for n, value in enumerate((total, diag) if first else (total,)):
            value = value * 0.125
            right_out[n, ym] = value[: 2 * ZB]
            own_out[n, ym] = value[ZB : 2 * ZB]
            left_out[n, ym] = value[ZB:]

    over(0, YB // 2, 4, restrict)


def coarse_kernel(first, sweeps, *refs):
    window = refs[0]
    if first:
        part, e1, q1, e2_out, k1, d1, k2, d2, g2sum = refs[1:10]
        va, t, wa, wb, q2, x2 = refs[10:]
    else:
        k1, d1, k2, d2, g2sum = refs[1:6]
        part, e1, q1, e2_out = refs[6:10]
        va, t, wa, wb, q2, x2 = refs[10:]
    fast = lax.axis_index("fast")
    slow = lax.axis_index("slow")
    lanes = lane_iota(ZM)
    even = (lanes & 1) == 0
    zrow = row_iota(ZM) + (fast * ZB - 2 * ZB)
    mask = jnp.where((zrow >= 0) & (zrow < lax.axis_size("fast") * ZB), 1.0, 0.0).astype(F32)
    zero = jnp.zeros((ZM, LANES), F32)
    for n in (*range(PADM), *range(PADM + YM, YM + 2 * PADM)):
        va[n] = zero
        e1[n] = zero
        q1[n] = zero
        if first:
            k1[n] = zero

    def opening(block):
        for ym in range(4):
            y = block * 4 + ym
            if first:
                full = window[block, 1, ym] + 1.5
                gain = (OMEGA / full) * mask
                k1[PADM + y] = gain * 0.25
                d1[y] = full * (1.0 / OMEGA)
                start = gain * window[block, 0, ym]
            else:
                start = (4.0 * k1[PADM + y]) * window[block, 0, ym]
            q1[PADM + y] = start
            va[PADM + y] = start
            e1[PADM + y] = start

    over(0, YM // 4, 2, opening)
    of_q1, of_k1 = (lambda y: q1[y]), (lambda y: k1[y])

    @pl.when(sweeps[1] >= 4)
    def _():
        flat_sweep(va, e1, of_q1, of_k1, PADM, PADM + YM, 8, lanes, 1)

    @pl.when(sweeps[1] >= 3)
    def _():
        flat_sweep(e1, va, of_q1, of_k1, PADM, PADM + YM, 8, lanes, 1)

    flat_sweep(va, e1, of_q1, of_k1, PADM, PADM + YM, 8, lanes, 1)

    def pair_sum(value):
        return value + jnp.where(even, pltpu.roll(value, LANES - 1, 1), pltpu.roll(value, 1, 1))

    def restrict(yc):
        total = zero
        for half in range(2):
            y = PADM + 2 * yc + half
            here, beside = flat_neighbours(e1, y, lanes, 1)
            total = total + (q1[y] - OMEGA * here + k1[y] * beside) * d1[2 * yc + half]
        t[yc, :ZM] = pair_sum(total)
        t[yc, ZM:] = jnp.zeros((8, LANES), F32)

    over(0, YM // 2, 4, restrict)
    lanes2 = lane_iota(24)
    rows2 = row_iota(24)
    zrow2 = rows2 + (fast * 4 - 8)
    mask2 = jnp.where(
        (zrow2 >= 0) & (zrow2 < lax.axis_size("fast") * 4) & (rows2 < 20), 1.0, 0.0
    ).astype(F32)
    own = jnp.where((rows2 >= 8) & (rows2 < 12), 0.5, 0.0).astype(F32)
    zero2 = jnp.zeros((24, LANES), F32)
    for n in (*range(PADL), *range(PADL + 16, 16 + 2 * PADL)):
        wa[n] = zero2
        wb[n] = zero2

    def halve(yc):
        return (t[yc, pl.ds(0, 24, stride=2), :] + t[yc, pl.ds(1, 24, stride=2), :]) * 0.125

    if first:
        for yc in range(16):
            q2[yc] = halve(yc)

        def coarse_diag(yc):
            block, ym = yc // 2, 2 * (yc % 2)
            t[yc, :ZM] = pair_sum(window[block, 1, ym] + window[block, 1, ym + 1])

        over(0, 16, 4, coarse_diag)
        total = zero2
        for yc in range(16):
            g2 = halve(yc)
            full = g2 + 0.375
            gain = (OMEGA / full) * mask2
            k2[yc] = gain * 0.0625
            d2[yc] = full * (1.0 / OMEGA)
            total = total + g2 * own
            start = gain * q2[yc]
            q2[yc] = start
            wa[PADL + yc] = start
            wb[PADL + yc] = start
        g2sum[...] = total
    else:
        for yc in range(16):
            start = (16.0 * k2[yc]) * halve(yc)
            q2[yc] = start
            wa[PADL + yc] = start
            wb[PADL + yc] = start
    of_q2, of_k2 = (lambda y: q2[y - PADL]), (lambda y: k2[y - PADL])

    @pl.when(sweeps[2] >= 4)
    def _():
        flat_sweep(wa, wb, of_q2, of_k2, PADL, PADL + 16, 16, lanes2, 2)

    @pl.when(sweeps[2] >= 3)
    def _():
        flat_sweep(wb, wa, of_q2, of_k2, PADL, PADL + 16, 16, lanes2, 2)

    flat_sweep(wa, wb, of_q2, of_k2, PADL, PADL + 16, 16, lanes2, 2)
    total = zero2
    for yc in range(16):
        here, beside = flat_neighbours(wb, yc + PADL, lanes2, 2)
        total = total + (q2[yc] - OMEGA * here + k2[yc] * beside) * d2[yc]
    numer = jnp.sum(total * own)
    denom = jnp.sum(g2sum[...])
    lanes_p = lane_iota(part.shape[0])
    part[...] = jnp.where(lanes_p == 0, numer, jnp.where(lanes_p == 1, denom, 0.0))
    for y in range(YPOST // 2):
        value = wb[2 * slow + (PADL - 3) + y]
        x2[y, pl.ds(0, 24, stride=2), :] = value
        x2[y, pl.ds(1, 24, stride=2), :] = value
        e2_out[y] = x2[y, ZB : 4 * ZB]


def after_kernel(last, faces, sweeps, parts, e1, q1, k1, e2, epre, q, k, fields, later, out, va, vb, a, b, halves):
    lanes = lane_iota(ZW)
    lanes_p = lane_iota(parts.shape[0])
    every = parts[...]
    numer = jnp.sum(jnp.where(lanes_p == 0, every, 0.0))
    denom = jnp.sum(jnp.where(lanes_p == 1, every, 0.0)) + 0.0625 * faces
    shift = jnp.full((ZW, LANES), numer, F32) / jnp.full((ZW, LANES), denom, F32)
    base = 4 * lax.axis_index("slow") + (PADM - 6)

    def of_q1(y):
        return q1[base + y, ZB : 4 * ZB]

    def of_k1(y):
        return k1[base + y, ZB : 4 * ZB]

    for y in range(YPOST):
        raised = e1[base + y, ZB : 4 * ZB] + (e2[y // 2] + shift)
        raised = jnp.where(of_k1(y) > 0.0, raised, 0.0)
        va[y] = raised
        vb[y] = raised

    @pl.when(sweeps[1] >= 4)
    def _():
        flat_sweep(vb, va, of_q1, of_k1, 1, 15, 14, lanes, 1)

    @pl.when(sweeps[1] >= 3)
    def _():
        flat_sweep(va, vb, of_q1, of_k1, 2, 14, 12, lanes, 1)

    flat_sweep(vb, va, of_q1, of_k1, 3, 13, 10, lanes, 1)
    flat_sweep(va, vb, of_q1, of_k1, 4, 12, 8, lanes, 1)

    def raise_fine(ym):
        value = vb[ym + 4]
        for half in range(2):
            y = 2 * ym + half
            for p in PARITIES:
                raised = jnp.where(k[(*p, y + 4)] > 0.0, epre[(*p, y)] + value, 0.0)
                a[(*p, y)] = raised
                b[(*p, y)] = raised

    over(0, YPOST // 2, 4, raise_fine)

    @pl.when(sweeps[0] >= 4)
    def _():
        fine_sweep(b, a, q, k, 1, 15, 7, lanes, offset=4)

    @pl.when(sweeps[0] >= 3)
    def _():
        fine_sweep(a, b, q, k, 2, 14, 6, lanes, offset=4)

    fine_sweep(b, a, q, k, 3, 13, 10, lanes, offset=4)
    fine_sweep(a, b, q, k, 4, 12, 8, lanes, offset=4)
    for pz, px in PARITIES:
        value = fields[0, pz, px] + 0.5 * b[pz, px, 4:12, ZB : 2 * ZB]
        if last:
            halves[px, pl.ds(pz, YB * ZB, stride=2), :] = value.reshape(YB * ZB, LANES)
        else:
            out[0, pz, px] = value
            out[1, pz, px] = later[pz, px]
    if last:
        both = jnp.concatenate([halves[0], halves[1]], axis=1)
        out[...] = exact_dot(both, parity_matrix(True)).reshape(YB, 2 * ZB, 2 * LANES)


def call(kernel, outs, scratch, scalars, *arrays, space=pltpu.VMEM, megabytes=16, kept=True):
    specs = [pl.BlockSpec(memory_space=pltpu.SMEM)] * len(scalars)
    if space == pltpu.HBM:
        arrays = [pltpu.with_memory_space_constraint(x, pltpu.HBM) for x in arrays]
    return pl.pallas_call(
        kernel,
        out_shape=[pltpu.VMEM(s, F32) if kept else jax.ShapeDtypeStruct(s, F32) for s in outs],
        in_specs=specs + [pl.BlockSpec(memory_space=space)] * len(arrays),
        out_specs=[pl.BlockSpec(memory_space=pltpu.VMEM)] * len(outs),
        scratch_shapes=[pltpu.VMEM(s, F32) if isinstance(s, tuple) else s for s in scratch],
        compiler_params=pltpu.CompilerParams(vmem_limit_bytes=megabytes * 1024 * 1024),
    )(*scalars, *arrays)


def both_ways(to_right, to_left, axis):
    count = lax.axis_size(axis)
    up = [(i, (i + 1) % count) for i in range(count)]
    down = [(target, source) for source, target in up]
    return lax.ppermute(to_right, axis, up), lax.ppermute(to_left, axis, down)


def window_of(fields):
    left, right = both_ways(fields, fields, "fast")
    mid = jnp.stack([left, fields, right])
    low, high = both_ways(mid, mid, "slow")
    return mid, low, high


def body(observed, start_field, diagonal, noise, sweeps):
    natural = observed.shape
    block = (2, 2, YB, ZB, LANES)
    post = (2, 2, YPOST, ZW, LANES)
    whole = (2, 2, YW, ZW, LANES)
    middle = (YM + 2 * PADM, ZM, LANES)
    low_window = (16, 24, LANES)
    fast_count, slow_count = lax.axis_size("fast"), lax.axis_size("slow")
    first, second, third = YB * slow_count // 4, 2 * ZB * fast_count // 4, 2 * LANES // 4
    faces = 2.0 * (first * second + first * third + second * third)
    fields, later = call(
        split_kernel, [(3, *block), block],
        [natural, natural, natural, (2, *natural), (4, 2, YB * 2 * ZB, LANES), pltpu.SemaphoreType.DMA((4,))],
        (), observed, start_field, diagonal, noise, space=pltpu.HBM,
    )
    kept_fine = kept_low = None
    for step in range(2):
        opening = step == 0
        count = 2 if opening else 1
        mid, low, high = window_of(fields)
        outs = [(count, 4, 16, LANES), (count, 4, 8, LANES), (count, 4, 16, LANES), post, whole]
        if opening:
            outs += [whole, (2, 2, YB, ZW, LANES)]
            given = (mid, low, high)
        else:
            given = (mid, low, high, *kept_fine)
        got = call(functools.partial(before_kernel, opening), outs, [whole] * 3, (sweeps,), *given)
        to_left, own, to_right, epre, q = got[:5]
        if opening:
            kept_fine = got[5:]
        left, right = both_ways(to_right, to_left, "fast")
        strip = jnp.concatenate([left, own, right], axis=2)
        strip = jnp.broadcast_to(strip[None], (slow_count, *strip.shape))
        strip = lax.all_to_all(strip, "slow", 0, 0, tiled=True)
        outs = [(fast_count, LANES), middle, middle, (YPOST // 2, ZW, LANES)]
        scratch = [
            middle, (16, ZM + 8, LANES), (16 + 2 * PADL, 24, LANES), (16 + 2 * PADL, 24, LANES),
            low_window, (YPOST // 2, 48, LANES),
        ]
        if opening:
            outs += [middle, (YM, ZM, LANES), low_window, low_window, (24, LANES)]
            given = (strip,)
        else:
            given = (strip, *kept_low)
        got = call(functools.partial(coarse_kernel, opening), outs, scratch, (sweeps,), *given)
        part, e1, q1, e2 = got[:4]
        if opening:
            kept_low = got[4:]
        parts = lax.all_to_all(part, "fast", 0, 0, tiled=True)
        outs = [(2, *block) if opening else natural]
        scratch = [(YPOST, ZW, LANES)] * 2 + [post] * 2 + [(2, YB * 2 * ZB, LANES)]
        (fields,) = call(
            functools.partial(after_kernel, not opening, faces), outs, scratch, (sweeps,),
            parts, e1, q1, kept_low[0], e2, epre, q, kept_fine[0], fields, later, kept=opening,
        )
    return fields


def solution(mesh):
    placed = (
        P("slow", "fast", None),
        P("slow", "fast", None),
        P("slow", "fast", None),
        P(None, "slow", "fast", None),
        P(),
    )
    return jax.shard_map(
        body, mesh=mesh, in_specs=placed, out_specs=P("slow", "fast", None), check_vma=False
    )
```

```python
import functools

import jax
import jax.numpy as jnp
from jax import lax
from jax.experimental import pallas as pl
from jax.experimental.pallas import tpu as pltpu
from jax.sharding import PartitionSpec as P

OMEGA = 0.7
KEEP = 1.0 - OMEGA
F32 = jnp.float32

YB, ZB, LANES = 8, 8, 128
YW, ZW = 3 * YB, 3 * ZB
ZM, YM = 40, 32
YPOST = 16
PADM, PADL = 8, 4
PARITIES = ((0, 0), (0, 1), (1, 0), (1, 1))


def lane_iota(rows):
    return lax.broadcasted_iota(jnp.int32, (rows, LANES), 1)


def row_iota(rows):
    return lax.broadcasted_iota(jnp.int32, (rows, LANES), 0)


def parity_matrix(transposed):
    row = lax.broadcasted_iota(jnp.int32, (2 * LANES, 2 * LANES), 0)
    col = lax.broadcasted_iota(jnp.int32, (2 * LANES, 2 * LANES), 1)
    if transposed:
        row, col = col, row
    return jnp.where(row == 2 * (col & (LANES - 1)) + (col >> 7), 1.0, 0.0).astype(F32)


def exact_dot(a, b):
    return lax.dot(a, b, precision=lax.Precision.HIGHEST, preferred_element_type=F32)


def over(low, high, chunk, one):
    turns, rest = divmod(high - low, chunk)
    assert rest == 0
    if turns == 1:
        for n in range(chunk):
            one(low + n)
        return

    def turn(at, carry):
        for n in range(chunk):
            one(low + at * chunk + n)
        return carry

    lax.fori_loop(0, turns, turn, 0)


def fine_neighbours(u, y, lanes):
    rows = u.shape[-2]
    here = {p: u[(*p, y)] for p in PARITIES}
    beside = {}
    for pz, px in PARITIES:
        total = u[pz, px, y - 1] + u[pz, px, y + 1]
        other = here[1 - pz, px]
        total = total + (other + pltpu.roll(other, 1 if pz == 0 else rows - 1, 0))
        other = here[pz, 1 - px]
        if px == 0:
            moved = jnp.where(lanes == 0, 0.0, pltpu.roll(other, 1, 1))
        else:
            moved = jnp.where(lanes == LANES - 1, 0.0, pltpu.roll(other, LANES - 1, 1))
        beside[pz, px] = total + (other + moved)
    return here, beside


def flat_neighbours(u, y, lanes, step):
    rows = u.shape[-2]
    here = u[y]
    total = u[y - 1] + u[y + 1]
    total = total + (pltpu.roll(here, 1, 0) + pltpu.roll(here, rows - 1, 0))
    left = jnp.where(lanes < step, 0.0, pltpu.roll(here, step, 1))
    right = jnp.where(lanes >= LANES - step, 0.0, pltpu.roll(here, LANES - step, 1))
    return here, total + (left + right)


def fine_sweep(source, target, q, k, low, high, chunk, lanes, shift=0, offset=0):
    def one(y):
        here, beside = fine_neighbours(source, y, lanes)
        for p in PARITIES:
            target[(*p, y - shift)] = (
                KEEP * here[p] + q[(*p, y + offset)] + k[(*p, y + offset)] * beside[p]
            )

    over(low, high, chunk, one)


def flat_sweep(source, target, q, k, low, high, chunk, lanes, step):
    def one(y):
        here, beside = flat_neighbours(source, y, lanes, step)
        target[y] = KEEP * here + q(y) + k(y) * beside

    over(low, high, chunk, one)


def closed_neighbours(u, y, lanes):
    rows = row_iota(ZB)
    here = {p: u[(*p, y)] for p in PARITIES}
    beside = {}
    for pz, px in PARITIES:
        total = u[pz, px, y - 1] + u[pz, px, y + 1]
        other = here[1 - pz, px]
        if pz == 0:
            moved = jnp.where(rows == 0, 0.0, pltpu.roll(other, 1, 0))
        else:
            moved = jnp.where(rows == ZB - 1, 0.0, pltpu.roll(other, ZB - 1, 0))
        total = total + (other + moved)
        other = here[pz, 1 - px]
        if px == 0:
            moved = jnp.where(lanes == 0, 0.0, pltpu.roll(other, 1, 1))
        else:
            moved = jnp.where(lanes == LANES - 1, 0.0, pltpu.roll(other, LANES - 1, 1))
        beside[pz, px] = total + (other + moved)
    return here, beside


def tile_of(p):
    return 2 * p[0] + p[1]


def pack_tiles(each):
    return 12 + 8 * each


def write_pack(s, linear, diag, out, each, lanes):
    for p in PARITIES:
        n = tile_of(p)
        out[n] = s[(*p, 1)]
        out[4 + 8 * each + n] = s[(*p, 8)]

    def one(y):
        here, beside = closed_neighbours(s, y + 1, lanes)
        for p in PARITIES:
            g = diag(p, y)
            out[4 + each * y + tile_of(p)] = linear(p, y) - (g + 6.0) * here[p] + beside[p]
            if each == 8:
                out[8 + each * y + tile_of(p)] = g

    for y in range(YB):
        one(y)
        for px in range(2):
            out[8 + 8 * each + px, y : y + 1] = s[0, px, y + 1, 0:1]
            out[10 + 8 * each + px, y : y + 1] = s[1, px, y + 1, ZB - 1 : ZB]


def zero_edges(s):
    for p in PARITIES:
        s[(*p, 0)] = jnp.zeros((ZB, LANES), F32)
        s[(*p, YB + 1)] = jnp.zeros((ZB, LANES), F32)


def split_kernel(observed, start, diagonal, noise, pack, field, later, a, b, c, d, halves, s, g, linear, sems):
    copies = [
        pltpu.make_async_copy(source, target, sems.at[n])
        for n, (source, target) in enumerate(((start, a), (diagonal, b), (observed, c), (noise, d)))
    ]
    for copy in copies:
        copy.start()
    matrix = parity_matrix(False)
    zero_edges(s)

    def split(n, value, *outs):
        both = exact_dot(value.reshape(YB * 2 * ZB, 2 * LANES), matrix)
        for px in range(2):
            halves[n, px] = both[:, px * LANES : (px + 1) * LANES]
        for pz, px in PARITIES:
            part = halves[n, px, pl.ds(pz, YB * ZB, stride=2), :].reshape(YB, ZB, LANES)
            for out in outs:
                out[pz, px] = part

    copies[0].wait()
    split(0, a[...], field, s.at[:, :, 1 : YB + 1])
    copies[1].wait()
    split(1, b[...], g)
    copies[2].wait()
    copies[3].wait()
    split(2, c[...] + 2.0 * d[0], linear)
    write_pack(s, lambda p, y: linear[(*p, y)], lambda p, y: g[(*p, y)], pack, 8, lane_iota(ZB))
    split(3, c[...] + 2.0 * d[1], later)


def inside(axis, which):
    at = lax.axis_index(axis) + (which - 1)
    return jnp.where((at >= 0) & (at < lax.axis_size(axis)), 1.0, 0.0).astype(F32)


def before_kernel(first, sweeps, *refs):
    across, low, high = refs[:3], refs[3], refs[4]
    if first:
        left_out, own_out, right_out, epre, q, k, dn = refs[5:12]
        a, b = refs[12:]
    else:
        k, dn = refs[5:7]
        left_out, own_out, right_out, epre, q = refs[7:12]
        a, b = refs[12:]
    each = 8 if first else 4
    lanes = lane_iota(ZW)
    rows = row_iota(ZW)
    tile_rows = row_iota(ZB)
    in_z = [inside("fast", n) for n in range(3)]
    in_y = [inside("slow", n) for n in range(3)]
    row_mask = jnp.where(rows < ZB, in_z[0], jnp.where(rows < 2 * ZB, 1.0, in_z[2]))
    masks = [row_mask * in_y[0], row_mask, row_mask * in_y[2]]

    def tile(yb, zb, n):
        if yb == 1:
            return across[zb].at[n]
        if yb == 0:
            return low.at[zb, n - (4 + each)]
        return high.at[zb, n]

    def z_face(yb, zb, which, px, y):
        n = 8 + 8 * each + 2 * which + px
        if yb == 2:
            n = 4 + 7 * each + 2 * which + px
        return tile(yb, zb, n)[pl.ds(y, 1), :]

    def wide(yb, n):
        return jnp.concatenate([tile(yb, zb, n)[...] for zb in range(3)], axis=0)

    def right_side(yb, y):
        row = yb * YB + y
        for p in PARITIES:
            pz, px = p
            tiles = [tile(yb, zb, 4 + each * y + tile_of(p))[...] for zb in range(3)]
            if pz == 1:
                edge = tile_rows == ZB - 1
                tiles[0] = tiles[0] + jnp.where(edge, z_face(yb, 1, 0, px, y), 0.0)
                tiles[1] = tiles[1] + jnp.where(edge, z_face(yb, 2, 0, px, y) * in_z[2], 0.0)
            else:
                edge = tile_rows == 0
                tiles[1] = tiles[1] + jnp.where(edge, z_face(yb, 0, 1, px, y) * in_z[0], 0.0)
                tiles[2] = tiles[2] + jnp.where(edge, z_face(yb, 1, 1, px, y), 0.0)
            rhs = jnp.concatenate(tiles, axis=0)
            if isinstance(y, int) and y == 0 and yb > 0:
                rhs = rhs + wide(yb - 1, 4 + 8 * each + tile_of(p)) * in_y[yb - 1]
            if isinstance(y, int) and y == YB - 1 and yb < 2:
                rhs = rhs + wide(yb + 1, tile_of(p)) * in_y[yb + 1]
            if first:
                full = wide(yb, 8 + each * y + tile_of(p)) + 6.0
                gain = (OMEGA / full) * masks[yb]
                k[(*p, row)] = gain
                if yb == 1:
                    dn[(*p, y)] = full * (1.0 / OMEGA)
            else:
                gain = k[(*p, row)]
            start = gain * rhs
            q[(*p, row)] = start
            a[(*p, row)] = start
            b[(*p, row)] = start

    for yb in range(3):
        over(1, YB - 1, 6, functools.partial(right_side, yb))
    right_side(0, YB - 1)
    right_side(1, 0)
    right_side(1, YB - 1)
    right_side(2, 0)

    @pl.when(sweeps[0] >= 4)
    def _():
        fine_sweep(a, b, q, k, 2, 22, 10, lanes)

    @pl.when(sweeps[0] >= 3)
    def _():
        fine_sweep(b, a, q, k, 3, 21, 9, lanes)

    fine_sweep(a, epre, q, k, 4, 20, 8, lanes, shift=4)
    zero = jnp.zeros((ZW, LANES), F32)

    def restrict(ym):
        total = zero
        diag = zero
        for half in range(2):
            row = YB + 2 * ym + half
            here, beside = fine_neighbours(epre, row - 4, lanes)
            for p in PARITIES:
                scaled = q[(*p, row)] - OMEGA * here[p] + k[(*p, row)] * beside[p]
                total = total + scaled * dn[(*p, 2 * ym + half)]
                if first:
                    diag = diag + wide(1, 8 + each * (2 * ym + half) + tile_of(p))
        for n, value in enumerate((total, diag) if first else (total,)):
            value = value * 0.125
            right_out[n, ym] = value[: 2 * ZB]
            own_out[n, ym] = value[ZB : 2 * ZB]
            left_out[n, ym] = value[ZB:]

    over(0, YB // 2, 4, restrict)


def coarse_kernel(first, sweeps, *refs):
    window = refs[0]
    if first:
        part, e1, q1, e2_out, k1, d1, k2, d2, g2sum = refs[1:10]
        va, t, wa, wb, q2, x2 = refs[10:]
    else:
        k1, d1, k2, d2, g2sum = refs[1:6]
        part, e1, q1, e2_out = refs[6:10]
        va, t, wa, wb, q2, x2 = refs[10:]
    fast = lax.axis_index("fast")
    slow = lax.axis_index("slow")
    lanes = lane_iota(ZM)
    even = (lanes & 1) == 0
    zrow = row_iota(ZM) + (fast * ZB - 2 * ZB)
    mask = jnp.where((zrow >= 0) & (zrow < lax.axis_size("fast") * ZB), 1.0, 0.0).astype(F32)
    zero = jnp.zeros((ZM, LANES), F32)
    for n in (*range(PADM), *range(PADM + YM, YM + 2 * PADM)):
        va[n] = zero
        e1[n] = zero
        q1[n] = zero
        if first:
            k1[n] = zero

    def opening(block):
        for ym in range(4):
            y = block * 4 + ym
            if first:
                full = window[block, 1, ym] + 1.5
                gain = (OMEGA / full) * mask
                k1[PADM + y] = gain * 0.25
                d1[y] = full * (1.0 / OMEGA)
                start = gain * window[block, 0, ym]
            else:
                start = (4.0 * k1[PADM + y]) * window[block, 0, ym]
            q1[PADM + y] = start
            va[PADM + y] = start
            e1[PADM + y] = start

    over(0, YM // 4, 2, opening)
    of_q1, of_k1 = (lambda y: q1[y]), (lambda y: k1[y])

    @pl.when(sweeps[1] >= 4)
    def _():
        flat_sweep(va, e1, of_q1, of_k1, PADM, PADM + YM, 8, lanes, 1)

    @pl.when(sweeps[1] >= 3)
    def _():
        flat_sweep(e1, va, of_q1, of_k1, PADM, PADM + YM, 8, lanes, 1)

    flat_sweep(va, e1, of_q1, of_k1, PADM, PADM + YM, 8, lanes, 1)

    def pair_sum(value):
        return value + jnp.where(even, pltpu.roll(value, LANES - 1, 1), pltpu.roll(value, 1, 1))

    def restrict(yc):
        total = zero
        for half in range(2):
            y = PADM + 2 * yc + half
            here, beside = flat_neighbours(e1, y, lanes, 1)
            total = total + (q1[y] - OMEGA * here + k1[y] * beside) * d1[2 * yc + half]
        t[yc, :ZM] = pair_sum(total)
        t[yc, ZM:] = jnp.zeros((8, LANES), F32)

    over(0, YM // 2, 4, restrict)
    lanes2 = lane_iota(24)
    rows2 = row_iota(24)
    zrow2 = rows2 + (fast * 4 - 8)
    mask2 = jnp.where(
        (zrow2 >= 0) & (zrow2 < lax.axis_size("fast") * 4) & (rows2 < 20), 1.0, 0.0
    ).astype(F32)
    own = jnp.where((rows2 >= 8) & (rows2 < 12), 0.5, 0.0).astype(F32)
    zero2 = jnp.zeros((24, LANES), F32)
    for n in (*range(PADL), *range(PADL + 16, 16 + 2 * PADL)):
        wa[n] = zero2
        wb[n] = zero2

    def halve(yc):
        return (t[yc, pl.ds(0, 24, stride=2), :] + t[yc, pl.ds(1, 24, stride=2), :]) * 0.125

    if first:
        for yc in range(16):
            q2[yc] = halve(yc)

        def coarse_diag(yc):
            block, ym = yc // 2, 2 * (yc % 2)
            t[yc, :ZM] = pair_sum(window[block, 1, ym] + window[block, 1, ym + 1])

        over(0, 16, 4, coarse_diag)
        total = zero2
        for yc in range(16):
            g2 = halve(yc)
            full = g2 + 0.375
            gain = (OMEGA / full) * mask2
            k2[yc] = gain * 0.0625
            d2[yc] = full * (1.0 / OMEGA)
            total = total + g2 * own
            start = gain * q2[yc]
            q2[yc] = start
            wa[PADL + yc] = start
            wb[PADL + yc] = start
        g2sum[...] = total
    else:
        for yc in range(16):
            start = (16.0 * k2[yc]) * halve(yc)
            q2[yc] = start
            wa[PADL + yc] = start
            wb[PADL + yc] = start
    of_q2, of_k2 = (lambda y: q2[y - PADL]), (lambda y: k2[y - PADL])

    @pl.when(sweeps[2] >= 4)
    def _():
        flat_sweep(wa, wb, of_q2, of_k2, PADL, PADL + 16, 16, lanes2, 2)

    @pl.when(sweeps[2] >= 3)
    def _():
        flat_sweep(wb, wa, of_q2, of_k2, PADL, PADL + 16, 16, lanes2, 2)

    flat_sweep(wa, wb, of_q2, of_k2, PADL, PADL + 16, 16, lanes2, 2)
    total = zero2
    for yc in range(16):
        here, beside = flat_neighbours(wb, yc + PADL, lanes2, 2)
        total = total + (q2[yc] - OMEGA * here + k2[yc] * beside) * d2[yc]
    numer = jnp.sum(total * own)
    denom = jnp.sum(g2sum[...])
    lanes_p = lane_iota(part.shape[0])
    part[...] = jnp.where(lanes_p == 0, numer, jnp.where(lanes_p == 1, denom, 0.0))
    for y in range(YPOST // 2):
        value = wb[2 * slow + (PADL - 3) + y]
        x2[y, pl.ds(0, 24, stride=2), :] = value
        x2[y, pl.ds(1, 24, stride=2), :] = value
        e2_out[y] = x2[y, ZB : 4 * ZB]


def after_kernel(last, faces, sweeps, *refs):
    if last:
        parts, e1, q1, k1, e2, epre, q, k, field, out, va, vb, a, b, halves = refs
    else:
        parts, e1, q1, k1, e2, epre, q, k, field, later, pack, out, field_out, va, vb, a, b, s = refs
    lanes = lane_iota(ZW)
    lanes_p = lane_iota(parts.shape[0])
    every = parts[...]
    numer = jnp.sum(jnp.where(lanes_p == 0, every, 0.0))
    denom = jnp.sum(jnp.where(lanes_p == 1, every, 0.0)) + 0.0625 * faces
    shift = jnp.full((ZW, LANES), numer, F32) / jnp.full((ZW, LANES), denom, F32)
    base = 4 * lax.axis_index("slow") + (PADM - 6)

    def of_q1(y):
        return q1[base + y, ZB : 4 * ZB]

    def of_k1(y):
        return k1[base + y, ZB : 4 * ZB]

    for y in range(YPOST):
        raised = e1[base + y, ZB : 4 * ZB] + (e2[y // 2] + shift)
        raised = jnp.where(of_k1(y) > 0.0, raised, 0.0)
        va[y] = raised
        vb[y] = raised

    @pl.when(sweeps[1] >= 4)
    def _():
        flat_sweep(vb, va, of_q1, of_k1, 1, 15, 14, lanes, 1)

    @pl.when(sweeps[1] >= 3)
    def _():
        flat_sweep(va, vb, of_q1, of_k1, 2, 14, 12, lanes, 1)

    flat_sweep(vb, va, of_q1, of_k1, 3, 13, 10, lanes, 1)
    flat_sweep(va, vb, of_q1, of_k1, 4, 12, 8, lanes, 1)

    def raise_fine(ym):
        value = vb[ym + 4]
        for half in range(2):
            y = 2 * ym + half
            for p in PARITIES:
                raised = jnp.where(k[(*p, y + 4)] > 0.0, epre[(*p, y)] + value, 0.0)
                a[(*p, y)] = raised
                b[(*p, y)] = raised

    over(0, YPOST // 2, 4, raise_fine)

    @pl.when(sweeps[0] >= 4)
    def _():
        fine_sweep(b, a, q, k, 1, 15, 7, lanes, offset=4)

    @pl.when(sweeps[0] >= 3)
    def _():
        fine_sweep(a, b, q, k, 2, 14, 6, lanes, offset=4)

    fine_sweep(b, a, q, k, 3, 13, 10, lanes, offset=4)
    fine_sweep(a, b, q, k, 4, 12, 8, lanes, offset=4)
    if not last:
        zero_edges(s)
    for pz, px in PARITIES:
        value = field[pz, px] + 0.5 * b[pz, px, 4:12, ZB : 2 * ZB]
        if last:
            halves[px, pl.ds(pz, YB * ZB, stride=2), :] = value.reshape(YB * ZB, LANES)
        else:
            field_out[pz, px] = value
            s[pz, px, 1 : YB + 1] = value
    if last:
        both = jnp.concatenate([halves[0], halves[1]], axis=1)
        out[...] = exact_dot(both, parity_matrix(True)).reshape(YB, 2 * ZB, 2 * LANES)
    else:
        write_pack(
            s, lambda p, y: later[(*p, y)], lambda p, y: pack[8 + 8 * y + tile_of(p)], out, 4, lane_iota(ZB)
        )


def call(kernel, outs, scratch, scalars, *arrays, space=pltpu.VMEM, megabytes=16, kept=True):
    specs = [pl.BlockSpec(memory_space=pltpu.SMEM)] * len(scalars)
    if space == pltpu.HBM:
        arrays = [pltpu.with_memory_space_constraint(x, pltpu.HBM) for x in arrays]
    return pl.pallas_call(
        kernel,
        out_shape=[pltpu.VMEM(s, F32) if kept else jax.ShapeDtypeStruct(s, F32) for s in outs],
        in_specs=specs + [pl.BlockSpec(memory_space=space)] * len(arrays),
        out_specs=[pl.BlockSpec(memory_space=pltpu.VMEM)] * len(outs),
        scratch_shapes=[pltpu.VMEM(s, F32) if isinstance(s, tuple) else s for s in scratch],
        compiler_params=pltpu.CompilerParams(vmem_limit_bytes=megabytes * 1024 * 1024),
    )(*scalars, *arrays)


def both_ways(to_right, to_left, axis):
    count = lax.axis_size(axis)
    up = [(i, (i + 1) % count) for i in range(count)]
    down = [(target, source) for source, target in up]
    return lax.ppermute(to_right, axis, up), lax.ppermute(to_left, axis, down)


def window_of(pack, each):
    left, right = both_ways(pack, pack, "fast")
    strip = jnp.stack([left, pack, right])
    upward = strip[:, 4 + each :]
    downward = jnp.concatenate([strip[:, : 4 + 7 * each], strip[:, 8 + 8 * each :]], axis=1)
    low, high = both_ways(upward, downward, "slow")
    return left, pack, right, low, high


def body(observed, start_field, diagonal, noise, sweeps):
    natural = observed.shape
    block = (2, 2, YB, ZB, LANES)
    edged = (2, 2, YB + 2, ZB, LANES)
    post = (2, 2, YPOST, ZW, LANES)
    whole = (2, 2, YW, ZW, LANES)
    middle = (YM + 2 * PADM, ZM, LANES)
    low_window = (16, 24, LANES)
    fast_count, slow_count = lax.axis_size("fast"), lax.axis_size("slow")
    first, second, third = YB * slow_count // 4, 2 * ZB * fast_count // 4, 2 * LANES // 4
    faces = 2.0 * (first * second + first * third + second * third)
    pack, field, later = call(
        split_kernel, [(pack_tiles(8), ZB, LANES), block, block],
        [
            natural, natural, natural, (2, *natural), (4, 2, YB * 2 * ZB, LANES),
            edged, block, block, pltpu.SemaphoreType.DMA((4,)),
        ],
        (), observed, start_field, diagonal, noise, space=pltpu.HBM,
    )
    own_pack = pack
    kept_fine = kept_low = None
    for step in range(2):
        opening = step == 0
        count = 2 if opening else 1
        given = window_of(pack, 8 if opening else 4)
        outs = [(count, 4, 16, LANES), (count, 4, 8, LANES), (count, 4, 16, LANES), post, whole]
        if opening:
            outs += [whole, (2, 2, YB, ZW, LANES)]
        else:
            given = (*given, *kept_fine)
        got = call(functools.partial(before_kernel, opening), outs, [whole] * 2, (sweeps,), *given)
        to_left, own, to_right, epre, q = got[:5]
        if opening:
            kept_fine = got[5:]
        left, right = both_ways(to_right, to_left, "fast")
        strip = jnp.concatenate([left, own, right], axis=2)
        strip = jnp.broadcast_to(strip[None], (slow_count, *strip.shape))
        strip = lax.all_to_all(strip, "slow", 0, 0, tiled=True)
        outs = [(fast_count, LANES), middle, middle, (YPOST // 2, ZW, LANES)]
        scratch = [
            middle, (16, ZM + 8, LANES), (16 + 2 * PADL, 24, LANES), (16 + 2 * PADL, 24, LANES),
            low_window, (YPOST // 2, 48, LANES),
        ]
        if opening:
            outs += [middle, (YM, ZM, LANES), low_window, low_window, (24, LANES)]
            given = (strip,)
        else:
            given = (strip, *kept_low)
        got = call(functools.partial(coarse_kernel, opening), outs, scratch, (sweeps,), *given)
        part, e1, q1, e2 = got[:4]
        if opening:
            kept_low = got[4:]
        parts = lax.all_to_all(part, "fast", 0, 0, tiled=True)
        given = (parts, e1, q1, kept_low[0], e2, epre, q, kept_fine[0], field)
        scratch = [(YPOST, ZW, LANES)] * 2 + [post] * 2
        kernel = functools.partial(after_kernel, not opening, faces)
        if opening:
            outs = [(pack_tiles(4), ZB, LANES), block]
            given = (*given, later, own_pack)
            pack, field = call(kernel, outs, scratch + [edged], (sweeps,), *given)
        else:
            halves = [(2, YB * 2 * ZB, LANES)]
            (out,) = call(kernel, [natural], scratch + halves, (sweeps,), *given, kept=False)
    return out


def solution(mesh):
    placed = (
        P("slow", "fast", None),
        P("slow", "fast", None),
        P("slow", "fast", None),
        P(None, "slow", "fast", None),
        P(),
    )
    return jax.shard_map(
        body, mesh=mesh, in_specs=placed, out_specs=P("slow", "fast", None), check_vma=False
    )
```

```python
import functools

import jax
import jax.numpy as jnp
from jax import lax
from jax.experimental import pallas as pl
from jax.experimental.pallas import tpu as pltpu
from jax.sharding import PartitionSpec as P

OMEGA = 0.7
KEEP = 1.0 - OMEGA
F32 = jnp.float32

YB, ZB, LANES = 8, 8, 128
YW, ZW = 3 * YB, 3 * ZB
ZM, YM = 40, 32
YPOST = 16
PADM, PADL = 8, 4
PARITIES = ((0, 0), (0, 1), (1, 0), (1, 1))


def lane_iota(rows):
    return lax.broadcasted_iota(jnp.int32, (rows, LANES), 1)


def row_iota(rows):
    return lax.broadcasted_iota(jnp.int32, (rows, LANES), 0)


def parity_matrix(transposed):
    row = lax.broadcasted_iota(jnp.int32, (2 * LANES, 2 * LANES), 0)
    col = lax.broadcasted_iota(jnp.int32, (2 * LANES, 2 * LANES), 1)
    if transposed:
        row, col = col, row
    return jnp.where(row == 2 * (col & (LANES - 1)) + (col >> 7), 1.0, 0.0).astype(F32)


def exact_dot(a, b):
    return lax.dot(a, b, precision=lax.Precision.HIGHEST, preferred_element_type=F32)


def over(low, high, chunk, one):
    turns, rest = divmod(high - low, chunk)
    assert rest == 0
    if turns == 1:
        for n in range(chunk):
            one(low + n)
        return

    def turn(at, carry):
        for n in range(chunk):
            one(low + at * chunk + n)
        return carry

    lax.fori_loop(0, turns, turn, 0)


def fine_neighbours(u, y, lanes):
    rows = u.shape[-2]
    here = {p: u[(*p, y)] for p in PARITIES}
    beside = {}
    for pz, px in PARITIES:
        total = u[pz, px, y - 1] + u[pz, px, y + 1]
        other = here[1 - pz, px]
        total = total + (other + pltpu.roll(other, 1 if pz == 0 else rows - 1, 0))
        other = here[pz, 1 - px]
        if px == 0:
            moved = jnp.where(lanes == 0, 0.0, pltpu.roll(other, 1, 1))
        else:
            moved = jnp.where(lanes == LANES - 1, 0.0, pltpu.roll(other, LANES - 1, 1))
        beside[pz, px] = total + (other + moved)
    return here, beside


def flat_neighbours(u, y, lanes, step):
    rows = u.shape[-2]
    here = u[y]
    total = u[y - 1] + u[y + 1]
    total = total + (pltpu.roll(here, 1, 0) + pltpu.roll(here, rows - 1, 0))
    left = jnp.where(lanes < step, 0.0, pltpu.roll(here, step, 1))
    right = jnp.where(lanes >= LANES - step, 0.0, pltpu.roll(here, LANES - step, 1))
    return here, total + (left + right)


def fine_sweep(source, target, q, k, low, high, chunk, lanes, shift=0, offset=0):
    def one(y):
        here, beside = fine_neighbours(source, y, lanes)
        for p in PARITIES:
            target[(*p, y - shift)] = (
                KEEP * here[p] + q[(*p, y + offset)] + k[(*p, y + offset)] * beside[p]
            )

    over(low, high, chunk, one)


def flat_sweep(source, target, q, k, low, high, chunk, lanes, step):
    def one(y):
        here, beside = flat_neighbours(source, y, lanes, step)
        target[y] = KEEP * here + q(y) + k(y) * beside

    over(low, high, chunk, one)


def closed_neighbours(u, y, lanes):
    rows = row_iota(ZB)
    here = {p: u[(*p, y)] for p in PARITIES}
    beside = {}
    for pz, px in PARITIES:
        total = u[pz, px, y - 1] + u[pz, px, y + 1]
        other = here[1 - pz, px]
        if pz == 0:
            moved = jnp.where(rows == 0, 0.0, pltpu.roll(other, 1, 0))
        else:
            moved = jnp.where(rows == ZB - 1, 0.0, pltpu.roll(other, ZB - 1, 0))
        total = total + (other + moved)
        other = here[pz, 1 - px]
        if px == 0:
            moved = jnp.where(lanes == 0, 0.0, pltpu.roll(other, 1, 1))
        else:
            moved = jnp.where(lanes == LANES - 1, 0.0, pltpu.roll(other, LANES - 1, 1))
        beside[pz, px] = total + (other + moved)
    return here, beside


def tile_of(p):
    return 2 * p[0] + p[1]


def pack_tiles(each):
    return 12 + 8 * each


def write_pack(s, linear, diag, out, each, lanes):
    for p in PARITIES:
        n = tile_of(p)
        out[n] = s[(*p, 1)]
        out[4 + 8 * each + n] = s[(*p, 8)]

    def one(y):
        here, beside = closed_neighbours(s, y + 1, lanes)
        for p in PARITIES:
            g = diag(p, y)
            out[4 + each * y + tile_of(p)] = linear(p, y) - (g + 6.0) * here[p] + beside[p]
            if each == 8:
                out[8 + each * y + tile_of(p)] = g

    for y in range(YB):
        one(y)
        for px in range(2):
            out[8 + 8 * each + px, y : y + 1] = s[0, px, y + 1, 0:1]
            out[10 + 8 * each + px, y : y + 1] = s[1, px, y + 1, ZB - 1 : ZB]


def zero_edges(s):
    for p in PARITIES:
        s[(*p, 0)] = jnp.zeros((ZB, LANES), F32)
        s[(*p, YB + 1)] = jnp.zeros((ZB, LANES), F32)


def split_kernel(observed, start, diagonal, noise, pack, field, later, a, b, c, d, halves, s, g, linear, sems):
    copies = [
        pltpu.make_async_copy(source, target, sems.at[n])
        for n, (source, target) in enumerate(((start, a), (diagonal, b), (observed, c), (noise, d)))
    ]
    for copy in copies:
        copy.start()
    matrix = parity_matrix(False)
    zero_edges(s)

    def split(n, value, *outs):
        both = exact_dot(value.reshape(YB * 2 * ZB, 2 * LANES), matrix)
        for px in range(2):
            halves[n, px] = both[:, px * LANES : (px + 1) * LANES]
        for pz, px in PARITIES:
            part = halves[n, px, pl.ds(pz, YB * ZB, stride=2), :].reshape(YB, ZB, LANES)
            for out in outs:
                out[pz, px] = part

    copies[0].wait()
    split(0, a[...], field, s.at[:, :, 1 : YB + 1])
    copies[1].wait()
    split(1, b[...], g)
    copies[2].wait()
    copies[3].wait()
    split(2, c[...] + 2.0 * d[0], linear)
    write_pack(s, lambda p, y: linear[(*p, y)], lambda p, y: g[(*p, y)], pack, 8, lane_iota(ZB))
    split(3, c[...] + 2.0 * d[1], later)


def inside(axis, which):
    at = lax.axis_index(axis) + (which - 1)
    return jnp.where((at >= 0) & (at < lax.axis_size(axis)), 1.0, 0.0).astype(F32)


def before_kernel(first, sweeps, *refs):
    across, low, high = refs[:3], refs[3], refs[4]
    if first:
        left_out, own_out, right_out, epre, q, k, dn = refs[5:12]
        a, b = refs[12:]
    else:
        k, dn = refs[5:7]
        left_out, own_out, right_out, epre, q = refs[7:12]
        a, b = refs[12:]
    each = 8 if first else 4
    lanes = lane_iota(ZW)
    rows = row_iota(ZW)
    tile_rows = row_iota(ZB)
    in_z = [inside("fast", n) for n in range(3)]
    in_y = [inside("slow", n) for n in range(3)]
    row_mask = jnp.where(rows < ZB, in_z[0], jnp.where(rows < 2 * ZB, 1.0, in_z[2]))
    masks = [row_mask * in_y[0], row_mask, row_mask * in_y[2]]

    def tile(yb, zb, n):
        if yb == 1:
            return across[zb].at[n]
        if yb == 0:
            return low.at[zb, n - (4 + each)]
        return high.at[zb, n]

    def z_face(yb, zb, which, px, y):
        n = 8 + 8 * each + 2 * which + px
        if yb == 2:
            n = 4 + 7 * each + 2 * which + px
        return tile(yb, zb, n)[pl.ds(y, 1), :]

    def wide(yb, n):
        return jnp.concatenate([tile(yb, zb, n)[...] for zb in range(3)], axis=0)

    def right_side(yb, y):
        row = yb * YB + y
        for p in PARITIES:
            pz, px = p
            tiles = [tile(yb, zb, 4 + each * y + tile_of(p))[...] for zb in range(3)]
            if pz == 1:
                edge = tile_rows == ZB - 1
                tiles[0] = tiles[0] + jnp.where(edge, z_face(yb, 1, 0, px, y), 0.0)
                tiles[1] = tiles[1] + jnp.where(edge, z_face(yb, 2, 0, px, y) * in_z[2], 0.0)
            else:
                edge = tile_rows == 0
                tiles[1] = tiles[1] + jnp.where(edge, z_face(yb, 0, 1, px, y) * in_z[0], 0.0)
                tiles[2] = tiles[2] + jnp.where(edge, z_face(yb, 1, 1, px, y), 0.0)
            rhs = jnp.concatenate(tiles, axis=0)
            if isinstance(y, int) and y == 0 and yb > 0:
                rhs = rhs + wide(yb - 1, 4 + 8 * each + tile_of(p)) * in_y[yb - 1]
            if isinstance(y, int) and y == YB - 1 and yb < 2:
                rhs = rhs + wide(yb + 1, tile_of(p)) * in_y[yb + 1]
            if first:
                full = wide(yb, 8 + each * y + tile_of(p)) + 6.0
                gain = (OMEGA / full) * masks[yb]
                k[(*p, row)] = gain
                if yb == 1:
                    dn[(*p, y)] = full * (1.0 / OMEGA)
            else:
                gain = k[(*p, row)]
            start = gain * rhs
            q[(*p, row)] = start
            a[(*p, row)] = start
            b[(*p, row)] = start

    for yb in range(3):
        over(1, YB - 1, 6, functools.partial(right_side, yb))
    right_side(0, YB - 1)
    right_side(1, 0)
    right_side(1, YB - 1)
    right_side(2, 0)

    @pl.when(sweeps[0] >= 4)
    def _():
        fine_sweep(a, b, q, k, 2, 22, 10, lanes)

    @pl.when(sweeps[0] >= 3)
    def _():
        fine_sweep(b, a, q, k, 3, 21, 9, lanes)

    fine_sweep(a, epre, q, k, 4, 20, 8, lanes, shift=4)
    zero = jnp.zeros((ZW, LANES), F32)

    def restrict(ym):
        total = zero
        diag = zero
        for half in range(2):
            row = YB + 2 * ym + half
            here, beside = fine_neighbours(epre, row - 4, lanes)
            for p in PARITIES:
                scaled = q[(*p, row)] - OMEGA * here[p] + k[(*p, row)] * beside[p]
                total = total + scaled * dn[(*p, 2 * ym + half)]
                if first:
                    diag = diag + wide(1, 8 + each * (2 * ym + half) + tile_of(p))
        for n, value in enumerate((total, diag) if first else (total,)):
            value = value * 0.125
            right_out[n, ym] = value[: 2 * ZB]
            own_out[n, ym] = value[ZB : 2 * ZB]
            left_out[n, ym] = value[ZB:]

    over(0, YB // 2, 4, restrict)


def coarse_kernel(first, sweeps, *refs):
    mine, other = refs[:2]
    if first:
        part, e1, q1, e2_out, k1, d1, k2, d2, g2sum = refs[2:11]
        va, t, wa, wb, q2, x2 = refs[11:]
    else:
        k1, d1, k2, d2, g2sum = refs[2:7]
        part, e1, q1, e2_out = refs[7:11]
        va, t, wa, wb, q2, x2 = refs[11:]
    fast = lax.axis_index("fast")
    slow = lax.axis_index("slow")

    def window(chip, core, n, ym):
        return jnp.where((slow & 1) == core, mine[chip, n, ym], other[chip, n, ym])

    lanes = lane_iota(ZM)
    even = (lanes & 1) == 0
    zrow = row_iota(ZM) + (fast * ZB - 2 * ZB)
    mask = jnp.where((zrow >= 0) & (zrow < lax.axis_size("fast") * ZB), 1.0, 0.0).astype(F32)
    zero = jnp.zeros((ZM, LANES), F32)
    for n in (*range(PADM), *range(PADM + YM, YM + 2 * PADM)):
        va[n] = zero
        e1[n] = zero
        q1[n] = zero
        if first:
            k1[n] = zero

    def opening(chip):
        for core in range(2):
            for ym in range(4):
                y = chip * 8 + core * 4 + ym
                rhs = window(chip, core, 0, ym)
                if first:
                    diag = window(chip, core, 1, ym)
                    d1[y] = diag
                    full = diag + 1.5
                    gain = (OMEGA / full) * mask
                    k1[PADM + y] = gain * 0.25
                    start = gain * rhs
                else:
                    start = (4.0 * k1[PADM + y]) * rhs
                q1[PADM + y] = start
                va[PADM + y] = start
                e1[PADM + y] = start

    over(0, YM // 8, 1, opening)
    of_q1, of_k1 = (lambda y: q1[y]), (lambda y: k1[y])

    @pl.when(sweeps[1] >= 4)
    def _():
        flat_sweep(va, e1, of_q1, of_k1, PADM, PADM + YM, 8, lanes, 1)

    @pl.when(sweeps[1] >= 3)
    def _():
        flat_sweep(e1, va, of_q1, of_k1, PADM, PADM + YM, 8, lanes, 1)

    flat_sweep(va, e1, of_q1, of_k1, PADM, PADM + YM, 8, lanes, 1)

    def pair_sum(value):
        return value + jnp.where(even, pltpu.roll(value, LANES - 1, 1), pltpu.roll(value, 1, 1))

    def restrict(yc):
        total = zero
        for half in range(2):
            y = PADM + 2 * yc + half
            here, beside = flat_neighbours(e1, y, lanes, 1)
            total = total + (q1[y] - OMEGA * here + k1[y] * beside) * (d1[2 * yc + half] + 1.5)
        t[yc, :ZM] = pair_sum(total * (1.0 / OMEGA))
        t[yc, ZM:] = jnp.zeros((8, LANES), F32)

    over(0, YM // 2, 4, restrict)
    lanes2 = lane_iota(24)
    rows2 = row_iota(24)
    zrow2 = rows2 + (fast * 4 - 8)
    mask2 = jnp.where(
        (zrow2 >= 0) & (zrow2 < lax.axis_size("fast") * 4) & (rows2 < 20), 1.0, 0.0
    ).astype(F32)
    own = jnp.where((rows2 >= 8) & (rows2 < 12), 0.5, 0.0).astype(F32)
    zero2 = jnp.zeros((24, LANES), F32)
    for n in (*range(PADL), *range(PADL + 16, 16 + 2 * PADL)):
        wa[n] = zero2
        wb[n] = zero2

    def halve(yc):
        return (t[yc, pl.ds(0, 24, stride=2), :] + t[yc, pl.ds(1, 24, stride=2), :]) * 0.125

    if first:
        for yc in range(16):
            q2[yc] = halve(yc)

        def coarse_diag(yc):
            t[yc, :ZM] = pair_sum(d1[2 * yc] + d1[2 * yc + 1])

        over(0, 16, 4, coarse_diag)
        total = zero2
        for yc in range(16):
            g2 = halve(yc)
            full = g2 + 0.375
            gain = (OMEGA / full) * mask2
            k2[yc] = gain * 0.0625
            d2[yc] = full * (1.0 / OMEGA)
            total = total + g2 * own
            start = gain * q2[yc]
            q2[yc] = start
            wa[PADL + yc] = start
            wb[PADL + yc] = start
        g2sum[...] = total
    else:
        for yc in range(16):
            start = (16.0 * k2[yc]) * halve(yc)
            q2[yc] = start
            wa[PADL + yc] = start
            wb[PADL + yc] = start
    of_q2, of_k2 = (lambda y: q2[y - PADL]), (lambda y: k2[y - PADL])

    @pl.when(sweeps[2] >= 4)
    def _():
        flat_sweep(wa, wb, of_q2, of_k2, PADL, PADL + 16, 16, lanes2, 2)

    @pl.when(sweeps[2] >= 3)
    def _():
        flat_sweep(wb, wa, of_q2, of_k2, PADL, PADL + 16, 16, lanes2, 2)

    flat_sweep(wa, wb, of_q2, of_k2, PADL, PADL + 16, 16, lanes2, 2)
    total = zero2
    for yc in range(16):
        here, beside = flat_neighbours(wb, yc + PADL, lanes2, 2)
        total = total + (q2[yc] - OMEGA * here + k2[yc] * beside) * d2[yc]
    numer = jnp.sum(total * own)
    denom = jnp.sum(g2sum[...])
    lanes_p = lane_iota(part.shape[0])
    part[...] = jnp.where(lanes_p == 0, numer, jnp.where(lanes_p == 1, denom, 0.0))
    for y in range(YPOST // 2):
        value = wb[2 * slow + (PADL - 3) + y]
        x2[y, pl.ds(0, 24, stride=2), :] = value
        x2[y, pl.ds(1, 24, stride=2), :] = value
        e2_out[y] = x2[y, ZB : 4 * ZB]


def after_kernel(last, faces, sweeps, *refs):
    if last:
        parts, e1, q1, k1, e2, epre, q, k, field, out, va, vb, a, b, halves = refs
    else:
        parts, e1, q1, k1, e2, epre, q, k, field, later, pack, out, field_out, va, vb, a, b, s = refs
    lanes = lane_iota(ZW)
    lanes_p = lane_iota(parts.shape[0])
    every = parts[...]
    numer = jnp.sum(jnp.where(lanes_p == 0, every, 0.0))
    denom = jnp.sum(jnp.where(lanes_p == 1, every, 0.0)) + 0.0625 * faces
    shift = jnp.full((ZW, LANES), numer, F32) / jnp.full((ZW, LANES), denom, F32)
    base = 4 * lax.axis_index("slow") + (PADM - 6)

    def of_q1(y):
        return q1[base + y, ZB : 4 * ZB]

    def of_k1(y):
        return k1[base + y, ZB : 4 * ZB]

    for y in range(YPOST):
        raised = e1[base + y, ZB : 4 * ZB] + (e2[y // 2] + shift)
        raised = jnp.where(of_k1(y) > 0.0, raised, 0.0)
        va[y] = raised
        vb[y] = raised

    @pl.when(sweeps[1] >= 4)
    def _():
        flat_sweep(vb, va, of_q1, of_k1, 1, 15, 14, lanes, 1)

    @pl.when(sweeps[1] >= 3)
    def _():
        flat_sweep(va, vb, of_q1, of_k1, 2, 14, 12, lanes, 1)

    flat_sweep(vb, va, of_q1, of_k1, 3, 13, 10, lanes, 1)
    flat_sweep(va, vb, of_q1, of_k1, 4, 12, 8, lanes, 1)

    def raise_fine(ym):
        value = vb[ym + 4]
        for half in range(2):
            y = 2 * ym + half
            for p in PARITIES:
                raised = jnp.where(k[(*p, y + 4)] > 0.0, epre[(*p, y)] + value, 0.0)
                a[(*p, y)] = raised
                b[(*p, y)] = raised

    over(0, YPOST // 2, 4, raise_fine)

    @pl.when(sweeps[0] >= 4)
    def _():
        fine_sweep(b, a, q, k, 1, 15, 7, lanes, offset=4)

    @pl.when(sweeps[0] >= 3)
    def _():
        fine_sweep(a, b, q, k, 2, 14, 6, lanes, offset=4)

    fine_sweep(b, a, q, k, 3, 13, 10, lanes, offset=4)
    fine_sweep(a, b, q, k, 4, 12, 8, lanes, offset=4)
    if not last:
        zero_edges(s)
    for pz, px in PARITIES:
        value = field[pz, px] + 0.5 * b[pz, px, 4:12, ZB : 2 * ZB]
        if last:
            halves[px, pl.ds(pz, YB * ZB, stride=2), :] = value.reshape(YB * ZB, LANES)
        else:
            field_out[pz, px] = value
            s[pz, px, 1 : YB + 1] = value
    if last:
        both = jnp.concatenate([halves[0], halves[1]], axis=1)
        out[...] = exact_dot(both, parity_matrix(True)).reshape(YB, 2 * ZB, 2 * LANES)
    else:
        write_pack(
            s, lambda p, y: later[(*p, y)], lambda p, y: pack[8 + 8 * y + tile_of(p)], out, 4, lane_iota(ZB)
        )


def call(kernel, outs, scratch, scalars, *arrays, space=pltpu.VMEM, megabytes=16, kept=True):
    specs = [pl.BlockSpec(memory_space=pltpu.SMEM)] * len(scalars)
    if space == pltpu.HBM:
        arrays = [pltpu.with_memory_space_constraint(x, pltpu.HBM) for x in arrays]
    return pl.pallas_call(
        kernel,
        out_shape=[pltpu.VMEM(s, F32) if kept else jax.ShapeDtypeStruct(s, F32) for s in outs],
        in_specs=specs + [pl.BlockSpec(memory_space=space)] * len(arrays),
        out_specs=[pl.BlockSpec(memory_space=pltpu.VMEM)] * len(outs),
        scratch_shapes=[pltpu.VMEM(s, F32) if isinstance(s, tuple) else s for s in scratch],
        compiler_params=pltpu.CompilerParams(vmem_limit_bytes=megabytes * 1024 * 1024),
    )(*scalars, *arrays)


def both_ways(to_right, to_left, axis):
    count = lax.axis_size(axis)
    up = [(i, (i + 1) % count) for i in range(count)]
    down = [(target, source) for source, target in up]
    return lax.ppermute(to_right, axis, up), lax.ppermute(to_left, axis, down)


def window_of(pack, each):
    left, right = both_ways(pack, pack, "fast")
    strip = jnp.stack([left, pack, right])
    upward = strip[:, 4 + each :]
    downward = jnp.concatenate([strip[:, : 4 + 7 * each], strip[:, 8 + 8 * each :]], axis=1)
    low, high = both_ways(upward, downward, "slow")
    return left, pack, right, low, high


def body(observed, start_field, diagonal, noise, sweeps):
    natural = observed.shape
    block = (2, 2, YB, ZB, LANES)
    edged = (2, 2, YB + 2, ZB, LANES)
    post = (2, 2, YPOST, ZW, LANES)
    whole = (2, 2, YW, ZW, LANES)
    middle = (YM + 2 * PADM, ZM, LANES)
    low_window = (16, 24, LANES)
    fast_count, slow_count = lax.axis_size("fast"), lax.axis_size("slow")
    first, second, third = YB * slow_count // 4, 2 * ZB * fast_count // 4, 2 * LANES // 4
    faces = 2.0 * (first * second + first * third + second * third)
    pack, field, later = call(
        split_kernel, [(pack_tiles(8), ZB, LANES), block, block],
        [
            natural, natural, natural, (2, *natural), (4, 2, YB * 2 * ZB, LANES),
            edged, block, block, pltpu.SemaphoreType.DMA((4,)),
        ],
        (), observed, start_field, diagonal, noise, space=pltpu.HBM,
    )
    own_pack = pack
    kept_fine = kept_low = None
    for step in range(2):
        opening = step == 0
        count = 2 if opening else 1
        given = window_of(pack, 8 if opening else 4)
        outs = [(count, 4, 16, LANES), (count, 4, 8, LANES), (count, 4, 16, LANES), post, whole]
        if opening:
            outs += [whole, (2, 2, YB, ZW, LANES)]
        else:
            given = (*given, *kept_fine)
        got = call(functools.partial(before_kernel, opening), outs, [whole] * 2, (sweeps,), *given)
        to_left, own, to_right, epre, q = got[:5]
        if opening:
            kept_fine = got[5:]
        left, right = both_ways(to_right, to_left, "fast")
        strip = jnp.concatenate([left, own, right], axis=2)
        strip = jnp.broadcast_to(strip[None], (slow_count // 2, *strip.shape))
        chips = [[2 * n + core for n in range(slow_count // 2)] for core in range(2)]
        mine = lax.all_to_all(strip, "slow", 0, 0, axis_index_groups=chips, tiled=True)
        other = lax.ppermute(mine, "slow", [(n, n ^ 1) for n in range(slow_count)])
        outs = [(fast_count, LANES), middle, middle, (YPOST // 2, ZW, LANES)]
        scratch = [
            middle, (16, ZM + 8, LANES), (16 + 2 * PADL, 24, LANES), (16 + 2 * PADL, 24, LANES),
            low_window, (YPOST // 2, 48, LANES),
        ]
        if opening:
            outs += [middle, (YM, ZM, LANES), low_window, low_window, (24, LANES)]
            given = (mine, other)
        else:
            given = (mine, other, *kept_low)
        got = call(functools.partial(coarse_kernel, opening), outs, scratch, (sweeps,), *given)
        part, e1, q1, e2 = got[:4]
        if opening:
            kept_low = got[4:]
        parts = lax.all_to_all(part, "fast", 0, 0, tiled=True)
        given = (parts, e1, q1, kept_low[0], e2, epre, q, kept_fine[0], field)
        scratch = [(YPOST, ZW, LANES)] * 2 + [post] * 2
        kernel = functools.partial(after_kernel, not opening, faces)
        if opening:
            outs = [(pack_tiles(4), ZB, LANES), block]
            given = (*given, later, own_pack)
            pack, field = call(kernel, outs, scratch + [edged], (sweeps,), *given)
        else:
            halves = [(2, YB * 2 * ZB, LANES)]
            (out,) = call(kernel, [natural], scratch + halves, (sweeps,), *given, kept=False)
    return out


def solution(mesh):
    placed = (
        P("slow", "fast", None),
        P("slow", "fast", None),
        P("slow", "fast", None),
        P(None, "slow", "fast", None),
        P(),
    )
    return jax.shard_map(
        body, mesh=mesh, in_specs=placed, out_specs=P("slow", "fast", None), check_vma=False
    )
```

```python
import functools

import jax
import jax.numpy as jnp
from jax import lax
from jax.experimental import pallas as pl
from jax.experimental.pallas import tpu as pltpu
from jax.sharding import PartitionSpec as P

OMEGA = 0.7
KEEP = 1.0 - OMEGA
F32 = jnp.float32

YB, ZB, LANES = 8, 8, 128
YW, ZW = 3 * YB, 3 * ZB
ZM, YM = 40, 32
YPOST = 16
PADM, PADL = 8, 4
FINE, FLAT = 24, 32
PARITIES = ((0, 0), (0, 1), (1, 0), (1, 1))


def lane_iota(rows):
    return lax.broadcasted_iota(jnp.int32, (rows, LANES), 1)


def row_iota(rows):
    return lax.broadcasted_iota(jnp.int32, (rows, LANES), 0)


def parity_matrix(transposed):
    row = lax.broadcasted_iota(jnp.int32, (2 * LANES, 2 * LANES), 0)
    col = lax.broadcasted_iota(jnp.int32, (2 * LANES, 2 * LANES), 1)
    if transposed:
        row, col = col, row
    return jnp.where(row == 2 * (col & (LANES - 1)) + (col >> 7), 1.0, 0.0).astype(F32)


def exact_dot(a, b):
    return lax.dot(a, b, precision=lax.Precision.HIGHEST, preferred_element_type=F32)


def over(low, high, chunk, one):
    chunk = min(chunk, high - low)
    turns, rest = divmod(high - low, chunk)
    for n in range(rest):
        one(high - rest + n)
    if turns == 1:
        for n in range(chunk):
            one(low + n)
        return

    def turn(at, carry):
        for n in range(chunk):
            one(low + at * chunk + n)
        return carry

    lax.fori_loop(0, turns, turn, 0)


def fine_neighbours(u, y, lanes):
    rows = u.shape[-2]
    here = {p: u[(*p, y)] for p in PARITIES}
    beside = {}
    for pz, px in PARITIES:
        total = u[pz, px, y - 1] + u[pz, px, y + 1]
        other = here[1 - pz, px]
        total = total + (other + pltpu.roll(other, 1 if pz == 0 else rows - 1, 0))
        other = here[pz, 1 - px]
        if px == 0:
            moved = jnp.where(lanes == 0, 0.0, pltpu.roll(other, 1, 1))
        else:
            moved = jnp.where(lanes == LANES - 1, 0.0, pltpu.roll(other, LANES - 1, 1))
        beside[pz, px] = total + (other + moved)
    return here, beside


def flat_neighbours(u, y, lanes, step):
    rows = u.shape[-2]
    here = u[y]
    total = u[y - 1] + u[y + 1]
    total = total + (pltpu.roll(here, 1, 0) + pltpu.roll(here, rows - 1, 0))
    left = jnp.where(lanes < step, 0.0, pltpu.roll(here, step, 1))
    right = jnp.where(lanes >= LANES - step, 0.0, pltpu.roll(here, LANES - step, 1))
    return here, total + (left + right)


def fine_sweep(source, target, q, k, low, high, chunk, lanes, shift=0, offset=0):
    def one(y):
        here, beside = fine_neighbours(source, y, lanes)
        for p in PARITIES:
            target[(*p, y - shift)] = (
                KEEP * here[p] + q[(*p, y + offset)] + k[(*p, y + offset)] * beside[p]
            )

    over(low, high, chunk, one)


def flat_sweep(source, target, q, k, low, high, chunk, lanes, step):
    def one(y):
        here, beside = flat_neighbours(source, y, lanes, step)
        target[y] = KEEP * here + q(y) + k(y) * beside

    over(low, high, chunk, one)


def closed_neighbours(u, y, lanes):
    rows = row_iota(ZB)
    here = {p: u[(*p, y)] for p in PARITIES}
    beside = {}
    for pz, px in PARITIES:
        total = u[pz, px, y - 1] + u[pz, px, y + 1]
        other = here[1 - pz, px]
        if pz == 0:
            moved = jnp.where(rows == 0, 0.0, pltpu.roll(other, 1, 0))
        else:
            moved = jnp.where(rows == ZB - 1, 0.0, pltpu.roll(other, ZB - 1, 0))
        total = total + (other + moved)
        other = here[pz, 1 - px]
        if px == 0:
            moved = jnp.where(lanes == 0, 0.0, pltpu.roll(other, 1, 1))
        else:
            moved = jnp.where(lanes == LANES - 1, 0.0, pltpu.roll(other, LANES - 1, 1))
        beside[pz, px] = total + (other + moved)
    return here, beside


def tile_of(p):
    return 2 * p[0] + p[1]


def pack_tiles(each):
    return 12 + 8 * each


def write_pack(s, linear, diag, out, each, lanes):
    for p in PARITIES:
        n = tile_of(p)
        out[n] = s[(*p, 1)]
        out[4 + 8 * each + n] = s[(*p, 8)]

    def one(y):
        here, beside = closed_neighbours(s, y + 1, lanes)
        for p in PARITIES:
            g = diag(p, y)
            out[4 + each * y + tile_of(p)] = linear(p, y) - (g + 6.0) * here[p] + beside[p]
            if each == 8:
                out[8 + each * y + tile_of(p)] = g

    for y in range(YB):
        one(y)
        for px in range(2):
            out[8 + 8 * each + px, y : y + 1] = s[0, px, y + 1, 0:1]
            out[10 + 8 * each + px, y : y + 1] = s[1, px, y + 1, ZB - 1 : ZB]


def zero_edges(s):
    for p in PARITIES:
        s[(*p, 0)] = jnp.zeros((ZB, LANES), F32)
        s[(*p, YB + 1)] = jnp.zeros((ZB, LANES), F32)


def split_by_parity(value, matrix, halves, *outs):
    both = exact_dot(value.reshape(YB * 2 * ZB, 2 * LANES), matrix)
    for px in range(2):
        halves[px] = both[:, px * LANES : (px + 1) * LANES]
    for pz, px in PARITIES:
        part = halves[px, pl.ds(pz, YB * ZB, stride=2), :].reshape(YB, ZB, LANES)
        for out in outs:
            out[pz, px] = part


def copies_of(pairs, sems):
    copies = [pltpu.make_async_copy(*pair, sems.at[n]) for n, pair in enumerate(pairs)]
    for copy in copies:
        copy.start()
    return copies


def pack_kernel(observed, start, diagonal, noise, pack, field, a, b, c, d, halves, s, g, linear, sems):
    copies = copies_of(((start, a), (diagonal, b), (observed, c), (noise.at[0], d)), sems)
    matrix = parity_matrix(False)
    zero_edges(s)
    copies[0].wait()
    split_by_parity(a[...], matrix, halves.at[0], field, s.at[:, :, 1 : YB + 1])
    copies[1].wait()
    split_by_parity(b[...], matrix, halves.at[1], g)
    copies[2].wait()
    copies[3].wait()
    split_by_parity(c[...] + 2.0 * d[...], matrix, halves.at[2], linear)
    write_pack(s, lambda p, y: linear[(*p, y)], lambda p, y: g[(*p, y)], pack, 8, lane_iota(ZB))


def later_kernel(observed, noise, later, c, d, halves, sems):
    for copy in copies_of(((observed, c), (noise.at[1], d)), sems):
        copy.wait()
    split_by_parity(c[...] + 2.0 * d[...], parity_matrix(False), halves, later)


def inside(axis, which):
    at = lax.axis_index(axis) + (which - 1)
    return jnp.where((at >= 0) & (at < lax.axis_size(axis)), 1.0, 0.0).astype(F32)


def before_kernel(first, sweeps, *refs):
    across, low, high = refs[:3], refs[3], refs[4]
    if first:
        left_out, own_out, right_out, epre, q, k, dn = refs[5:12]
        a, b = refs[12:]
    else:
        k, dn = refs[5:7]
        left_out, own_out, right_out, epre, q = refs[7:12]
        a, b = refs[12:]
    each = 8 if first else 4
    lanes = lane_iota(ZW)
    rows = row_iota(ZW)
    tile_rows = row_iota(ZB)
    in_z = [inside("fast", n) for n in range(3)]
    in_y = [inside("slow", n) for n in range(3)]
    row_mask = jnp.where(rows < ZB, in_z[0], jnp.where(rows < 2 * ZB, 1.0, in_z[2]))
    masks = [row_mask * in_y[0], row_mask, row_mask * in_y[2]]

    def tile(yb, zb, n):
        if yb == 1:
            return across[zb].at[n]
        rows, y = (7, (n - 4) // each) if zb == 1 else (6, (n - 4) // each)
        base = (0, 6 * each + 6, 13 * each + 14)[zb]
        if n < 4:
            at = n
        elif y < YB:
            left_out_rows = YB - rows if yb == 0 else 0
            if y < left_out_rows or y >= left_out_rows + rows:
                return None
            at = n - (4 + left_out_rows * each) + (0 if yb == 0 else 4)
        else:
            at = n - (4 + 8 * each) + rows * each
        return (low if yb == 0 else high).at[base + at]

    def z_face(yb, zb, which, px, y):
        n = 2 * which + px
        if yb == 1:
            face = across[zb].at[8 + 8 * each + n]
        else:
            base = (6 * each + 4 - 2, 13 * each + 10, 19 * each + 18)[zb]
            face = (low if yb == 0 else high).at[base + n]
        return face[pl.ds(y, 1), :]

    def wide(yb, n):
        return jnp.concatenate([load(yb, zb, n) for zb in range(3)], axis=0)

    def load(yb, zb, n):
        at = tile(yb, zb, n)
        return jnp.zeros((ZB, LANES), F32) if at is None else at[...]

    def right_side(yb, y):
        row = yb * YB + y
        for p in PARITIES:
            pz, px = p
            tiles = [load(yb, zb, 4 + each * y + tile_of(p)) for zb in range(3)]
            if pz == 1:
                edge = tile_rows == ZB - 1
                tiles[0] = tiles[0] + jnp.where(edge, z_face(yb, 1, 0, px, y), 0.0)
                tiles[1] = tiles[1] + jnp.where(edge, z_face(yb, 2, 0, px, y) * in_z[2], 0.0)
            else:
                edge = tile_rows == 0
                tiles[1] = tiles[1] + jnp.where(edge, z_face(yb, 0, 1, px, y) * in_z[0], 0.0)
                tiles[2] = tiles[2] + jnp.where(edge, z_face(yb, 1, 1, px, y), 0.0)
            rhs = jnp.concatenate(tiles, axis=0)
            if isinstance(y, int) and y == 0 and yb > 0:
                rhs = rhs + wide(yb - 1, 4 + 8 * each + tile_of(p)) * in_y[yb - 1]
            if isinstance(y, int) and y == YB - 1 and yb < 2:
                rhs = rhs + wide(yb + 1, tile_of(p)) * in_y[yb + 1]
            if first:
                full = wide(yb, 8 + each * y + tile_of(p)) + 6.0
                gain = (OMEGA / full) * masks[yb]
                k[(*p, row)] = gain
                if yb == 1:
                    dn[(*p, y)] = full * (1.0 / OMEGA)
            else:
                gain = k[(*p, row)]
            start = gain * rhs
            q[(*p, row)] = start
            a[(*p, row)] = start
            b[(*p, row)] = start

    for yb in range(3):
        over(1, YB - 1, YB, functools.partial(right_side, yb))
    right_side(0, YB - 1)
    right_side(1, 0)
    right_side(1, YB - 1)
    right_side(2, 0)

    @pl.when(sweeps[0] >= 4)
    def _():
        fine_sweep(a, b, q, k, 2, 22, FINE, lanes)

    @pl.when(sweeps[0] >= 3)
    def _():
        fine_sweep(b, a, q, k, 3, 21, FINE, lanes)

    fine_sweep(a, epre, q, k, 4, 20, FINE, lanes, shift=4)
    zero = jnp.zeros((ZW, LANES), F32)

    def restrict(ym):
        total = zero
        diag = zero
        for half in range(2):
            row = YB + 2 * ym + half
            here, beside = fine_neighbours(epre, row - 4, lanes)
            for p in PARITIES:
                scaled = q[(*p, row)] - OMEGA * here[p] + k[(*p, row)] * beside[p]
                total = total + scaled * dn[(*p, 2 * ym + half)]
                if first:
                    diag = diag + wide(1, 8 + each * (2 * ym + half) + tile_of(p))
        for n, value in enumerate((total, diag) if first else (total,)):
            value = value * 0.125
            right_out[n, ym] = value[: 2 * ZB]
            own_out[n, ym] = value[ZB : 2 * ZB]
            left_out[n, ym] = value[ZB:]

    over(0, YB // 2, 4, restrict)


def coarse_kernel(first, sweeps, *refs):
    mine, other = refs[:2]
    if first:
        part, e1, q1, e2_out, k1, d1, k2, d2, g2sum = refs[2:11]
        va, t, wa, wb, q2, x2 = refs[11:]
    else:
        k1, d1, k2, d2, g2sum = refs[2:7]
        part, e1, q1, e2_out = refs[7:11]
        va, t, wa, wb, q2, x2 = refs[11:]
    fast = lax.axis_index("fast")
    slow = lax.axis_index("slow")

    lanes = lane_iota(ZM)
    even = (lanes & 1) == 0
    zrow = row_iota(ZM) + (fast * ZB - 2 * ZB)
    mask = jnp.where((zrow >= 0) & (zrow < lax.axis_size("fast") * ZB), 1.0, 0.0).astype(F32)
    zero = jnp.zeros((ZM, LANES), F32)
    for n in (*range(PADM), *range(PADM + YM, YM + 2 * PADM)):
        va[n] = zero
        e1[n] = zero
        q1[n] = zero
        if first:
            k1[n] = zero

    here_first = slow & 1

    def opening(chip):
        for gathered, core in ((mine, here_first), (other, 1 - here_first)):
            for ym in range(4):
                y = chip * 8 + core * 4 + ym
                rhs = gathered[chip, 0, ym]
                if first:
                    diag = gathered[chip, 1, ym]
                    d1[y] = diag
                    full = diag + 1.5
                    gain = (OMEGA / full) * mask
                    k1[PADM + y] = gain * 0.25
                    start = gain * rhs
                else:
                    start = (4.0 * k1[PADM + y]) * rhs
                q1[PADM + y] = start
                va[PADM + y] = start
                e1[PADM + y] = start

    over(0, YM // 8, 4, opening)
    of_q1, of_k1 = (lambda y: q1[y]), (lambda y: k1[y])

    @pl.when(sweeps[1] >= 4)
    def _():
        flat_sweep(va, e1, of_q1, of_k1, PADM, PADM + YM, FLAT, lanes, 1)

    @pl.when(sweeps[1] >= 3)
    def _():
        flat_sweep(e1, va, of_q1, of_k1, PADM, PADM + YM, FLAT, lanes, 1)

    flat_sweep(va, e1, of_q1, of_k1, PADM, PADM + YM, FLAT, lanes, 1)

    def pair_sum(value):
        return value + jnp.where(even, pltpu.roll(value, LANES - 1, 1), pltpu.roll(value, 1, 1))

    def restrict(yc):
        total = zero
        for half in range(2):
            y = PADM + 2 * yc + half
            here, beside = flat_neighbours(e1, y, lanes, 1)
            total = total + (q1[y] - OMEGA * here + k1[y] * beside) * (d1[2 * yc + half] + 1.5)
        t[yc, :ZM] = pair_sum(total * (1.0 / OMEGA))
        t[yc, ZM:] = jnp.zeros((8, LANES), F32)

    over(0, YM // 2, 16, restrict)
    lanes2 = lane_iota(24)
    rows2 = row_iota(24)
    zrow2 = rows2 + (fast * 4 - 8)
    mask2 = jnp.where(
        (zrow2 >= 0) & (zrow2 < lax.axis_size("fast") * 4) & (rows2 < 20), 1.0, 0.0
    ).astype(F32)
    own = jnp.where((rows2 >= 8) & (rows2 < 12), 0.5, 0.0).astype(F32)
    zero2 = jnp.zeros((24, LANES), F32)
    for n in (*range(PADL), *range(PADL + 16, 16 + 2 * PADL)):
        wa[n] = zero2
        wb[n] = zero2

    def halve(yc):
        return (t[yc, pl.ds(0, 24, stride=2), :] + t[yc, pl.ds(1, 24, stride=2), :]) * 0.125

    if first:
        for yc in range(16):
            q2[yc] = halve(yc)

        def coarse_diag(yc):
            t[yc, :ZM] = pair_sum(d1[2 * yc] + d1[2 * yc + 1])

        over(0, 16, 4, coarse_diag)
        total = zero2
        for yc in range(16):
            g2 = halve(yc)
            full = g2 + 0.375
            gain = (OMEGA / full) * mask2
            k2[yc] = gain * 0.0625
            d2[yc] = full * (1.0 / OMEGA)
            total = total + g2 * own
            start = gain * q2[yc]
            q2[yc] = start
            wa[PADL + yc] = start
            wb[PADL + yc] = start
        g2sum[...] = total
    else:
        for yc in range(16):
            start = (16.0 * k2[yc]) * halve(yc)
            q2[yc] = start
            wa[PADL + yc] = start
            wb[PADL + yc] = start
    of_q2, of_k2 = (lambda y: q2[y - PADL]), (lambda y: k2[y - PADL])

    @pl.when(sweeps[2] >= 4)
    def _():
        flat_sweep(wa, wb, of_q2, of_k2, PADL, PADL + 16, FLAT, lanes2, 2)

    @pl.when(sweeps[2] >= 3)
    def _():
        flat_sweep(wb, wa, of_q2, of_k2, PADL, PADL + 16, FLAT, lanes2, 2)

    flat_sweep(wa, wb, of_q2, of_k2, PADL, PADL + 16, FLAT, lanes2, 2)
    total = zero2
    for yc in range(16):
        here, beside = flat_neighbours(wb, yc + PADL, lanes2, 2)
        total = total + (q2[yc] - OMEGA * here + k2[yc] * beside) * d2[yc]
    numer = jnp.sum(total * own)
    denom = jnp.sum(g2sum[...])
    lanes_p = lane_iota(part.shape[0])
    part[...] = jnp.where(lanes_p == 0, numer, jnp.where(lanes_p == 1, denom, 0.0))
    for y in range(YPOST // 2):
        value = wb[2 * slow + (PADL - 3) + y]
        x2[y, pl.ds(0, 24, stride=2), :] = value
        x2[y, pl.ds(1, 24, stride=2), :] = value
        e2_out[y] = x2[y, ZB : 4 * ZB]


def after_kernel(last, faces, sweeps, *refs):
    if last:
        parts, e1, q1, k1, e2, epre, q, k, field, out, va, vb, a, b, halves = refs
    else:
        parts, e1, q1, k1, e2, epre, q, k, field, later, pack, out, field_out, va, vb, a, b, s = refs
    lanes = lane_iota(ZW)
    lanes_p = lane_iota(parts.shape[0])
    every = parts[...]
    numer = jnp.sum(jnp.where(lanes_p == 0, every, 0.0))
    denom = jnp.sum(jnp.where(lanes_p == 1, every, 0.0)) + 0.0625 * faces
    shift = jnp.full((ZW, LANES), numer, F32) / jnp.full((ZW, LANES), denom, F32)
    base = 4 * lax.axis_index("slow") + (PADM - 6)

    def of_q1(y):
        return q1[base + y, ZB : 4 * ZB]

    def of_k1(y):
        return k1[base + y, ZB : 4 * ZB]

    for y in range(YPOST):
        raised = e1[base + y, ZB : 4 * ZB] + (e2[y // 2] + shift)
        raised = jnp.where(of_k1(y) > 0.0, raised, 0.0)
        va[y] = raised
        vb[y] = raised

    @pl.when(sweeps[1] >= 4)
    def _():
        flat_sweep(vb, va, of_q1, of_k1, 1, 15, FLAT, lanes, 1)

    @pl.when(sweeps[1] >= 3)
    def _():
        flat_sweep(va, vb, of_q1, of_k1, 2, 14, FLAT, lanes, 1)

    flat_sweep(vb, va, of_q1, of_k1, 3, 13, FLAT, lanes, 1)
    flat_sweep(va, vb, of_q1, of_k1, 4, 12, FLAT, lanes, 1)

    def raise_fine(ym):
        value = vb[ym + 4]
        for half in range(2):
            y = 2 * ym + half
            for p in PARITIES:
                raised = jnp.where(k[(*p, y + 4)] > 0.0, epre[(*p, y)] + value, 0.0)
                a[(*p, y)] = raised
                b[(*p, y)] = raised

    over(0, YPOST // 2, 8, raise_fine)

    @pl.when(sweeps[0] >= 4)
    def _():
        fine_sweep(b, a, q, k, 1, 15, FINE, lanes, offset=4)

    @pl.when(sweeps[0] >= 3)
    def _():
        fine_sweep(a, b, q, k, 2, 14, FINE, lanes, offset=4)

    fine_sweep(b, a, q, k, 3, 13, FINE, lanes, offset=4)
    fine_sweep(a, b, q, k, 4, 12, FINE, lanes, offset=4)
    if not last:
        zero_edges(s)
    for pz, px in PARITIES:
        value = field[pz, px] + 0.5 * b[pz, px, 4:12, ZB : 2 * ZB]
        if last:
            halves[px, pl.ds(pz, YB * ZB, stride=2), :] = value.reshape(YB * ZB, LANES)
        else:
            field_out[pz, px] = value
            s[pz, px, 1 : YB + 1] = value
    if last:
        both = jnp.concatenate([halves[0], halves[1]], axis=1)
        out[...] = exact_dot(both, parity_matrix(True)).reshape(YB, 2 * ZB, 2 * LANES)
    else:
        write_pack(
            s, lambda p, y: later[(*p, y)], lambda p, y: pack[8 + 8 * y + tile_of(p)], out, 4, lane_iota(ZB)
        )


def call(kernel, outs, scratch, scalars, *arrays, space=pltpu.VMEM, megabytes=16, kept=True):
    specs = [pl.BlockSpec(memory_space=pltpu.SMEM)] * len(scalars)
    if space == pltpu.HBM:
        arrays = [pltpu.with_memory_space_constraint(x, pltpu.HBM) for x in arrays]
    return pl.pallas_call(
        kernel,
        out_shape=[pltpu.VMEM(s, F32) if kept else jax.ShapeDtypeStruct(s, F32) for s in outs],
        in_specs=specs + [pl.BlockSpec(memory_space=space)] * len(arrays),
        out_specs=[pl.BlockSpec(memory_space=pltpu.VMEM)] * len(outs),
        scratch_shapes=[pltpu.VMEM(s, F32) if isinstance(s, tuple) else s for s in scratch],
        compiler_params=pltpu.CompilerParams(vmem_limit_bytes=megabytes * 1024 * 1024),
    )(*scalars, *arrays)


def both_ways(to_right, to_left, axis):
    count = lax.axis_size(axis)
    up = [(i, (i + 1) % count) for i in range(count)]
    down = [(target, source) for source, target in up]
    return lax.ppermute(to_right, axis, up), lax.ppermute(to_left, axis, down)


def window_of(pack, each):
    left, right = both_ways(pack, pack, "fast")
    faces = 8 + 8 * each
    upward = [
        left[4 + 2 * each : faces], left[faces + 2 :], pack[4 + each :],
        right[4 + 2 * each : faces], right[faces : faces + 2],
    ]
    downward = [
        left[: 4 + 6 * each], left[faces + 2 :], pack[: 4 + 7 * each], pack[faces:],
        right[: 4 + 6 * each], right[faces : faces + 2],
    ]
    low, high = both_ways(jnp.concatenate(upward), jnp.concatenate(downward), "slow")
    return left, pack, right, low, high


def body(observed, start_field, diagonal, noise, sweeps):
    natural = observed.shape
    block = (2, 2, YB, ZB, LANES)
    edged = (2, 2, YB + 2, ZB, LANES)
    post = (2, 2, YPOST, ZW, LANES)
    whole = (2, 2, YW, ZW, LANES)
    middle = (YM + 2 * PADM, ZM, LANES)
    low_window = (16, 24, LANES)
    fast_count, slow_count = lax.axis_size("fast"), lax.axis_size("slow")
    first, second, third = YB * slow_count // 4, 2 * ZB * fast_count // 4, 2 * LANES // 4
    faces = 2.0 * (first * second + first * third + second * third)
    lines = (2, YB * 2 * ZB, LANES)
    pack, field = call(
        pack_kernel, [(pack_tiles(8), ZB, LANES), block],
        [*[natural] * 4, (3, *lines), edged, block, block, pltpu.SemaphoreType.DMA((4,))],
        (), observed, start_field, diagonal, noise, space=pltpu.HBM,
    )
    (later,) = call(
        later_kernel, [block], [natural, natural, lines, pltpu.SemaphoreType.DMA((2,))],
        (), observed, noise, space=pltpu.HBM,
    )
    own_pack = pack
    kept_fine = kept_low = None
    for step in range(2):
        opening = step == 0
        count = 2 if opening else 1
        given = window_of(pack, 8 if opening else 4)
        outs = [(count, 4, 16, LANES), (count, 4, 8, LANES), (count, 4, 16, LANES), post, whole]
        if opening:
            *given, later = lax.optimization_barrier((*given, later))
            outs += [whole, (2, 2, YB, ZW, LANES)]
        else:
            given = (*given, *kept_fine)
        got = call(functools.partial(before_kernel, opening), outs, [whole] * 2, (sweeps,), *given)
        to_left, own, to_right, epre, q = got[:5]
        if opening:
            kept_fine = got[5:]
        left, right = both_ways(to_right, to_left, "fast")
        strip = jnp.concatenate([left, own, right], axis=2)
        strip = jnp.broadcast_to(strip[None], (slow_count // 2, *strip.shape))
        chips = [[2 * n + core for n in range(slow_count // 2)] for core in range(2)]
        mine = lax.all_to_all(strip, "slow", 0, 0, axis_index_groups=chips, tiled=True)
        other = lax.ppermute(mine, "slow", [(n, n ^ 1) for n in range(slow_count)])
        outs = [(fast_count, LANES), middle, middle, (YPOST // 2, ZW, LANES)]
        scratch = [
            middle, (16, ZM + 8, LANES), (16 + 2 * PADL, 24, LANES), (16 + 2 * PADL, 24, LANES),
            low_window, (YPOST // 2, 48, LANES),
        ]
        if opening:
            outs += [middle, (YM, ZM, LANES), low_window, low_window, (24, LANES)]
            given = (mine, other)
        else:
            given = (mine, other, *kept_low)
        got = call(functools.partial(coarse_kernel, opening), outs, scratch, (sweeps,), *given)
        part, e1, q1, e2 = got[:4]
        if opening:
            kept_low = got[4:]
        parts = lax.all_to_all(part, "fast", 0, 0, tiled=True)
        given = (parts, e1, q1, kept_low[0], e2, epre, q, kept_fine[0], field)
        scratch = [(YPOST, ZW, LANES)] * 2 + [post] * 2
        kernel = functools.partial(after_kernel, not opening, faces)
        if opening:
            outs = [(pack_tiles(4), ZB, LANES), block]
            given = (*given, later, own_pack)
            pack, field = call(kernel, outs, scratch + [edged], (sweeps,), *given)
        else:
            halves = [(2, YB * 2 * ZB, LANES)]
            (out,) = call(kernel, [natural], scratch + halves, (sweeps,), *given, kept=False)
    return out


def solution(mesh):
    placed = (
        P("slow", "fast", None),
        P("slow", "fast", None),
        P("slow", "fast", None),
        P(None, "slow", "fast", None),
        P(),
    )
    return jax.shard_map(
        body, mesh=mesh, in_specs=placed, out_specs=P("slow", "fast", None), check_vma=False
    )
```

```python
import functools

import jax
import jax.numpy as jnp
from jax import lax
from jax.experimental import pallas as pl
from jax.experimental.pallas import tpu as pltpu
from jax.sharding import PartitionSpec as P

OMEGA = 0.7
KEEP = 1.0 - OMEGA
F32 = jnp.float32

YB, ZB, LANES = 8, 8, 128
YW, ZW = 3 * YB, 3 * ZB
ZM, YM = 40, 32
YPOST = 16
PADM, PADL = 8, 4
FINE, FLAT = 24, 32
PARITIES = ((0, 0), (0, 1), (1, 0), (1, 1))


def lane_iota(rows):
    return lax.broadcasted_iota(jnp.int32, (rows, LANES), 1)


def row_iota(rows):
    return lax.broadcasted_iota(jnp.int32, (rows, LANES), 0)


def parity_matrix(transposed):
    row = lax.broadcasted_iota(jnp.int32, (2 * LANES, 2 * LANES), 0)
    col = lax.broadcasted_iota(jnp.int32, (2 * LANES, 2 * LANES), 1)
    if transposed:
        row, col = col, row
    return jnp.where(row == 2 * (col & (LANES - 1)) + (col >> 7), 1.0, 0.0).astype(F32)


def exact_dot(a, b):
    return lax.dot(a, b, precision=lax.Precision.HIGHEST, preferred_element_type=F32)


def over(low, high, chunk, one):
    chunk = min(chunk, high - low)
    turns, rest = divmod(high - low, chunk)
    for n in range(rest):
        one(high - rest + n)
    if turns == 1:
        for n in range(chunk):
            one(low + n)
        return

    def turn(at, carry):
        for n in range(chunk):
            one(low + at * chunk + n)
        return carry

    lax.fori_loop(0, turns, turn, 0)


def fine_neighbours(u, y, lanes):
    rows = u.shape[-2]
    here = {p: u[(*p, y)] for p in PARITIES}
    beside = {}
    for pz, px in PARITIES:
        total = u[pz, px, y - 1] + u[pz, px, y + 1]
        other = here[1 - pz, px]
        total = total + (other + pltpu.roll(other, 1 if pz == 0 else rows - 1, 0))
        other = here[pz, 1 - px]
        if px == 0:
            moved = jnp.where(lanes == 0, 0.0, pltpu.roll(other, 1, 1))
        else:
            moved = jnp.where(lanes == LANES - 1, 0.0, pltpu.roll(other, LANES - 1, 1))
        beside[pz, px] = total + (other + moved)
    return here, beside


def flat_neighbours(u, y, lanes, step):
    rows = u.shape[-2]
    here = u[y]
    total = u[y - 1] + u[y + 1]
    total = total + (pltpu.roll(here, 1, 0) + pltpu.roll(here, rows - 1, 0))
    left = jnp.where(lanes < step, 0.0, pltpu.roll(here, step, 1))
    right = jnp.where(lanes >= LANES - step, 0.0, pltpu.roll(here, LANES - step, 1))
    return here, total + (left + right)


def fine_sweep(source, target, q, k, low, high, chunk, lanes, shift=0, offset=0):
    def one(y):
        here, beside = fine_neighbours(source, y, lanes)
        for p in PARITIES:
            target[(*p, y - shift)] = (
                KEEP * here[p] + q[(*p, y + offset)] + k[(*p, y + offset)] * beside[p]
            )

    over(low, high, chunk, one)


def flat_sweep(source, target, q, k, low, high, chunk, lanes, step):
    def one(y):
        here, beside = flat_neighbours(source, y, lanes, step)
        target[y] = KEEP * here + q(y) + k(y) * beside

    over(low, high, chunk, one)


def closed_neighbours(u, y, lanes):
    rows = row_iota(ZB)
    here = {p: u[(*p, y)] for p in PARITIES}
    beside = {}
    for pz, px in PARITIES:
        total = u[pz, px, y - 1] + u[pz, px, y + 1]
        other = here[1 - pz, px]
        if pz == 0:
            moved = jnp.where(rows == 0, 0.0, pltpu.roll(other, 1, 0))
        else:
            moved = jnp.where(rows == ZB - 1, 0.0, pltpu.roll(other, ZB - 1, 0))
        total = total + (other + moved)
        other = here[pz, 1 - px]
        if px == 0:
            moved = jnp.where(lanes == 0, 0.0, pltpu.roll(other, 1, 1))
        else:
            moved = jnp.where(lanes == LANES - 1, 0.0, pltpu.roll(other, LANES - 1, 1))
        beside[pz, px] = total + (other + moved)
    return here, beside


def tile_of(p):
    return 2 * p[0] + p[1]


def pack_tiles(each):
    return 12 + 8 * each


def write_pack(s, linear, diag, out, each, lanes):
    for p in PARITIES:
        n = tile_of(p)
        out[n] = s[(*p, 1)]
        out[4 + 8 * each + n] = s[(*p, 8)]

    def one(y):
        here, beside = closed_neighbours(s, y + 1, lanes)
        for p in PARITIES:
            g = diag(p, y)
            out[4 + each * y + tile_of(p)] = linear(p, y) - (g + 6.0) * here[p] + beside[p]
            if each == 8:
                out[8 + each * y + tile_of(p)] = g

    for y in range(YB):
        one(y)
        for px in range(2):
            out[8 + 8 * each + px, y : y + 1] = s[0, px, y + 1, 0:1]
            out[10 + 8 * each + px, y : y + 1] = s[1, px, y + 1, ZB - 1 : ZB]


def zero_edges(s):
    for p in PARITIES:
        s[(*p, 0)] = jnp.zeros((ZB, LANES), F32)
        s[(*p, YB + 1)] = jnp.zeros((ZB, LANES), F32)


def split_by_parity(value, matrix, halves, *outs):
    both = exact_dot(value.reshape(YB * 2 * ZB, 2 * LANES), matrix)
    for px in range(2):
        halves[px] = both[:, px * LANES : (px + 1) * LANES]
    for pz, px in PARITIES:
        part = halves[px, pl.ds(pz, YB * ZB, stride=2), :].reshape(YB, ZB, LANES)
        for out in outs:
            out[pz, px] = part


def copies_of(pairs, sems):
    copies = [pltpu.make_async_copy(*pair, sems.at[n]) for n, pair in enumerate(pairs)]
    for copy in copies:
        copy.start()
    return copies


def pack_kernel(observed, start, diagonal, noise, pack, field, a, b, c, d, halves, s, g, linear, sems):
    copies = copies_of(((start, a), (diagonal, b), (observed, c), (noise.at[0], d)), sems)
    matrix = parity_matrix(False)
    zero_edges(s)
    copies[0].wait()
    split_by_parity(a[...], matrix, halves.at[0], field, s.at[:, :, 1 : YB + 1])
    copies[1].wait()
    split_by_parity(b[...], matrix, halves.at[1], g)
    copies[2].wait()
    copies[3].wait()
    split_by_parity(c[...] + 2.0 * d[...], matrix, halves.at[2], linear)
    write_pack(s, lambda p, y: linear[(*p, y)], lambda p, y: g[(*p, y)], pack, 8, lane_iota(ZB))


def later_kernel(observed, noise, later, c, d, halves, sems):
    for copy in copies_of(((observed, c), (noise.at[1], d)), sems):
        copy.wait()
    split_by_parity(c[...] + 2.0 * d[...], parity_matrix(False), halves, later)


def inside(axis, which):
    at = lax.axis_index(axis) + (which - 1)
    return jnp.where((at >= 0) & (at < lax.axis_size(axis)), 1.0, 0.0).astype(F32)


def before_kernel(first, sweeps, *refs):
    across, low, high = refs[:3], refs[3], refs[4]
    if first:
        left_out, own_out, right_out, epre, q, k, dn = refs[5:12]
        a, b = refs[12:]
    else:
        k, dn = refs[5:7]
        left_out, own_out, right_out, epre, q = refs[7:12]
        a, b = refs[12:]
    each = 8 if first else 4
    lanes = lane_iota(ZW)
    rows = row_iota(ZW)
    tile_rows = row_iota(ZB)
    in_z = [inside("fast", n) for n in range(3)]
    in_y = [inside("slow", n) for n in range(3)]
    row_mask = jnp.where(rows < ZB, in_z[0], jnp.where(rows < 2 * ZB, 1.0, in_z[2]))
    masks = [row_mask * in_y[0], row_mask, row_mask * in_y[2]]

    corner = 4 * each + 6 + each // 4
    bases = (0, corner, corner + 7 * each + 8)

    def load(yb, zb, n):
        if yb == 1:
            return across[zb][n]
        ref, base, y = low if yb == 0 else high, bases[zb], (n - 4) // each
        if zb == 1:
            return ref[base + n - (4 + each if yb == 0 else 0)]
        if yb == 0 and y >= 4:
            return ref[base + n - (4 + 4 * each)]
        if yb == 2 and y < 4:
            return ref[base + n]
        at = n - 4 - (2 if yb == 0 else 4) * each
        if not 0 <= at < 2 * each:
            return jnp.zeros((ZB, LANES), F32)
        row = ref[base + 4 * each + 4 + at // 8, at % 8 : at % 8 + 1]
        return jnp.where(tile_rows == (ZB - 1 if zb == 0 else 0), row, 0.0)

    def z_face(yb, zb, which, px, y):
        if yb == 1:
            face = across[zb].at[8 + 8 * each + 2 * which + px]
        elif zb == 1:
            face = (low if yb == 0 else high).at[bases[1] + 7 * each + 4 + 2 * which + px]
        else:
            face = (low if yb == 0 else high).at[bases[zb] + corner - 2 + px]
        return face[pl.ds(y, 1), :]

    def wide(yb, n):
        return jnp.concatenate([load(yb, zb, n) for zb in range(3)], axis=0)

    def right_side(yb, y):
        row = yb * YB + y
        for p in PARITIES:
            pz, px = p
            tiles = [load(yb, zb, 4 + each * y + tile_of(p)) for zb in range(3)]
            if pz == 1:
                edge = tile_rows == ZB - 1
                tiles[0] = tiles[0] + jnp.where(edge, z_face(yb, 1, 0, px, y), 0.0)
                tiles[1] = tiles[1] + jnp.where(edge, z_face(yb, 2, 0, px, y) * in_z[2], 0.0)
            else:
                edge = tile_rows == 0
                tiles[1] = tiles[1] + jnp.where(edge, z_face(yb, 0, 1, px, y) * in_z[0], 0.0)
                tiles[2] = tiles[2] + jnp.where(edge, z_face(yb, 1, 1, px, y), 0.0)
            rhs = jnp.concatenate(tiles, axis=0)
            if isinstance(y, int) and y == 0 and yb > 0:
                rhs = rhs + wide(yb - 1, 4 + 8 * each + tile_of(p)) * in_y[yb - 1]
            if isinstance(y, int) and y == YB - 1 and yb < 2:
                rhs = rhs + wide(yb + 1, tile_of(p)) * in_y[yb + 1]
            if first:
                full = wide(yb, 8 + each * y + tile_of(p)) + 6.0
                gain = (OMEGA / full) * masks[yb]
                k[(*p, row)] = gain
                if yb == 1:
                    dn[(*p, y)] = full * (1.0 / OMEGA)
            else:
                gain = k[(*p, row)]
            start = gain * rhs
            q[(*p, row)] = start
            a[(*p, row)] = start
            b[(*p, row)] = start

    for yb in range(3):
        over(1, YB - 1, YB, functools.partial(right_side, yb))
    right_side(0, YB - 1)
    right_side(1, 0)
    right_side(1, YB - 1)
    right_side(2, 0)

    @pl.when(sweeps[0] >= 4)
    def _():
        fine_sweep(a, b, q, k, 2, 22, FINE, lanes)

    @pl.when(sweeps[0] >= 3)
    def _():
        fine_sweep(b, a, q, k, 3, 21, FINE, lanes)

    fine_sweep(a, epre, q, k, 4, 20, FINE, lanes, shift=4)
    zero = jnp.zeros((ZW, LANES), F32)

    def restrict(ym):
        total = zero
        diag = zero
        for half in range(2):
            row = YB + 2 * ym + half
            here, beside = fine_neighbours(epre, row - 4, lanes)
            for p in PARITIES:
                scaled = q[(*p, row)] - OMEGA * here[p] + k[(*p, row)] * beside[p]
                total = total + scaled * dn[(*p, 2 * ym + half)]
                if first:
                    diag = diag + wide(1, 8 + each * (2 * ym + half) + tile_of(p))
        for n, value in enumerate((total, diag) if first else (total,)):
            value = value * 0.125
            right_out[n, ym] = value[: 2 * ZB]
            own_out[n, ym] = value[ZB : 2 * ZB]
            left_out[n, ym] = value[ZB:]

    over(0, YB // 2, 4, restrict)


def coarse_kernel(first, sweeps, *refs):
    mine, other = refs[:2]
    if first:
        part, e1, q1, e2_out, k1, d1, k2, d2, g2sum = refs[2:11]
        va, t, wa, wb, q2, x2 = refs[11:]
    else:
        k1, d1, k2, d2, g2sum = refs[2:7]
        part, e1, q1, e2_out = refs[7:11]
        va, t, wa, wb, q2, x2 = refs[11:]
    fast = lax.axis_index("fast")
    slow = lax.axis_index("slow")

    lanes = lane_iota(ZM)
    even = (lanes & 1) == 0
    zrow = row_iota(ZM) + (fast * ZB - 2 * ZB)
    mask = jnp.where((zrow >= 0) & (zrow < lax.axis_size("fast") * ZB), 1.0, 0.0).astype(F32)
    zero = jnp.zeros((ZM, LANES), F32)
    for n in (*range(PADM), *range(PADM + YM, YM + 2 * PADM)):
        va[n] = zero
        e1[n] = zero
        q1[n] = zero
        if first:
            k1[n] = zero

    here_first = slow & 1

    def opening(chip):
        for gathered, core in ((mine, here_first), (other, 1 - here_first)):
            for ym in range(4):
                y = chip * 8 + core * 4 + ym
                rhs = gathered[chip, 0, ym]
                if first:
                    diag = gathered[chip, 1, ym]
                    d1[y] = diag
                    full = diag + 1.5
                    gain = (OMEGA / full) * mask
                    k1[PADM + y] = gain * 0.25
                    start = gain * rhs
                else:
                    start = (4.0 * k1[PADM + y]) * rhs
                q1[PADM + y] = start
                va[PADM + y] = start
                e1[PADM + y] = start

    over(0, YM // 8, 4, opening)
    of_q1, of_k1 = (lambda y: q1[y]), (lambda y: k1[y])

    @pl.when(sweeps[1] >= 4)
    def _():
        flat_sweep(va, e1, of_q1, of_k1, PADM, PADM + YM, FLAT, lanes, 1)

    @pl.when(sweeps[1] >= 3)
    def _():
        flat_sweep(e1, va, of_q1, of_k1, PADM, PADM + YM, FLAT, lanes, 1)

    flat_sweep(va, e1, of_q1, of_k1, PADM, PADM + YM, FLAT, lanes, 1)

    def pair_sum(value):
        return value + jnp.where(even, pltpu.roll(value, LANES - 1, 1), pltpu.roll(value, 1, 1))

    def restrict(yc):
        total = zero
        for half in range(2):
            y = PADM + 2 * yc + half
            here, beside = flat_neighbours(e1, y, lanes, 1)
            total = total + (q1[y] - OMEGA * here + k1[y] * beside) * (d1[2 * yc + half] + 1.5)
        t[yc, :ZM] = pair_sum(total * (1.0 / OMEGA))
        t[yc, ZM:] = jnp.zeros((8, LANES), F32)

    over(0, YM // 2, 16, restrict)
    lanes2 = lane_iota(24)
    rows2 = row_iota(24)
    zrow2 = rows2 + (fast * 4 - 8)
    mask2 = jnp.where(
        (zrow2 >= 0) & (zrow2 < lax.axis_size("fast") * 4) & (rows2 < 20), 1.0, 0.0
    ).astype(F32)
    own = jnp.where((rows2 >= 8) & (rows2 < 12), 1.0, 0.0).astype(F32)
    zero2 = jnp.zeros((24, LANES), F32)
    for n in (*range(PADL), *range(PADL + 16, 16 + 2 * PADL)):
        wa[n] = zero2
        wb[n] = zero2

    def halve(yc):
        return (t[yc, pl.ds(0, 24, stride=2), :] + t[yc, pl.ds(1, 24, stride=2), :]) * 0.125

    if first:
        for yc in range(16):
            q2[yc] = halve(yc)

        def coarse_diag(yc):
            t[yc, :ZM] = pair_sum(d1[2 * yc] + d1[2 * yc + 1])

        over(0, 16, 4, coarse_diag)
        total = zero2
        for yc in range(16):
            g2 = halve(yc)
            full = g2 + 0.375
            gain = (OMEGA / full) * mask2
            k2[yc] = gain * 0.0625
            d2[yc] = full * (1.0 / OMEGA)
            total = total + g2 * own
            start = gain * q2[yc]
            q2[yc] = start
            wa[PADL + yc] = start
            wb[PADL + yc] = start
        g2sum[...] = total
    else:
        for yc in range(16):
            start = (16.0 * k2[yc]) * halve(yc)
            q2[yc] = start
            wa[PADL + yc] = start
            wb[PADL + yc] = start
    of_q2, of_k2 = (lambda y: q2[y - PADL]), (lambda y: k2[y - PADL])

    @pl.when(sweeps[2] >= 4)
    def _():
        flat_sweep(wa, wb, of_q2, of_k2, PADL, PADL + 16, FLAT, lanes2, 2)

    @pl.when(sweeps[2] >= 3)
    def _():
        flat_sweep(wb, wa, of_q2, of_k2, PADL, PADL + 16, FLAT, lanes2, 2)

    flat_sweep(wa, wb, of_q2, of_k2, PADL, PADL + 16, FLAT, lanes2, 2)
    total = zero2
    for yc in range(16):
        here, beside = flat_neighbours(wb, yc + PADL, lanes2, 2)
        total = total + (q2[yc] - OMEGA * here + k2[yc] * beside) * d2[yc]
    numer = jnp.sum(total * own, axis=0, keepdims=True)
    denom = jnp.sum(g2sum[...], axis=0, keepdims=True)
    part[...] = jnp.where((lane_iota(part.shape[0]) & 1) == 0, numer, denom)
    for y in range(YPOST // 2):
        value = wb[2 * slow + (PADL - 3) + y]
        x2[y, pl.ds(0, 24, stride=2), :] = value
        x2[y, pl.ds(1, 24, stride=2), :] = value
        e2_out[y] = x2[y, ZB : 4 * ZB]


def after_kernel(last, faces, sweeps, *refs):
    if last:
        parts, e1, q1, k1, e2, epre, q, k, field, out, va, vb, a, b, halves = refs
    else:
        parts, e1, q1, k1, e2, epre, q, k, field, later, pack, out, field_out, va, vb, a, b, s = refs
    lanes = lane_iota(ZW)
    lanes_p = lane_iota(parts.shape[0])
    every = parts[...]
    numer = jnp.sum(jnp.where((lanes_p & 1) == 0, every, 0.0))
    denom = jnp.sum(jnp.where((lanes_p & 1) == 1, every, 0.0)) + 0.0625 * faces
    shift = jnp.full((ZW, LANES), numer, F32) / jnp.full((ZW, LANES), denom, F32)
    base = 4 * lax.axis_index("slow") + (PADM - 6)

    def of_q1(y):
        return q1[base + y, ZB : 4 * ZB]

    def of_k1(y):
        return k1[base + y, ZB : 4 * ZB]

    for y in range(YPOST):
        raised = e1[base + y, ZB : 4 * ZB] + (e2[y // 2] + shift)
        raised = jnp.where(of_k1(y) > 0.0, raised, 0.0)
        va[y] = raised
        vb[y] = raised

    @pl.when(sweeps[1] >= 4)
    def _():
        flat_sweep(vb, va, of_q1, of_k1, 1, 15, FLAT, lanes, 1)

    @pl.when(sweeps[1] >= 3)
    def _():
        flat_sweep(va, vb, of_q1, of_k1, 2, 14, FLAT, lanes, 1)

    flat_sweep(vb, va, of_q1, of_k1, 3, 13, FLAT, lanes, 1)
    flat_sweep(va, vb, of_q1, of_k1, 4, 12, FLAT, lanes, 1)

    def raise_fine(ym):
        value = vb[ym + 4]
        for half in range(2):
            y = 2 * ym + half
            for p in PARITIES:
                raised = jnp.where(k[(*p, y + 4)] > 0.0, epre[(*p, y)] + value, 0.0)
                a[(*p, y)] = raised
                b[(*p, y)] = raised

    over(0, YPOST // 2, 8, raise_fine)

    @pl.when(sweeps[0] >= 4)
    def _():
        fine_sweep(b, a, q, k, 1, 15, FINE, lanes, offset=4)

    @pl.when(sweeps[0] >= 3)
    def _():
        fine_sweep(a, b, q, k, 2, 14, FINE, lanes, offset=4)

    fine_sweep(b, a, q, k, 3, 13, FINE, lanes, offset=4)
    fine_sweep(a, b, q, k, 4, 12, FINE, lanes, offset=4)
    if not last:
        zero_edges(s)
    for pz, px in PARITIES:
        value = field[pz, px] + 0.5 * b[pz, px, 4:12, ZB : 2 * ZB]
        if last:
            halves[px, pl.ds(pz, YB * ZB, stride=2), :] = value.reshape(YB * ZB, LANES)
        else:
            field_out[pz, px] = value
            s[pz, px, 1 : YB + 1] = value
    if last:
        both = jnp.concatenate([halves[0], halves[1]], axis=1)
        out[...] = exact_dot(both, parity_matrix(True)).reshape(YB, 2 * ZB, 2 * LANES)
    else:
        write_pack(
            s, lambda p, y: later[(*p, y)], lambda p, y: pack[8 + 8 * y + tile_of(p)], out, 4, lane_iota(ZB)
        )


def call(kernel, outs, scratch, scalars, *arrays, space=pltpu.VMEM, megabytes=16, kept=True):
    specs = [pl.BlockSpec(memory_space=pltpu.SMEM)] * len(scalars)
    if space == pltpu.HBM:
        arrays = [pltpu.with_memory_space_constraint(x, pltpu.HBM) for x in arrays]
    return pl.pallas_call(
        kernel,
        out_shape=[pltpu.VMEM(s, F32) if kept else jax.ShapeDtypeStruct(s, F32) for s in outs],
        in_specs=specs + [pl.BlockSpec(memory_space=space)] * len(arrays),
        out_specs=[pl.BlockSpec(memory_space=pltpu.VMEM)] * len(outs),
        scratch_shapes=[pltpu.VMEM(s, F32) if isinstance(s, tuple) else s for s in scratch],
        compiler_params=pltpu.CompilerParams(vmem_limit_bytes=megabytes * 1024 * 1024),
    )(*scalars, *arrays)


def both_ways(to_right, to_left, axis):
    count = lax.axis_size(axis)
    up = [(i, (i + 1) % count) for i in range(count)]
    down = [(target, source) for source, target in up]
    return lax.ppermute(to_right, axis, up), lax.ppermute(to_left, axis, down)


def window_of(pack, each):
    left, right = both_ways(pack, pack, "fast")
    faces = 8 + 8 * each

    def packed(block, first, half_row):
        return block[first : first + 2 * each, half_row : half_row + 1].reshape(each // 4, ZB, LANES)

    upward = [
        left[4 + 4 * each : faces], packed(left, 4 + 2 * each, ZB - 1), left[faces + 2 :],
        pack[4 + each :],
        right[4 + 4 * each : faces], packed(right, 4 + 2 * each, 0), right[faces : faces + 2],
    ]
    downward = [
        left[: 4 + 4 * each], packed(left, 4 + 4 * each, ZB - 1), left[faces + 2 :],
        pack[: 4 + 7 * each], pack[faces:],
        right[: 4 + 4 * each], packed(right, 4 + 4 * each, 0), right[faces : faces + 2],
    ]
    low, high = both_ways(jnp.concatenate(upward), jnp.concatenate(downward), "slow")
    return left, pack, right, low, high


def body(observed, start_field, diagonal, noise, sweeps):
    natural = observed.shape
    block = (2, 2, YB, ZB, LANES)
    edged = (2, 2, YB + 2, ZB, LANES)
    post = (2, 2, YPOST, ZW, LANES)
    whole = (2, 2, YW, ZW, LANES)
    middle = (YM + 2 * PADM, ZM, LANES)
    low_window = (16, 24, LANES)
    fast_count, slow_count = lax.axis_size("fast"), lax.axis_size("slow")
    first, second, third = YB * slow_count // 4, 2 * ZB * fast_count // 4, 2 * LANES // 4
    faces = 2.0 * (first * second + first * third + second * third)
    lines = (2, YB * 2 * ZB, LANES)
    pack, field = call(
        pack_kernel, [(pack_tiles(8), ZB, LANES), block],
        [*[natural] * 4, (3, *lines), edged, block, block, pltpu.SemaphoreType.DMA((4,))],
        (), observed, start_field, diagonal, noise, space=pltpu.HBM,
    )
    (later,) = call(
        later_kernel, [block], [natural, natural, lines, pltpu.SemaphoreType.DMA((2,))],
        (), observed, noise, space=pltpu.HBM,
    )
    own_pack = pack
    kept_fine = kept_low = None
    for step in range(2):
        opening = step == 0
        count = 2 if opening else 1
        given = window_of(pack, 8 if opening else 4)
        outs = [(count, 4, 16, LANES), (count, 4, 8, LANES), (count, 4, 16, LANES), post, whole]
        if opening:
            *given, later = lax.optimization_barrier((*given, later))
            outs += [whole, (2, 2, YB, ZW, LANES)]
        else:
            given = (*given, *kept_fine)
        got = call(functools.partial(before_kernel, opening), outs, [whole] * 2, (sweeps,), *given)
        to_left, own, to_right, epre, q = got[:5]
        if opening:
            kept_fine = got[5:]
        left, right = both_ways(to_right, to_left, "fast")
        strip = jnp.concatenate([left, own, right], axis=2)
        strip = jnp.broadcast_to(strip[None], (slow_count // 2, *strip.shape))
        chips = [[2 * n + core for n in range(slow_count // 2)] for core in range(2)]
        mine = lax.all_to_all(strip, "slow", 0, 0, axis_index_groups=chips, tiled=True)
        other = lax.ppermute(mine, "slow", [(n, n ^ 1) for n in range(slow_count)])
        outs = [(fast_count, LANES), middle, middle, (YPOST // 2, ZW, LANES)]
        scratch = [
            middle, (16, ZM + 8, LANES), (16 + 2 * PADL, 24, LANES), (16 + 2 * PADL, 24, LANES),
            low_window, (YPOST // 2, 48, LANES),
        ]
        if opening:
            outs += [middle, (YM, ZM, LANES), low_window, low_window, (24, LANES)]
            given = (mine, other)
        else:
            given = (mine, other, *kept_low)
        got = call(functools.partial(coarse_kernel, opening), outs, scratch, (sweeps,), *given)
        part, e1, q1, e2 = got[:4]
        if opening:
            kept_low = got[4:]
        parts = lax.all_to_all(part, "fast", 0, 0, tiled=True)
        given = (parts, e1, q1, kept_low[0], e2, epre, q, kept_fine[0], field)
        scratch = [(YPOST, ZW, LANES)] * 2 + [post] * 2
        kernel = functools.partial(after_kernel, not opening, faces)
        if opening:
            outs = [(pack_tiles(4), ZB, LANES), block]
            given = (*given, later, own_pack)
            pack, field = call(kernel, outs, scratch + [edged], (sweeps,), *given)
        else:
            halves = [(2, YB * 2 * ZB, LANES)]
            (out,) = call(kernel, [natural], scratch + halves, (sweeps,), *given, kept=False)
    return out


def solution(mesh):
    placed = (
        P("slow", "fast", None),
        P("slow", "fast", None),
        P("slow", "fast", None),
        P(None, "slow", "fast", None),
        P(),
    )
    return jax.shard_map(
        body, mesh=mesh, in_specs=placed, out_specs=P("slow", "fast", None), check_vma=False
    )
```

```python
import functools

import jax
import jax.numpy as jnp
from jax import lax
from jax.experimental import pallas as pl
from jax.experimental.pallas import tpu as pltpu
from jax.sharding import PartitionSpec as P

OMEGA = 0.7
KEEP = 1.0 - OMEGA
F32 = jnp.float32

YB, ZB, LANES = 8, 8, 128
YW, ZW = 3 * YB, 3 * ZB
ZM, YM = 40, 32
YPOST = 16
PADM, PADL = 8, 4
FINE, FLAT = 24, 32
PARITIES = ((0, 0), (0, 1), (1, 0), (1, 1))


def lane_iota(rows):
    return lax.broadcasted_iota(jnp.int32, (rows, LANES), 1)


def row_iota(rows):
    return lax.broadcasted_iota(jnp.int32, (rows, LANES), 0)


def parity_matrix(transposed):
    row = lax.broadcasted_iota(jnp.int32, (2 * LANES, 2 * LANES), 0)
    col = lax.broadcasted_iota(jnp.int32, (2 * LANES, 2 * LANES), 1)
    if transposed:
        row, col = col, row
    return jnp.where(row == 2 * (col & (LANES - 1)) + (col >> 7), 1.0, 0.0).astype(F32)


def exact_dot(a, b):
    return lax.dot(a, b, precision=lax.Precision.HIGHEST, preferred_element_type=F32)


def over(low, high, chunk, one):
    chunk = min(chunk, high - low)
    turns, rest = divmod(high - low, chunk)
    for n in range(rest):
        one(high - rest + n)
    if turns == 1:
        for n in range(chunk):
            one(low + n)
        return

    def turn(at, carry):
        for n in range(chunk):
            one(low + at * chunk + n)
        return carry

    lax.fori_loop(0, turns, turn, 0)


def fine_neighbours(u, y, lanes):
    rows = u.shape[-2]
    here = {p: u[(*p, y)] for p in PARITIES}
    beside = {}
    for pz, px in PARITIES:
        total = u[pz, px, y - 1] + u[pz, px, y + 1]
        other = here[1 - pz, px]
        total = total + (other + pltpu.roll(other, 1 if pz == 0 else rows - 1, 0))
        other = here[pz, 1 - px]
        if px == 0:
            moved = jnp.where(lanes == 0, 0.0, pltpu.roll(other, 1, 1))
        else:
            moved = jnp.where(lanes == LANES - 1, 0.0, pltpu.roll(other, LANES - 1, 1))
        beside[pz, px] = total + (other + moved)
    return here, beside


def flat_neighbours(u, y, lanes, step):
    rows = u.shape[-2]
    here = u[y]
    total = u[y - 1] + u[y + 1]
    total = total + (pltpu.roll(here, 1, 0) + pltpu.roll(here, rows - 1, 0))
    left = jnp.where(lanes < step, 0.0, pltpu.roll(here, step, 1))
    right = jnp.where(lanes >= LANES - step, 0.0, pltpu.roll(here, LANES - step, 1))
    return here, total + (left + right)


def fine_sweep(source, target, q, k, low, high, chunk, lanes, shift=0, offset=0):
    def one(y):
        here, beside = fine_neighbours(source, y, lanes)
        for p in PARITIES:
            target[(*p, y - shift)] = (
                KEEP * here[p] + q[(*p, y + offset)] + k[(*p, y + offset)] * beside[p]
            )

    over(low, high, chunk, one)


def flat_sweep(source, target, q, k, low, high, chunk, lanes, step):
    def one(y):
        here, beside = flat_neighbours(source, y, lanes, step)
        target[y] = KEEP * here + q(y) + k(y) * beside

    over(low, high, chunk, one)


def closed_neighbours(u, y, lanes):
    rows = row_iota(ZB)
    here = {p: u[(*p, y)] for p in PARITIES}
    beside = {}
    for pz, px in PARITIES:
        total = u[pz, px, y - 1] + u[pz, px, y + 1]
        other = here[1 - pz, px]
        if pz == 0:
            moved = jnp.where(rows == 0, 0.0, pltpu.roll(other, 1, 0))
        else:
            moved = jnp.where(rows == ZB - 1, 0.0, pltpu.roll(other, ZB - 1, 0))
        total = total + (other + moved)
        other = here[pz, 1 - px]
        if px == 0:
            moved = jnp.where(lanes == 0, 0.0, pltpu.roll(other, 1, 1))
        else:
            moved = jnp.where(lanes == LANES - 1, 0.0, pltpu.roll(other, LANES - 1, 1))
        beside[pz, px] = total + (other + moved)
    return here, beside


def tile_of(p):
    return 2 * p[0] + p[1]


def pack_tiles(each):
    return 12 + 8 * each


def write_pack(s, linear, diag, out, each, lanes):
    for p in PARITIES:
        n = tile_of(p)
        out[n] = s[(*p, 1)]
        out[4 + 8 * each + n] = s[(*p, 8)]

    def one(y):
        here, beside = closed_neighbours(s, y + 1, lanes)
        for p in PARITIES:
            g = diag(p, y)
            out[4 + each * y + tile_of(p)] = linear(p, y) - (g + 6.0) * here[p] + beside[p]
            if each == 8:
                out[8 + each * y + tile_of(p)] = g

    for y in range(YB):
        one(y)
        for px in range(2):
            out[8 + 8 * each + px, y : y + 1] = s[0, px, y + 1, 0:1]
            out[10 + 8 * each + px, y : y + 1] = s[1, px, y + 1, ZB - 1 : ZB]


def zero_edges(s):
    for p in PARITIES:
        s[(*p, 0)] = jnp.zeros((ZB, LANES), F32)
        s[(*p, YB + 1)] = jnp.zeros((ZB, LANES), F32)


def split_by_parity(value, matrix, halves, *outs):
    both = exact_dot(value.reshape(YB * 2 * ZB, 2 * LANES), matrix)
    for px in range(2):
        halves[px] = both[:, px * LANES : (px + 1) * LANES]
    for pz, px in PARITIES:
        part = halves[px, pl.ds(pz, YB * ZB, stride=2), :].reshape(YB, ZB, LANES)
        for out in outs:
            out[pz, px] = part


def copies_of(pairs, sems):
    copies = [pltpu.make_async_copy(*pair, sems.at[n]) for n, pair in enumerate(pairs)]
    for copy in copies:
        copy.start()
    return copies


def pack_kernel(observed, start, diagonal, noise, pack, field, a, b, c, d, halves, s, g, linear, sems):
    copies = copies_of(((start, a), (diagonal, b), (observed, c), (noise.at[0], d)), sems)
    matrix = parity_matrix(False)
    zero_edges(s)
    copies[0].wait()
    split_by_parity(a[...], matrix, halves.at[0], field, s.at[:, :, 1 : YB + 1])
    copies[1].wait()
    split_by_parity(b[...], matrix, halves.at[1], g)
    copies[2].wait()
    copies[3].wait()
    split_by_parity(c[...] + 2.0 * d[...], matrix, halves.at[2], linear)
    write_pack(s, lambda p, y: linear[(*p, y)], lambda p, y: g[(*p, y)], pack, 8, lane_iota(ZB))


def later_kernel(observed, noise, later, c, d, halves, sems):
    for copy in copies_of(((observed, c), (noise.at[1], d)), sems):
        copy.wait()
    split_by_parity(c[...] + 2.0 * d[...], parity_matrix(False), halves, later)


def inside(axis, which):
    at = lax.axis_index(axis) + (which - 1)
    return jnp.where((at >= 0) & (at < lax.axis_size(axis)), 1.0, 0.0).astype(F32)


def before_kernel(first, sweeps, *refs):
    across, low, high = refs[:3], refs[3], refs[4]
    if first:
        outer_out, own_out, inner_out, epre, q, k, dn = refs[5:12]
        a, b = refs[12:]
    else:
        k, dn = refs[5:7]
        outer_out, own_out, inner_out, epre, q = refs[7:12]
        a, b = refs[12:]
    each = 8 if first else 4
    lanes = lane_iota(ZW)
    rows = row_iota(ZW)
    tile_rows = row_iota(ZB)
    in_z = [inside("fast", n) for n in range(3)]
    in_y = [inside("slow", n) for n in range(3)]
    row_mask = jnp.where(rows < ZB, in_z[0], jnp.where(rows < 2 * ZB, 1.0, in_z[2]))
    masks = [row_mask * in_y[0], row_mask, row_mask * in_y[2]]

    corner = 4 * each + 6 + each // 4
    bases = (0, corner, corner + 7 * each + 8)

    def load(yb, zb, n):
        if yb == 1:
            return across[zb][n]
        ref, base, y = low if yb == 0 else high, bases[zb], (n - 4) // each
        if zb == 1:
            return ref[base + n - (4 + each if yb == 0 else 0)]
        if yb == 0 and y >= 4:
            return ref[base + n - (4 + 4 * each)]
        if yb == 2 and y < 4:
            return ref[base + n]
        at = n - 4 - (2 if yb == 0 else 4) * each
        if not 0 <= at < 2 * each:
            return jnp.zeros((ZB, LANES), F32)
        row = ref[base + 4 * each + 4 + at // 8, at % 8 : at % 8 + 1]
        return jnp.where(tile_rows == (ZB - 1 if zb == 0 else 0), row, 0.0)

    def z_face(yb, zb, which, px, y):
        if yb == 1:
            face = across[zb].at[8 + 8 * each + 2 * which + px]
        elif zb == 1:
            face = (low if yb == 0 else high).at[bases[1] + 7 * each + 4 + 2 * which + px]
        else:
            face = (low if yb == 0 else high).at[bases[zb] + corner - 2 + px]
        return face[pl.ds(y, 1), :]

    def wide(yb, n):
        return jnp.concatenate([load(yb, zb, n) for zb in range(3)], axis=0)

    def right_side(yb, y):
        row = yb * YB + y
        for p in PARITIES:
            pz, px = p
            tiles = [load(yb, zb, 4 + each * y + tile_of(p)) for zb in range(3)]
            if pz == 1:
                edge = tile_rows == ZB - 1
                tiles[0] = tiles[0] + jnp.where(edge, z_face(yb, 1, 0, px, y), 0.0)
                tiles[1] = tiles[1] + jnp.where(edge, z_face(yb, 2, 0, px, y) * in_z[2], 0.0)
            else:
                edge = tile_rows == 0
                tiles[1] = tiles[1] + jnp.where(edge, z_face(yb, 0, 1, px, y) * in_z[0], 0.0)
                tiles[2] = tiles[2] + jnp.where(edge, z_face(yb, 1, 1, px, y), 0.0)
            rhs = jnp.concatenate(tiles, axis=0)
            if isinstance(y, int) and y == 0 and yb > 0:
                rhs = rhs + wide(yb - 1, 4 + 8 * each + tile_of(p)) * in_y[yb - 1]
            if isinstance(y, int) and y == YB - 1 and yb < 2:
                rhs = rhs + wide(yb + 1, tile_of(p)) * in_y[yb + 1]
            if first:
                full = wide(yb, 8 + each * y + tile_of(p)) + 6.0
                gain = (OMEGA / full) * masks[yb]
                k[(*p, row)] = gain
                if yb == 1:
                    dn[(*p, y)] = full * (1.0 / OMEGA)
            else:
                gain = k[(*p, row)]
            start = gain * rhs
            q[(*p, row)] = start
            a[(*p, row)] = start
            b[(*p, row)] = start

    for yb in range(3):
        over(1, YB - 1, YB, functools.partial(right_side, yb))
    right_side(0, YB - 1)
    right_side(1, 0)
    right_side(1, YB - 1)
    right_side(2, 0)

    @pl.when(sweeps[0] >= 4)
    def _():
        fine_sweep(a, b, q, k, 2, 22, FINE, lanes)

    @pl.when(sweeps[0] >= 3)
    def _():
        fine_sweep(b, a, q, k, 3, 21, FINE, lanes)

    fine_sweep(a, epre, q, k, 4, 20, FINE, lanes, shift=4)
    zero = jnp.zeros((ZW, LANES), F32)
    odd = (lax.axis_index("fast") & 1) == 1

    def restrict(ym):
        total = zero
        diag = zero
        for half in range(2):
            row = YB + 2 * ym + half
            here, beside = fine_neighbours(epre, row - 4, lanes)
            for p in PARITIES:
                scaled = q[(*p, row)] - OMEGA * here[p] + k[(*p, row)] * beside[p]
                total = total + scaled * dn[(*p, 2 * ym + half)]
                if first:
                    diag = diag + wide(1, 8 + each * (2 * ym + half) + tile_of(p))
        for n, value in enumerate((total, diag) if first else (total,)):
            value = value * 0.125
            own_out[n, ym] = value[ZB : 2 * ZB]
            inner_out[n, ym] = jnp.where(odd, value[ZB:], value[: 2 * ZB])
            outer_out[n, ym] = jnp.where(odd, value[: 2 * ZB], value[ZB:])

    over(0, YB // 2, 4, restrict)


def coarse_kernel(first, sweeps, *refs):
    mine, other = refs[:2]
    if first:
        part, e1, q1, e2_out, k1, d1, k2, d2, g2sum = refs[2:11]
        va, t, wa, wb, q2, x2 = refs[11:]
    else:
        k1, d1, k2, d2, g2sum = refs[2:7]
        part, e1, q1, e2_out = refs[7:11]
        va, t, wa, wb, q2, x2 = refs[11:]
    fast = lax.axis_index("fast")
    slow = lax.axis_index("slow")

    lanes = lane_iota(ZM)
    even = (lanes & 1) == 0
    zrow = row_iota(ZM) + (fast * ZB - 2 * ZB)
    mask = jnp.where((zrow >= 0) & (zrow < lax.axis_size("fast") * ZB), 1.0, 0.0).astype(F32)
    zero = jnp.zeros((ZM, LANES), F32)
    for n in (*range(PADM), *range(PADM + YM, YM + 2 * PADM)):
        va[n] = zero
        e1[n] = zero
        q1[n] = zero
        if first:
            k1[n] = zero

    here_first = slow & 1

    def opening(chip):
        for gathered, core in ((mine, here_first), (other, 1 - here_first)):
            for ym in range(4):
                y = chip * 8 + core * 4 + ym
                rhs = gathered[chip, 0, ym]
                if first:
                    diag = gathered[chip, 1, ym]
                    d1[y] = diag
                    full = diag + 1.5
                    gain = (OMEGA / full) * mask
                    k1[PADM + y] = gain * 0.25
                    start = gain * rhs
                else:
                    start = (4.0 * k1[PADM + y]) * rhs
                q1[PADM + y] = start
                va[PADM + y] = start
                e1[PADM + y] = start

    over(0, YM // 8, 4, opening)
    of_q1, of_k1 = (lambda y: q1[y]), (lambda y: k1[y])

    @pl.when(sweeps[1] >= 4)
    def _():
        flat_sweep(va, e1, of_q1, of_k1, PADM, PADM + YM, FLAT, lanes, 1)

    @pl.when(sweeps[1] >= 3)
    def _():
        flat_sweep(e1, va, of_q1, of_k1, PADM, PADM + YM, FLAT, lanes, 1)

    flat_sweep(va, e1, of_q1, of_k1, PADM, PADM + YM, FLAT, lanes, 1)

    def pair_sum(value):
        return value + jnp.where(even, pltpu.roll(value, LANES - 1, 1), pltpu.roll(value, 1, 1))

    def restrict(yc):
        total = zero
        for half in range(2):
            y = PADM + 2 * yc + half
            here, beside = flat_neighbours(e1, y, lanes, 1)
            total = total + (q1[y] - OMEGA * here + k1[y] * beside) * (d1[2 * yc + half] + 1.5)
        t[yc, :ZM] = pair_sum(total * (1.0 / OMEGA))
        t[yc, ZM:] = jnp.zeros((8, LANES), F32)

    over(0, YM // 2, 16, restrict)
    lanes2 = lane_iota(24)
    rows2 = row_iota(24)
    zrow2 = rows2 + (fast * 4 - 8)
    mask2 = jnp.where(
        (zrow2 >= 0) & (zrow2 < lax.axis_size("fast") * 4) & (rows2 < 20), 1.0, 0.0
    ).astype(F32)
    own = jnp.where((rows2 >= 8) & (rows2 < 12), 1.0, 0.0).astype(F32)
    zero2 = jnp.zeros((24, LANES), F32)
    for n in (*range(PADL), *range(PADL + 16, 16 + 2 * PADL)):
        wa[n] = zero2
        wb[n] = zero2

    def halve(yc):
        return (t[yc, pl.ds(0, 24, stride=2), :] + t[yc, pl.ds(1, 24, stride=2), :]) * 0.125

    if first:
        for yc in range(16):
            q2[yc] = halve(yc)

        def coarse_diag(yc):
            t[yc, :ZM] = pair_sum(d1[2 * yc] + d1[2 * yc + 1])

        over(0, 16, 4, coarse_diag)
        total = zero2
        for yc in range(16):
            g2 = halve(yc)
            full = g2 + 0.375
            gain = (OMEGA / full) * mask2
            k2[yc] = gain * 0.0625
            d2[yc] = full * (1.0 / OMEGA)
            total = total + g2 * own
            start = gain * q2[yc]
            q2[yc] = start
            wa[PADL + yc] = start
            wb[PADL + yc] = start
        g2sum[...] = total
    else:
        for yc in range(16):
            start = (16.0 * k2[yc]) * halve(yc)
            q2[yc] = start
            wa[PADL + yc] = start
            wb[PADL + yc] = start
    of_q2, of_k2 = (lambda y: q2[y - PADL]), (lambda y: k2[y - PADL])

    @pl.when(sweeps[2] >= 4)
    def _():
        flat_sweep(wa, wb, of_q2, of_k2, PADL, PADL + 16, FLAT, lanes2, 2)

    @pl.when(sweeps[2] >= 3)
    def _():
        flat_sweep(wb, wa, of_q2, of_k2, PADL, PADL + 16, FLAT, lanes2, 2)

    flat_sweep(wa, wb, of_q2, of_k2, PADL, PADL + 16, FLAT, lanes2, 2)
    total = zero2
    for yc in range(16):
        here, beside = flat_neighbours(wb, yc + PADL, lanes2, 2)
        total = total + (q2[yc] - OMEGA * here + k2[yc] * beside) * d2[yc]
    numer = jnp.sum(total * own, axis=0, keepdims=True)
    denom = jnp.sum(g2sum[...], axis=0, keepdims=True)
    part[...] = jnp.where((lane_iota(part.shape[0]) & 1) == 0, numer, denom)
    for y in range(YPOST // 2):
        value = wb[2 * slow + (PADL - 3) + y]
        x2[y, pl.ds(0, 24, stride=2), :] = value
        x2[y, pl.ds(1, 24, stride=2), :] = value
        e2_out[y] = x2[y, ZB : 4 * ZB]


def after_kernel(last, faces, sweeps, *refs):
    if last:
        parts, e1, q1, k1, e2, epre, q, k, field, out, va, vb, a, b, halves = refs
    else:
        parts, e1, q1, k1, e2, epre, q, k, field, later, pack, out, field_out, va, vb, a, b, s = refs
    lanes = lane_iota(ZW)
    lanes_p = lane_iota(parts.shape[0])
    every = parts[...]
    numer = jnp.sum(jnp.where((lanes_p & 1) == 0, every, 0.0))
    denom = jnp.sum(jnp.where((lanes_p & 1) == 1, every, 0.0)) + 0.0625 * faces
    shift = jnp.full((ZW, LANES), numer, F32) / jnp.full((ZW, LANES), denom, F32)
    base = 4 * lax.axis_index("slow") + (PADM - 6)

    def of_q1(y):
        return q1[base + y, ZB : 4 * ZB]

    def of_k1(y):
        return k1[base + y, ZB : 4 * ZB]

    for y in range(YPOST):
        raised = e1[base + y, ZB : 4 * ZB] + (e2[y // 2] + shift)
        raised = jnp.where(of_k1(y) > 0.0, raised, 0.0)
        va[y] = raised
        vb[y] = raised

    @pl.when(sweeps[1] >= 4)
    def _():
        flat_sweep(vb, va, of_q1, of_k1, 1, 15, FLAT, lanes, 1)

    @pl.when(sweeps[1] >= 3)
    def _():
        flat_sweep(va, vb, of_q1, of_k1, 2, 14, FLAT, lanes, 1)

    flat_sweep(vb, va, of_q1, of_k1, 3, 13, FLAT, lanes, 1)
    flat_sweep(va, vb, of_q1, of_k1, 4, 12, FLAT, lanes, 1)

    def raise_fine(ym):
        value = vb[ym + 4]
        for half in range(2):
            y = 2 * ym + half
            for p in PARITIES:
                raised = jnp.where(k[(*p, y + 4)] > 0.0, epre[(*p, y)] + value, 0.0)
                a[(*p, y)] = raised
                b[(*p, y)] = raised

    over(0, YPOST // 2, 8, raise_fine)

    @pl.when(sweeps[0] >= 4)
    def _():
        fine_sweep(b, a, q, k, 1, 15, FINE, lanes, offset=4)

    @pl.when(sweeps[0] >= 3)
    def _():
        fine_sweep(a, b, q, k, 2, 14, FINE, lanes, offset=4)

    fine_sweep(b, a, q, k, 3, 13, FINE, lanes, offset=4)
    fine_sweep(a, b, q, k, 4, 12, FINE, lanes, offset=4)
    if not last:
        zero_edges(s)
    for pz, px in PARITIES:
        value = field[pz, px] + 0.5 * b[pz, px, 4:12, ZB : 2 * ZB]
        if last:
            halves[px, pl.ds(pz, YB * ZB, stride=2), :] = value.reshape(YB * ZB, LANES)
        else:
            field_out[pz, px] = value
            s[pz, px, 1 : YB + 1] = value
    if last:
        both = jnp.concatenate([halves[0], halves[1]], axis=1)
        out[...] = exact_dot(both, parity_matrix(True)).reshape(YB, 2 * ZB, 2 * LANES)
    else:
        write_pack(
            s, lambda p, y: later[(*p, y)], lambda p, y: pack[8 + 8 * y + tile_of(p)], out, 4, lane_iota(ZB)
        )


def call(kernel, outs, scratch, scalars, *arrays, space=pltpu.VMEM, megabytes=16, kept=True):
    specs = [pl.BlockSpec(memory_space=pltpu.SMEM)] * len(scalars)
    if space == pltpu.HBM:
        arrays = [pltpu.with_memory_space_constraint(x, pltpu.HBM) for x in arrays]
    return pl.pallas_call(
        kernel,
        out_shape=[pltpu.VMEM(s, F32) if kept else jax.ShapeDtypeStruct(s, F32) for s in outs],
        in_specs=specs + [pl.BlockSpec(memory_space=space)] * len(arrays),
        out_specs=[pl.BlockSpec(memory_space=pltpu.VMEM)] * len(outs),
        scratch_shapes=[pltpu.VMEM(s, F32) if isinstance(s, tuple) else s for s in scratch],
        compiler_params=pltpu.CompilerParams(vmem_limit_bytes=megabytes * 1024 * 1024),
    )(*scalars, *arrays)


def both_ways(to_right, to_left, axis):
    count = lax.axis_size(axis)
    up = [(i, (i + 1) % count) for i in range(count)]
    down = [(target, source) for source, target in up]
    return lax.ppermute(to_right, axis, up), lax.ppermute(to_left, axis, down)


def swap_fast(first, second):
    count = lax.axis_size("fast")
    inner = [(i, i ^ 1) for i in range(count)]
    outer = [(i, (i + (1 if i & 1 else -1)) % count) for i in range(count)]
    a, b = lax.ppermute(first, "fast", inner), lax.ppermute(second, "fast", outer)
    odd = (lax.axis_index("fast") & 1) == 1
    return jnp.where(odd, a, b), jnp.where(odd, b, a)


def window_of(pack, each):
    left, right = swap_fast(pack, pack)
    faces = 8 + 8 * each

    def packed(block, first, half_row):
        return block[first : first + 2 * each, half_row : half_row + 1].reshape(each // 4, ZB, LANES)

    upward = [
        left[4 + 4 * each : faces], packed(left, 4 + 2 * each, ZB - 1), left[faces + 2 :],
        pack[4 + each :],
        right[4 + 4 * each : faces], packed(right, 4 + 2 * each, 0), right[faces : faces + 2],
    ]
    downward = [
        left[: 4 + 4 * each], packed(left, 4 + 4 * each, ZB - 1), left[faces + 2 :],
        pack[: 4 + 7 * each], pack[faces:],
        right[: 4 + 4 * each], packed(right, 4 + 4 * each, 0), right[faces : faces + 2],
    ]
    low, high = both_ways(jnp.concatenate(upward), jnp.concatenate(downward), "slow")
    return left, pack, right, low, high


def body(observed, start_field, diagonal, noise, sweeps):
    natural = observed.shape
    block = (2, 2, YB, ZB, LANES)
    edged = (2, 2, YB + 2, ZB, LANES)
    post = (2, 2, YPOST, ZW, LANES)
    whole = (2, 2, YW, ZW, LANES)
    middle = (YM + 2 * PADM, ZM, LANES)
    low_window = (16, 24, LANES)
    fast_count, slow_count = lax.axis_size("fast"), lax.axis_size("slow")
    first, second, third = YB * slow_count // 4, 2 * ZB * fast_count // 4, 2 * LANES // 4
    faces = 2.0 * (first * second + first * third + second * third)
    lines = (2, YB * 2 * ZB, LANES)
    pack, field = call(
        pack_kernel, [(pack_tiles(8), ZB, LANES), block],
        [*[natural] * 4, (3, *lines), edged, block, block, pltpu.SemaphoreType.DMA((4,))],
        (), observed, start_field, diagonal, noise, space=pltpu.HBM,
    )
    (later,) = call(
        later_kernel, [block], [natural, natural, lines, pltpu.SemaphoreType.DMA((2,))],
        (), observed, noise, space=pltpu.HBM,
    )
    own_pack = pack
    kept_fine = kept_low = None
    for step in range(2):
        opening = step == 0
        count = 2 if opening else 1
        given = window_of(pack, 8 if opening else 4)
        outs = [(count, 4, 16, LANES), (count, 4, 8, LANES), (count, 4, 16, LANES), post, whole]
        if opening:
            *given, later = lax.optimization_barrier((*given, later))
            outs += [whole, (2, 2, YB, ZW, LANES)]
        else:
            given = (*given, *kept_fine)
        got = call(functools.partial(before_kernel, opening), outs, [whole] * 2, (sweeps,), *given)
        outer, own, inner, epre, q = got[:5]
        if opening:
            kept_fine = got[5:]
        left, right = swap_fast(inner, outer)
        strip = jnp.concatenate([left, own, right], axis=2)
        strip = jnp.broadcast_to(strip[None], (slow_count // 2, *strip.shape))
        chips = [[2 * n + core for n in range(slow_count // 2)] for core in range(2)]
        mine = lax.all_to_all(strip, "slow", 0, 0, axis_index_groups=chips, tiled=True)
        other = lax.ppermute(mine, "slow", [(n, n ^ 1) for n in range(slow_count)])
        outs = [(fast_count, LANES), middle, middle, (YPOST // 2, ZW, LANES)]
        scratch = [
            middle, (16, ZM + 8, LANES), (16 + 2 * PADL, 24, LANES), (16 + 2 * PADL, 24, LANES),
            low_window, (YPOST // 2, 48, LANES),
        ]
        if opening:
            outs += [middle, (YM, ZM, LANES), low_window, low_window, (24, LANES)]
            given = (mine, other)
        else:
            given = (mine, other, *kept_low)
        got = call(functools.partial(coarse_kernel, opening), outs, scratch, (sweeps,), *given)
        part, e1, q1, e2 = got[:4]
        if opening:
            kept_low = got[4:]
        parts = lax.all_to_all(part, "fast", 0, 0, tiled=True)
        given = (parts, e1, q1, kept_low[0], e2, epre, q, kept_fine[0], field)
        scratch = [(YPOST, ZW, LANES)] * 2 + [post] * 2
        kernel = functools.partial(after_kernel, not opening, faces)
        if opening:
            outs = [(pack_tiles(4), ZB, LANES), block]
            given = (*given, later, own_pack)
            pack, field = call(kernel, outs, scratch + [edged], (sweeps,), *given)
        else:
            halves = [(2, YB * 2 * ZB, LANES)]
            (out,) = call(kernel, [natural], scratch + halves, (sweeps,), *given, kept=False)
    return out


def solution(mesh):
    placed = (
        P("slow", "fast", None),
        P("slow", "fast", None),
        P("slow", "fast", None),
        P(None, "slow", "fast", None),
        P(),
    )
    return jax.shard_map(
        body, mesh=mesh, in_specs=placed, out_specs=P("slow", "fast", None), check_vma=False
    )
```

```python
import functools

import jax
import jax.numpy as jnp
from jax import lax
from jax.experimental import pallas as pl
from jax.experimental.pallas import tpu as pltpu
from jax.sharding import PartitionSpec as P

OMEGA = 0.7
KEEP = 1.0 - OMEGA
F32 = jnp.float32

YB, ZB, LANES = 8, 8, 128
YW, ZW = 3 * YB, 3 * ZB
ZM, YM = 40, 32
YPOST = 16
PADM, PADL = 8, 4
FINE, FLAT = 24, 32
PARITIES = ((0, 0), (0, 1), (1, 0), (1, 1))


def lane_iota(rows):
    return lax.broadcasted_iota(jnp.int32, (rows, LANES), 1)


def row_iota(rows):
    return lax.broadcasted_iota(jnp.int32, (rows, LANES), 0)


def parity_matrix(transposed):
    row = lax.broadcasted_iota(jnp.int32, (2 * LANES, 2 * LANES), 0)
    col = lax.broadcasted_iota(jnp.int32, (2 * LANES, 2 * LANES), 1)
    if transposed:
        row, col = col, row
    return jnp.where(row == 2 * (col & (LANES - 1)) + (col >> 7), 1.0, 0.0).astype(F32)


def exact_dot(a, b):
    return lax.dot(a, b, precision=lax.Precision.HIGHEST, preferred_element_type=F32)


def over(low, high, chunk, one):
    chunk = min(chunk, high - low)
    turns, rest = divmod(high - low, chunk)
    for n in range(rest):
        one(high - rest + n)
    if turns == 1:
        for n in range(chunk):
            one(low + n)
        return

    def turn(at, carry):
        for n in range(chunk):
            one(low + at * chunk + n)
        return carry

    lax.fori_loop(0, turns, turn, 0)


def fine_neighbours(u, y, lanes):
    rows = u.shape[-2]
    here = {p: u[(*p, y)] for p in PARITIES}
    beside = {}
    for pz, px in PARITIES:
        total = u[pz, px, y - 1] + u[pz, px, y + 1]
        other = here[1 - pz, px]
        total = total + (other + pltpu.roll(other, 1 if pz == 0 else rows - 1, 0))
        other = here[pz, 1 - px]
        if px == 0:
            moved = jnp.where(lanes == 0, 0.0, pltpu.roll(other, 1, 1))
        else:
            moved = jnp.where(lanes == LANES - 1, 0.0, pltpu.roll(other, LANES - 1, 1))
        beside[pz, px] = total + (other + moved)
    return here, beside


def flat_neighbours(u, y, lanes, step):
    rows = u.shape[-2]
    here = u[y]
    total = u[y - 1] + u[y + 1]
    total = total + (pltpu.roll(here, 1, 0) + pltpu.roll(here, rows - 1, 0))
    left = jnp.where(lanes < step, 0.0, pltpu.roll(here, step, 1))
    right = jnp.where(lanes >= LANES - step, 0.0, pltpu.roll(here, LANES - step, 1))
    return here, total + (left + right)


def fine_sweep(source, target, q, k, low, high, chunk, lanes, shift=0, offset=0):
    def one(y):
        here, beside = fine_neighbours(source, y, lanes)
        for p in PARITIES:
            target[(*p, y - shift)] = (
                KEEP * here[p] + q[(*p, y + offset)] + k[(*p, y + offset)] * beside[p]
            )

    over(low, high, chunk, one)


def flat_sweep(source, target, q, k, low, high, chunk, lanes, step):
    def one(y):
        here, beside = flat_neighbours(source, y, lanes, step)
        target[y] = KEEP * here + q(y) + k(y) * beside

    over(low, high, chunk, one)


def closed_neighbours(u, y, lanes):
    rows = row_iota(ZB)
    here = {p: u[(*p, y)] for p in PARITIES}
    beside = {}
    for pz, px in PARITIES:
        total = u[pz, px, y - 1] + u[pz, px, y + 1]
        other = here[1 - pz, px]
        if pz == 0:
            moved = jnp.where(rows == 0, 0.0, pltpu.roll(other, 1, 0))
        else:
            moved = jnp.where(rows == ZB - 1, 0.0, pltpu.roll(other, ZB - 1, 0))
        total = total + (other + moved)
        other = here[pz, 1 - px]
        if px == 0:
            moved = jnp.where(lanes == 0, 0.0, pltpu.roll(other, 1, 1))
        else:
            moved = jnp.where(lanes == LANES - 1, 0.0, pltpu.roll(other, LANES - 1, 1))
        beside[pz, px] = total + (other + moved)
    return here, beside


def tile_of(p):
    return 2 * p[0] + p[1]


def pack_tiles(each):
    return 12 + 8 * each


def write_pack(s, linear, diag, out, each, lanes):
    for p in PARITIES:
        n = tile_of(p)
        out[n] = s[(*p, 1)]
        out[4 + 8 * each + n] = s[(*p, 8)]

    def one(y):
        here, beside = closed_neighbours(s, y + 1, lanes)
        for p in PARITIES:
            g = diag(p, y)
            out[4 + each * y + tile_of(p)] = linear(p, y) - (g + 6.0) * here[p] + beside[p]
            if each == 8:
                out[8 + each * y + tile_of(p)] = g

    for y in range(YB):
        one(y)
        for px in range(2):
            out[8 + 8 * each + px, y : y + 1] = s[0, px, y + 1, 0:1]
            out[10 + 8 * each + px, y : y + 1] = s[1, px, y + 1, ZB - 1 : ZB]


def zero_edges(s):
    for p in PARITIES:
        s[(*p, 0)] = jnp.zeros((ZB, LANES), F32)
        s[(*p, YB + 1)] = jnp.zeros((ZB, LANES), F32)


def split_by_parity(value, matrix, halves, *outs):
    both = exact_dot(value.reshape(YB * 2 * ZB, 2 * LANES), matrix)
    for px in range(2):
        halves[px] = both[:, px * LANES : (px + 1) * LANES]
    for pz, px in PARITIES:
        part = halves[px, pl.ds(pz, YB * ZB, stride=2), :].reshape(YB, ZB, LANES)
        for out in outs:
            out[pz, px] = part


def copies_of(pairs, sems):
    copies = [pltpu.make_async_copy(*pair, sems.at[n]) for n, pair in enumerate(pairs)]
    for copy in copies:
        copy.start()
    return copies


def pack_kernel(observed, start, diagonal, noise, pack, field, a, b, c, d, halves, s, g, linear, sems):
    copies = copies_of(((start, a), (diagonal, b), (observed, c), (noise.at[0], d)), sems)
    matrix = parity_matrix(False)
    zero_edges(s)
    copies[0].wait()
    split_by_parity(a[...], matrix, halves.at[0], field, s.at[:, :, 1 : YB + 1])
    copies[1].wait()
    split_by_parity(b[...], matrix, halves.at[1], g)
    copies[2].wait()
    copies[3].wait()
    split_by_parity(c[...] + 2.0 * d[...], matrix, halves.at[2], linear)
    write_pack(s, lambda p, y: linear[(*p, y)], lambda p, y: g[(*p, y)], pack, 8, lane_iota(ZB))


def later_kernel(observed, noise, later, c, d, halves, sems):
    for copy in copies_of(((observed, c), (noise.at[1], d)), sems):
        copy.wait()
    split_by_parity(c[...] + 2.0 * d[...], parity_matrix(False), halves, later)


def inside(axis, which):
    at = lax.axis_index(axis) + (which - 1)
    return jnp.where((at >= 0) & (at < lax.axis_size(axis)), 1.0, 0.0).astype(F32)


def before_kernel(first, sweeps, *refs):
    across, low, high = refs[:3], refs[3], refs[4]
    if first:
        outer_out, own_out, inner_out, epre, q, k, dn = refs[5:12]
        a, b = refs[12:]
    else:
        k, dn = refs[5:7]
        outer_out, own_out, inner_out, epre, q = refs[7:12]
        a, b = refs[12:]
    each = 8 if first else 4
    lanes = lane_iota(ZW)
    rows = row_iota(ZW)
    tile_rows = row_iota(ZB)
    in_z = [inside("fast", n) for n in range(3)]
    in_y = [inside("slow", n) for n in range(3)]
    row_mask = jnp.where(rows < ZB, in_z[0], jnp.where(rows < 2 * ZB, 1.0, in_z[2]))
    masks = [row_mask * in_y[0], row_mask, row_mask * in_y[2]]

    corner = 4 * each + 6 + each // 4
    bases = (0, corner, corner + 7 * each + 8)

    def load(yb, zb, n):
        if yb == 1:
            return across[zb][n]
        ref, base, y = low if yb == 0 else high, bases[zb], (n - 4) // each
        if zb == 1:
            return ref[base + n - (4 + each if yb == 0 else 0)]
        if yb == 0 and y >= 4:
            return ref[base + n - (4 + 4 * each)]
        if yb == 2 and y < 4:
            return ref[base + n]
        at = n - 4 - (2 if yb == 0 else 4) * each
        if not 0 <= at < 2 * each:
            return jnp.zeros((ZB, LANES), F32)
        row = ref[base + 4 * each + 4 + at // 8, at % 8 : at % 8 + 1]
        return jnp.where(tile_rows == (ZB - 1 if zb == 0 else 0), row, 0.0)

    def z_face(yb, zb, which, px, y):
        if yb == 1:
            face = across[zb].at[8 + 8 * each + 2 * which + px]
        elif zb == 1:
            face = (low if yb == 0 else high).at[bases[1] + 7 * each + 4 + 2 * which + px]
        else:
            face = (low if yb == 0 else high).at[bases[zb] + corner - 2 + px]
        return face[pl.ds(y, 1), :]

    def wide(yb, n):
        return jnp.concatenate([load(yb, zb, n) for zb in range(3)], axis=0)

    def right_side(yb, y):
        row = yb * YB + y
        for p in PARITIES:
            pz, px = p
            tiles = [load(yb, zb, 4 + each * y + tile_of(p)) for zb in range(3)]
            if pz == 1:
                edge = tile_rows == ZB - 1
                tiles[0] = tiles[0] + jnp.where(edge, z_face(yb, 1, 0, px, y), 0.0)
                tiles[1] = tiles[1] + jnp.where(edge, z_face(yb, 2, 0, px, y) * in_z[2], 0.0)
            else:
                edge = tile_rows == 0
                tiles[1] = tiles[1] + jnp.where(edge, z_face(yb, 0, 1, px, y) * in_z[0], 0.0)
                tiles[2] = tiles[2] + jnp.where(edge, z_face(yb, 1, 1, px, y), 0.0)
            rhs = jnp.concatenate(tiles, axis=0)
            if isinstance(y, int) and y == 0 and yb > 0:
                rhs = rhs + wide(yb - 1, 4 + 8 * each + tile_of(p)) * in_y[yb - 1]
            if isinstance(y, int) and y == YB - 1 and yb < 2:
                rhs = rhs + wide(yb + 1, tile_of(p)) * in_y[yb + 1]
            if first:
                full = wide(yb, 8 + each * y + tile_of(p)) + 6.0
                gain = (OMEGA / full) * masks[yb]
                k[(*p, row)] = gain
                if yb == 1:
                    dn[(*p, y)] = full * (1.0 / OMEGA)
            else:
                gain = k[(*p, row)]
            start = gain * rhs
            q[(*p, row)] = start

    for yb in range(3):
        over(1, YB - 1, YB, functools.partial(right_side, yb))
    right_side(0, YB - 1)
    right_side(1, 0)
    right_side(1, YB - 1)
    right_side(2, 0)

    @pl.when(sweeps[0] >= 4)
    def _():
        fine_sweep(q, b, q, k, 2, 22, FINE, lanes)
        fine_sweep(b, a, q, k, 3, 21, FINE, lanes)

    @pl.when(sweeps[0] == 3)
    def _():
        fine_sweep(q, a, q, k, 3, 21, FINE, lanes)

    @pl.when(sweeps[0] >= 3)
    def _():
        fine_sweep(a, epre, q, k, 4, 20, FINE, lanes, shift=4)

    @pl.when(sweeps[0] < 3)
    def _():
        fine_sweep(q, epre, q, k, 4, 20, FINE, lanes, shift=4)

    zero = jnp.zeros((ZW, LANES), F32)
    odd = (lax.axis_index("fast") & 1) == 1

    def restrict(ym):
        total = zero
        diag = zero
        for half in range(2):
            row = YB + 2 * ym + half
            here, beside = fine_neighbours(epre, row - 4, lanes)
            for p in PARITIES:
                scaled = q[(*p, row)] - OMEGA * here[p] + k[(*p, row)] * beside[p]
                total = total + scaled * dn[(*p, 2 * ym + half)]
                if first:
                    diag = diag + wide(1, 8 + each * (2 * ym + half) + tile_of(p))
        for n, value in enumerate((total, diag) if first else (total,)):
            value = value * 0.125
            own_out[n, ym] = value[ZB : 2 * ZB]
            inner_out[n, ym] = jnp.where(odd, value[ZB:], value[: 2 * ZB])
            outer_out[n, ym] = jnp.where(odd, value[: 2 * ZB], value[ZB:])

    over(0, YB // 2, 4, restrict)


def coarse_kernel(first, sweeps, *refs):
    mine, other = refs[:2]
    if first:
        part, e1, q1, e2_out, k1, d1, k2, d2, g2sum = refs[2:11]
        va, t, wa, wb, q2, x2 = refs[11:]
    else:
        k1, d1, k2, d2, g2sum = refs[2:7]
        part, e1, q1, e2_out = refs[7:11]
        va, t, wa, wb, q2, x2 = refs[11:]
    fast = lax.axis_index("fast")
    slow = lax.axis_index("slow")

    lanes = lane_iota(ZM)
    even = (lanes & 1) == 0
    zrow = row_iota(ZM) + (fast * ZB - 2 * ZB)
    mask = jnp.where((zrow >= 0) & (zrow < lax.axis_size("fast") * ZB), 1.0, 0.0).astype(F32)
    zero = jnp.zeros((ZM, LANES), F32)
    for n in (*range(PADM), *range(PADM + YM, YM + 2 * PADM)):
        va[n] = zero
        e1[n] = zero
        q1[n] = zero
        if first:
            k1[n] = zero

    here_first = slow & 1

    def opening(chip):
        for gathered, core in ((mine, here_first), (other, 1 - here_first)):
            for ym in range(4):
                y = chip * 8 + core * 4 + ym
                rhs = gathered[chip, 0, ym]
                if first:
                    diag = gathered[chip, 1, ym]
                    d1[y] = diag
                    full = diag + 1.5
                    gain = (OMEGA / full) * mask
                    k1[PADM + y] = gain * 0.25
                    start = gain * rhs
                else:
                    start = (4.0 * k1[PADM + y]) * rhs
                q1[PADM + y] = start

    over(0, YM // 8, 4, opening)
    of_q1, of_k1 = (lambda y: q1[y]), (lambda y: k1[y])

    def middle_sweep(source, target):
        flat_sweep(source, target, of_q1, of_k1, PADM, PADM + YM, FLAT, lanes, 1)

    @pl.when(sweeps[1] >= 4)
    def _():
        middle_sweep(q1, e1)
        middle_sweep(e1, va)

    @pl.when(sweeps[1] == 3)
    def _():
        middle_sweep(q1, va)

    @pl.when(sweeps[1] >= 3)
    def _():
        middle_sweep(va, e1)

    @pl.when(sweeps[1] < 3)
    def _():
        middle_sweep(q1, e1)

    def pair_sum(value):
        return value + jnp.where(even, pltpu.roll(value, LANES - 1, 1), pltpu.roll(value, 1, 1))

    def restrict(yc):
        total = zero
        for half in range(2):
            y = PADM + 2 * yc + half
            here, beside = flat_neighbours(e1, y, lanes, 1)
            total = total + (q1[y] - OMEGA * here + k1[y] * beside) * (d1[2 * yc + half] + 1.5)
        t[yc, :ZM] = pair_sum(total * (1.0 / OMEGA))
        t[yc, ZM:] = jnp.zeros((8, LANES), F32)

    over(0, YM // 2, 16, restrict)
    lanes2 = lane_iota(24)
    rows2 = row_iota(24)
    zrow2 = rows2 + (fast * 4 - 8)
    mask2 = jnp.where(
        (zrow2 >= 0) & (zrow2 < lax.axis_size("fast") * 4) & (rows2 < 20), 1.0, 0.0
    ).astype(F32)
    own = jnp.where((rows2 >= 8) & (rows2 < 12), 1.0, 0.0).astype(F32)
    zero2 = jnp.zeros((24, LANES), F32)
    for n in (*range(PADL), *range(PADL + 16, 16 + 2 * PADL)):
        wa[n] = zero2
        wb[n] = zero2

    def halve(yc):
        return (t[yc, pl.ds(0, 24, stride=2), :] + t[yc, pl.ds(1, 24, stride=2), :]) * 0.125

    if first:
        for yc in range(16):
            q2[yc] = halve(yc)

        def coarse_diag(yc):
            t[yc, :ZM] = pair_sum(d1[2 * yc] + d1[2 * yc + 1])

        over(0, 16, 4, coarse_diag)
        total = zero2
        for yc in range(16):
            g2 = halve(yc)
            full = g2 + 0.375
            gain = (OMEGA / full) * mask2
            k2[yc] = gain * 0.0625
            d2[yc] = full * (1.0 / OMEGA)
            total = total + g2 * own
            start = gain * q2[yc]
            q2[yc] = start
            wa[PADL + yc] = start
            wb[PADL + yc] = start
        g2sum[...] = total
    else:
        for yc in range(16):
            start = (16.0 * k2[yc]) * halve(yc)
            q2[yc] = start
            wa[PADL + yc] = start
            wb[PADL + yc] = start
    of_q2, of_k2 = (lambda y: q2[y - PADL]), (lambda y: k2[y - PADL])

    @pl.when(sweeps[2] >= 4)
    def _():
        flat_sweep(wa, wb, of_q2, of_k2, PADL, PADL + 16, FLAT, lanes2, 2)

    @pl.when(sweeps[2] >= 3)
    def _():
        flat_sweep(wb, wa, of_q2, of_k2, PADL, PADL + 16, FLAT, lanes2, 2)

    flat_sweep(wa, wb, of_q2, of_k2, PADL, PADL + 16, FLAT, lanes2, 2)
    total = zero2
    for yc in range(16):
        here, beside = flat_neighbours(wb, yc + PADL, lanes2, 2)
        total = total + (q2[yc] - OMEGA * here + k2[yc] * beside) * d2[yc]
    numer = jnp.sum(total * own, axis=0, keepdims=True)
    denom = jnp.sum(g2sum[...], axis=0, keepdims=True)
    part[...] = jnp.where((lane_iota(part.shape[0]) & 1) == 0, numer, denom)
    for y in range(YPOST // 2):
        value = wb[2 * slow + (PADL - 3) + y]
        x2[y, pl.ds(0, 24, stride=2), :] = value
        x2[y, pl.ds(1, 24, stride=2), :] = value
        e2_out[y] = x2[y, ZB : 4 * ZB]


def after_kernel(last, faces, sweeps, *refs):
    if last:
        parts, e1, q1, k1, e2, epre, q, k, field, out, va, vb, ab, halves = refs
    else:
        parts, e1, q1, k1, e2, epre, q, k, field, later, pack, out, field_out, va, vb, ab, s = refs
    a, b = ab.at[0], ab.at[1]
    begin = 1 - (sweeps[0] & 1)
    lanes = lane_iota(ZW)
    lanes_p = lane_iota(parts.shape[0])
    every = parts[...]
    numer = jnp.sum(jnp.where((lanes_p & 1) == 0, every, 0.0))
    denom = jnp.sum(jnp.where((lanes_p & 1) == 1, every, 0.0)) + 0.0625 * faces
    shift = jnp.full((ZW, LANES), numer, F32) / jnp.full((ZW, LANES), denom, F32)
    base = 4 * lax.axis_index("slow") + (PADM - 6)

    def of_q1(y):
        return q1[base + y, ZB : 4 * ZB]

    def of_k1(y):
        return k1[base + y, ZB : 4 * ZB]

    for y in range(YPOST):
        raised = e1[base + y, ZB : 4 * ZB] + (e2[y // 2] + shift)
        raised = jnp.where(of_k1(y) > 0.0, raised, 0.0)
        va[y] = raised
        vb[y] = raised

    @pl.when(sweeps[1] >= 4)
    def _():
        flat_sweep(vb, va, of_q1, of_k1, 1, 15, FLAT, lanes, 1)

    @pl.when(sweeps[1] >= 3)
    def _():
        flat_sweep(va, vb, of_q1, of_k1, 2, 14, FLAT, lanes, 1)

    flat_sweep(vb, va, of_q1, of_k1, 3, 13, FLAT, lanes, 1)
    flat_sweep(va, vb, of_q1, of_k1, 4, 12, FLAT, lanes, 1)

    def raise_fine(ym):
        value = vb[ym + 4]
        for half in range(2):
            y = 2 * ym + half
            for p in PARITIES:
                raised = jnp.where(k[(*p, y + 4)] > 0.0, epre[(*p, y)] + value, 0.0)
                ab[(begin, *p, y)] = raised

    over(0, YPOST // 2, 8, raise_fine)

    @pl.when(sweeps[0] >= 4)
    def _():
        fine_sweep(b, a, q, k, 1, 15, FINE, lanes, offset=4)

    @pl.when(sweeps[0] >= 3)
    def _():
        fine_sweep(a, b, q, k, 2, 14, FINE, lanes, offset=4)

    fine_sweep(b, a, q, k, 3, 13, FINE, lanes, offset=4)
    fine_sweep(a, b, q, k, 4, 12, FINE, lanes, offset=4)
    if not last:
        zero_edges(s)
    for pz, px in PARITIES:
        value = field[pz, px] + 0.5 * b[pz, px, 4:12, ZB : 2 * ZB]
        if last:
            halves[px, pl.ds(pz, YB * ZB, stride=2), :] = value.reshape(YB * ZB, LANES)
        else:
            field_out[pz, px] = value
            s[pz, px, 1 : YB + 1] = value
    if last:
        both = jnp.concatenate([halves[0], halves[1]], axis=1)
        out[...] = exact_dot(both, parity_matrix(True)).reshape(YB, 2 * ZB, 2 * LANES)
    else:
        write_pack(
            s, lambda p, y: later[(*p, y)], lambda p, y: pack[8 + 8 * y + tile_of(p)], out, 4, lane_iota(ZB)
        )


def call(kernel, outs, scratch, scalars, *arrays, space=pltpu.VMEM, megabytes=16, kept=True):
    specs = [pl.BlockSpec(memory_space=pltpu.SMEM)] * len(scalars)
    if space == pltpu.HBM:
        arrays = [pltpu.with_memory_space_constraint(x, pltpu.HBM) for x in arrays]
    return pl.pallas_call(
        kernel,
        out_shape=[pltpu.VMEM(s, F32) if kept else jax.ShapeDtypeStruct(s, F32) for s in outs],
        in_specs=specs + [pl.BlockSpec(memory_space=space)] * len(arrays),
        out_specs=[pl.BlockSpec(memory_space=pltpu.VMEM)] * len(outs),
        scratch_shapes=[pltpu.VMEM(s, F32) if isinstance(s, tuple) else s for s in scratch],
        compiler_params=pltpu.CompilerParams(vmem_limit_bytes=megabytes * 1024 * 1024),
    )(*scalars, *arrays)


def both_ways(to_right, to_left, axis):
    count = lax.axis_size(axis)
    up = [(i, (i + 1) % count) for i in range(count)]
    down = [(target, source) for source, target in up]
    return lax.ppermute(to_right, axis, up), lax.ppermute(to_left, axis, down)


def swap_fast(first, second):
    count = lax.axis_size("fast")
    inner = [(i, i ^ 1) for i in range(count)]
    outer = [(i, (i + (1 if i & 1 else -1)) % count) for i in range(count)]
    a, b = lax.ppermute(first, "fast", inner), lax.ppermute(second, "fast", outer)
    odd = (lax.axis_index("fast") & 1) == 1
    return jnp.where(odd, a, b), jnp.where(odd, b, a)


def window_of(pack, each):
    left, right = swap_fast(pack, pack)
    faces = 8 + 8 * each

    def packed(block, first, half_row):
        return block[first : first + 2 * each, half_row : half_row + 1].reshape(each // 4, ZB, LANES)

    upward = [
        left[4 + 4 * each : faces], packed(left, 4 + 2 * each, ZB - 1), left[faces + 2 :],
        pack[4 + each :],
        right[4 + 4 * each : faces], packed(right, 4 + 2 * each, 0), right[faces : faces + 2],
    ]
    downward = [
        left[: 4 + 4 * each], packed(left, 4 + 4 * each, ZB - 1), left[faces + 2 :],
        pack[: 4 + 7 * each], pack[faces:],
        right[: 4 + 4 * each], packed(right, 4 + 4 * each, 0), right[faces : faces + 2],
    ]
    low, high = both_ways(jnp.concatenate(upward), jnp.concatenate(downward), "slow")
    return left, pack, right, low, high


def body(observed, start_field, diagonal, noise, sweeps):
    natural = observed.shape
    block = (2, 2, YB, ZB, LANES)
    edged = (2, 2, YB + 2, ZB, LANES)
    post = (2, 2, YPOST, ZW, LANES)
    whole = (2, 2, YW, ZW, LANES)
    middle = (YM + 2 * PADM, ZM, LANES)
    low_window = (16, 24, LANES)
    fast_count, slow_count = lax.axis_size("fast"), lax.axis_size("slow")
    first, second, third = YB * slow_count // 4, 2 * ZB * fast_count // 4, 2 * LANES // 4
    faces = 2.0 * (first * second + first * third + second * third)
    lines = (2, YB * 2 * ZB, LANES)
    pack, field = call(
        pack_kernel, [(pack_tiles(8), ZB, LANES), block],
        [*[natural] * 4, (3, *lines), edged, block, block, pltpu.SemaphoreType.DMA((4,))],
        (), observed, start_field, diagonal, noise, space=pltpu.HBM,
    )
    (later,) = call(
        later_kernel, [block], [natural, natural, lines, pltpu.SemaphoreType.DMA((2,))],
        (), observed, noise, space=pltpu.HBM,
    )
    own_pack = pack
    kept_fine = kept_low = None
    for step in range(2):
        opening = step == 0
        count = 2 if opening else 1
        given = window_of(pack, 8 if opening else 4)
        outs = [(count, 4, 16, LANES), (count, 4, 8, LANES), (count, 4, 16, LANES), post, whole]
        if opening:
            *given, later = lax.optimization_barrier((*given, later))
            outs += [whole, (2, 2, YB, ZW, LANES)]
        else:
            given = (*given, *kept_fine)
        got = call(functools.partial(before_kernel, opening), outs, [whole] * 2, (sweeps,), *given)
        outer, own, inner, epre, q = got[:5]
        if opening:
            kept_fine = got[5:]
        left, right = swap_fast(inner, outer)
        strip = jnp.concatenate([left, own, right], axis=2)
        strip = jnp.broadcast_to(strip[None], (slow_count // 2, *strip.shape))
        chips = [[2 * n + core for n in range(slow_count // 2)] for core in range(2)]
        mine = lax.all_to_all(strip, "slow", 0, 0, axis_index_groups=chips, tiled=True)
        other = lax.ppermute(mine, "slow", [(n, n ^ 1) for n in range(slow_count)])
        outs = [(fast_count, LANES), middle, middle, (YPOST // 2, ZW, LANES)]
        scratch = [
            middle, (16, ZM + 8, LANES), (16 + 2 * PADL, 24, LANES), (16 + 2 * PADL, 24, LANES),
            low_window, (YPOST // 2, 48, LANES),
        ]
        if opening:
            outs += [middle, (YM, ZM, LANES), low_window, low_window, (24, LANES)]
            given = (mine, other)
        else:
            given = (mine, other, *kept_low)
        got = call(functools.partial(coarse_kernel, opening), outs, scratch, (sweeps,), *given)
        part, e1, q1, e2 = got[:4]
        if opening:
            kept_low = got[4:]
        parts = lax.all_to_all(part, "fast", 0, 0, tiled=True)
        given = (parts, e1, q1, kept_low[0], e2, epre, q, kept_fine[0], field)
        scratch = [(YPOST, ZW, LANES)] * 2 + [(2, *post)]
        kernel = functools.partial(after_kernel, not opening, faces)
        if opening:
            outs = [(pack_tiles(4), ZB, LANES), block]
            given = (*given, later, own_pack)
            pack, field = call(kernel, outs, scratch + [edged], (sweeps,), *given)
        else:
            halves = [(2, YB * 2 * ZB, LANES)]
            (out,) = call(kernel, [natural], scratch + halves, (sweeps,), *given, kept=False)
    return out


def solution(mesh):
    placed = (
        P("slow", "fast", None),
        P("slow", "fast", None),
        P("slow", "fast", None),
        P(None, "slow", "fast", None),
        P(),
    )
    return jax.shard_map(
        body, mesh=mesh, in_specs=placed, out_specs=P("slow", "fast", None), check_vma=False
    )
```
